32 devices in a mesh: section: 4 (over z), mp: 8 (over y, x, core).
Axes of the slice: x: 2, y: 2, z: 4, core: 2. Of those that a mesh axis runs over, the one named last changes fastest.
Arguments:
- entering_hidden: bfloat16 [4, 256, 8192], P('section', None, 'mp'), may hold values from -12 to 12
- section_weight: bfloat16 [4, 8192, 8192], P('section', None, 'mp'), may hold values from -0.0625 to 0.0625
- section_norm_gain: bfloat16 [4, 8192], P('section', 'mp'), may hold values from 0.5 to 1.5
- plugin_narrowing_factors: bfloat16 [4, 8, 8192, 64], P('section', 'mp'), may hold values from -0.0625 to 0.0625
- plugin_widening_factors: bfloat16 [4, 8, 64, 8192], P('section', 'mp'), may hold values from -0.75 to 0.75
- reward_head: bfloat16 [8192], P('mp'), may hold values from -0.0625 to 0.0625
- adapter_of_block: int32 [4, 2], replicated, may hold values from 0 to 7
- live_block_rows: int32 [4, 2], P('section'), may hold values from 1 to 128
Outputs:
- hidden_out: bfloat16 [4, 256, 8192], P('section', None, 'mp')
- scores: float32 [4, 256], P('section')
The draws below stay inside these ranges and needn't reach their ends.
All inputs are finite; a program needn't handle non-finite values.
Results may differ from the reference program's by a relative error of at most 0.022.
Values may be sent and summed in bfloat16 or wider, within the bound.
No kernel may reach another device: no remote copies, remote signals or barrier semaphores. Data moves between devices by JAX's collectives and lax.ppermute only.
A program may use at most 64 MiB of HBM per device.

```python
import math
import jax
import jax.numpy as jnp
import numpy as np
from jax import lax

EMBED_DIMENSION = 8192
FACTOR_DIMENSION = 64
BLOCK = 128
BLK_MB = 2
PLUGIN_TOTAL = 8
MICRO = 4
ROWS_MB = 256
N_SECTION = 4


def draw_entering_hidden(key, part):
    first_key = jax.random.fold_in(key, 0)
    column = jnp.arange(EMBED_DIMENSION, dtype=jnp.float32) / EMBED_DIMENSION
    rising = 0.5 * jnp.exp(column * math.log(3.0))
    values = jnp.clip(jax.random.normal(first_key, (MICRO, ROWS_MB, EMBED_DIMENSION), jnp.float32), -4.0, 4.0)
    return jnp.clip(values * rising[None, None, :], -12.0, 12.0).astype(jnp.bfloat16)


def set_ends(entries, key, low, largest):
    extent = entries.shape
    index_at = [jax.random.randint(jax.random.fold_in(key, axis), (), 0, extent[axis]) for axis in range(len(extent))]
    entries = entries.at[tuple(index_at)].set(low)
    longest = extent.index(max(extent))
    index_at[longest] = (index_at[longest] + 1) % extent[longest]
    return entries.at[tuple(index_at)].set(largest)


def steps_of(own_key, shape, cuts, smallest, high):
    level, own = 1.0, jax.random.fold_in(own_key, 6)
    for position, parts in cuts:
        heights = jnp.exp(jax.random.uniform(jax.random.fold_in(own, position), (parts,), jnp.float32, smallest / len(cuts), high / len(cuts)))
        level = level * jnp.repeat(heights, shape[position] // parts).reshape([-1 if axis == position else 1 for axis in range(len(shape))])
    return level


def cumulative_ranks(amount, slope):
    loads = [(1 << 20) // math.isqrt(rank ** slope) + 1 for rank in range(1, amount + 1)]
    scale = 1 + sum(loads) // (1 << 30)
    return np.cumsum(np.array([max(1, weight // scale) for weight in loads]))


def ranked_ids(key, extent, amount, slope):
    grid = cumulative_ranks(amount, slope)
    lot = jax.random.randint(jax.random.fold_in(key, 1), extent, 0, int(grid[amount - 1]))
    standing = jnp.searchsorted(jnp.asarray(grid, jnp.int32), lot, side="right")
    return jax.random.permutation(jax.random.fold_in(key, 2), amount)[standing].astype(jnp.int32)


def centred(key, dims, scale, most, cuts=(), kind=jnp.bfloat16):
    result = jax.random.normal(key, dims, jnp.float32) * scale
    if len(cuts) > 0:
        result = steps_of(key, dims, cuts, -0.22, 0.18) * result
    return jnp.clip(result, min=-most, max=most).astype(kind)


def setup_inputs(seed: int = 0) -> dict:
    streams_of = jax.random.split(jax.random.key(seed), 9)
    return {
        "entering_hidden": draw_entering_hidden(jax.random.fold_in(streams_of[8], 71), 0),
        "section_weight": centred(streams_of[1], (N_SECTION, EMBED_DIMENSION, EMBED_DIMENSION), EMBED_DIMENSION ** -0.5, 0.0625, ((0, 4), (2, 8))),
        "section_norm_gain": jnp.clip(1.0 + 0.1 * jax.random.normal(streams_of[2], (N_SECTION, EMBED_DIMENSION), jnp.float32), 0.5, 1.5).astype(jnp.bfloat16),
        "plugin_narrowing_factors": centred(streams_of[3], (N_SECTION, PLUGIN_TOTAL, EMBED_DIMENSION, FACTOR_DIMENSION), EMBED_DIMENSION ** -0.5, 0.0625, ((0, 4), (1, 8))),
        "plugin_widening_factors": centred(streams_of[4], (N_SECTION, PLUGIN_TOTAL, FACTOR_DIMENSION, EMBED_DIMENSION), FACTOR_DIMENSION ** -0.5, 0.75, ((0, 4), (1, 8))),
        "reward_head": centred(streams_of[5], (EMBED_DIMENSION,), EMBED_DIMENSION ** -0.5, 0.0625, ((0, 8),)),
        "adapter_of_block": set_ends(ranked_ids(streams_of[6], (MICRO, BLK_MB), PLUGIN_TOTAL, 2), jax.random.fold_in(streams_of[6], 3), 0, PLUGIN_TOTAL - 1).astype(jnp.int32),
        "live_block_rows": set_ends(jax.random.randint(streams_of[7], (MICRO, BLK_MB), 1, BLOCK + 1), jax.random.fold_in(streams_of[7], 1), 1, BLOCK).astype(jnp.int32),
    }


def layer_of_section(hidden_state, weight, gain, down_maps, up_maps, adapter_numbers):
    hidden_f = hidden_state.astype(jnp.float32)
    squares = lax.optimization_barrier(jnp.sum(hidden_f * hidden_f, axis=1, keepdims=True))
    rescaled_activation = (hidden_f * lax.rsqrt(squares / EMBED_DIMENSION + 1e-05) * gain.astype(jnp.float32)).astype(jnp.bfloat16)
    base = jnp.dot(rescaled_activation.astype(jnp.float32), weight.astype(jnp.float32), preferred_element_type=jnp.float32, precision=lax.Precision.HIGHEST)
    blocks = rescaled_activation.reshape(-1, BLOCK, EMBED_DIMENSION).astype(jnp.float32)
    chosen_down = down_maps[adapter_numbers].astype(jnp.float32)
    compressed_projection = jnp.einsum('brd,bdk->brk', blocks, chosen_down, precision=lax.Precision.HIGHEST).astype(jnp.bfloat16)
    chosen_expansion_matrix = up_maps[adapter_numbers].astype(jnp.float32)
    thin_correction = jnp.einsum('sin,sny->siy', compressed_projection.astype(jnp.float32), chosen_expansion_matrix, precision=lax.Precision.HIGHEST).reshape(-1, EMBED_DIMENSION)
    return (hidden_f + base + 2.0 * thin_correction).astype(jnp.bfloat16)

def reference(entering_hidden, section_weight, section_norm_gain, plugin_narrowing_factors, plugin_widening_factors, reward_head, adapter_of_block, live_block_rows):
    hidden_state = entering_hidden.reshape(MICRO * ROWS_MB, EMBED_DIMENSION)
    adapter_numbers = adapter_of_block.reshape(-1)
    for section_ordinal in range(N_SECTION):
        hidden_state = layer_of_section(hidden_state, section_weight[section_ordinal], section_norm_gain[section_ordinal], plugin_narrowing_factors[section_ordinal], plugin_widening_factors[section_ordinal], adapter_numbers)
    hidden_out = hidden_state.reshape(MICRO, ROWS_MB, EMBED_DIMENSION)
    raw = lax.optimization_barrier(jnp.sum(hidden_out.astype(jnp.float32) * reward_head.astype(jnp.float32), axis=2))
    place = jnp.arange(ROWS_MB, dtype=jnp.int32) % BLOCK
    limits = jnp.repeat(live_block_rows, BLOCK, axis=1)
    scores = jnp.where(place[None, :] < limits, raw, jnp.float32(0.0))
    return (hidden_out, scores)
```

```python
import functools

import jax
import jax.numpy as jnp
from jax import lax
from jax.experimental import pallas as pl
from jax.experimental.pallas import tpu as pltpu
from jax.sharding import PartitionSpec as P

BLOCK = 128
SIDE = 128
LAG = 2
GATHER = "ag"


def prep_kernel(rank, s_ref, *refs):
    *sources, gain_ref, table_ref, x_ref, m_ref = refs
    copies, _, _ = m_ref.shape
    piece = x_ref.shape[1]
    if len(sources) == 2:
        x = jnp.where(s_ref[1] == 0, sources[0][...].astype(jnp.float32), sources[1][...].astype(jnp.float32))
    else:
        x = sources[0][...].astype(jnp.float32)
    x_ref[...] = x.astype(jnp.bfloat16)
    scaled = (x * gain_ref[...].astype(jnp.float32)).astype(jnp.bfloat16)
    squares = jnp.sum(x * x, axis=1, keepdims=True)
    high = squares.astype(jnp.bfloat16).astype(jnp.float32)
    low = squares - high
    inner = lax.dot_general(
        scaled, table_ref[0], (((1,), (1,)), ((), ())), preferred_element_type=jnp.float32
    )
    lane = lax.broadcasted_iota(jnp.int32, inner.shape, 1)
    side = jnp.where(lane < rank, inner, jnp.where(lane == rank, high, jnp.where(lane == rank + 1, low, 0.0)))
    side = side[:, :SIDE].astype(jnp.bfloat16)
    for copy in range(copies):
        m_ref[copy, :, :piece] = scaled
        m_ref[copy, :, piece:] = side


def prep(scalars, sources, block, gain, table, rank, copies):
    piece = gain.shape[1]
    rows = BLOCK
    specs = [
        pl.BlockSpec((rows, piece), functools.partial(lambda b, i, s: (b, 0), b))
        for b in block
    ]
    return pl.pallas_call(
        functools.partial(prep_kernel, rank),
        out_shape=(
            jax.ShapeDtypeStruct((rows, piece), jnp.bfloat16),
            jax.ShapeDtypeStruct((copies, rows, piece + SIDE), jnp.bfloat16),
        ),
        grid_spec=pltpu.PrefetchScalarGridSpec(
            num_scalar_prefetch=1,
            grid=(1,),
            in_specs=specs
            + [
                pl.BlockSpec((1, piece), lambda i, s: (0, 0)),
                pl.BlockSpec((1,) + table.shape[1:], lambda i, s: (s[0], 0, 0)),
            ],
            out_specs=(
                pl.BlockSpec((rows, piece), lambda i, s: (0, 0)),
                pl.BlockSpec((copies, rows, piece + SIDE), lambda i, s: (0, 0, 0)),
            ),
        ),
        cost_estimate=pl.CostEstimate(
            flops=2 * rows * piece * SIDE, bytes_accessed=rows * piece * 8, transcendentals=0
        ),
        name="prep",
    )(scalars, *sources, gain, table)


def layer_kernel(rank, width, counts, s_ref, *refs):
    *parts, w_ref, x_ref, table_ref, o_ref, total, side = refs
    step = pl.program_id(0)
    piece = o_ref.shape[1]

    @pl.when(step == 0)
    def _():
        total[...] = jnp.zeros_like(total)
        side[...] = jnp.zeros_like(side)

    start = 0
    for part, count in zip(parts, counts):
        @pl.when((step >= start) & (step < start + count))
        def _():
            total[...] += jnp.dot(part[0, :, :piece], w_ref[...], preferred_element_type=jnp.float32)
            side[...] += part[0, :, piece:].astype(jnp.float32)

        start += count

    @pl.when(step == start - 1)
    def _():
        squares = side[:, rank : rank + 1] + side[:, rank + 1 : rank + 2]
        scale = lax.rsqrt(squares / width + 1e-05)
        inner = side[:, :rank].astype(jnp.bfloat16)
        delta = jnp.dot(inner, table_ref[0, rank : 2 * rank, :], preferred_element_type=jnp.float32)
        h = x_ref[...].astype(jnp.float32)
        o_ref[...] = (h + scale * (total[...] + 2.0 * delta)).astype(jnp.bfloat16)


def layer(scalars, parts, weight, x, table, rank):
    rows, piece = x.shape
    width = weight.shape[0]
    counts = tuple(part.shape[0] for part in parts)
    owners = sum(counts)
    part_specs = []
    start = 0
    for count in counts:
        part_specs.append(
            pl.BlockSpec(
                (1, rows, piece + SIDE),
                functools.partial(lambda a, c, i, s: (jnp.clip(i - a, 0, c - 1), 0, 0), start, count),
            )
        )
        start += count
    return pl.pallas_call(
        functools.partial(layer_kernel, rank, width, counts),
        out_shape=jax.ShapeDtypeStruct((rows, piece), jnp.bfloat16),
        grid_spec=pltpu.PrefetchScalarGridSpec(
            num_scalar_prefetch=1,
            grid=(owners,),
            in_specs=part_specs
            + [
                pl.BlockSpec((piece, piece), lambda i, s: (s[2 + i], 0)),
                pl.BlockSpec((rows, piece), lambda i, s: (0, 0)),
                pl.BlockSpec((1,) + table.shape[1:], lambda i, s: (s[0], 0, 0)),
            ],
            out_specs=pl.BlockSpec((rows, piece), lambda i, s: (0, 0)),
            scratch_shapes=[
                pltpu.VMEM((rows, piece), jnp.float32),
                pltpu.VMEM((rows, SIDE), jnp.float32),
            ],
        ),
        cost_estimate=pl.CostEstimate(
            flops=2 * rows * width * piece, bytes_accessed=2 * width * piece, transcendentals=0
        ),
        name="layer",
    )(scalars, *parts, weight, x, table)


def shards(
    entering_hidden,
    section_weight,
    section_norm_gain,
    plugin_narrowing_factors,
    plugin_widening_factors,
    reward_head,
    adapter_of_block,
    live_block_rows,
):
    sections = lax.axis_size("section")
    section = lax.axis_index("section")
    chips = lax.axis_size("chip")
    cores = lax.axis_size("core")
    owners = chips * cores
    everyone = ("chip", "core")
    me = lax.axis_index(everyone)
    batches_here, rows, piece = entering_hidden.shape
    micro = batches_here * sections
    per_micro = rows // BLOCK
    owned = plugin_narrowing_factors.shape[1]
    rank = plugin_narrowing_factors.shape[3]
    weight = section_weight[0]
    chunks = micro * per_micro

    down = jnp.swapaxes(plugin_narrowing_factors[0], 1, 2)
    maps = jnp.concatenate([down, plugin_widening_factors[0]], axis=1)
    maps = jnp.moveaxis(maps.reshape(owned, 2 * rank, owners, piece), 2, 0)
    table = lax.all_to_all(maps, everyone, split_axis=0, concat_axis=0, tiled=True)
    table = table.reshape(owners * owned, 2 * rank, piece)

    feeds = []
    for m in range(micro):
        home, slot = divmod(m, batches_here)
        block = entering_hidden[slot]
        feeds.append(block if home == 0 else lax.ppermute(block, "section", [(home, 0)]))

    adapters = adapter_of_block.reshape(-1)
    if GATHER == "ag":
        order = jnp.arange(owners, dtype=jnp.int32)
        copies = 1
    else:
        chip, core = lax.axis_index("chip"), lax.axis_index("core")
        base = jnp.arange(chips, dtype=jnp.int32) * cores
        order = jnp.concatenate([base + (core + k) % cores for k in range(cores)])
        copies = chips

    def gathered(message):
        if GATHER == "ag":
            return [lax.all_gather(message, everyone, axis=0, tiled=True)]
        parts = lax.all_to_all(message, "chip", split_axis=0, concat_axis=0, tiled=True)
        out = [parts]
        for k in range(1, cores):
            out.append(lax.ppermute(parts, "core", [((c + k) % cores, c) for c in range(cores)]))
        return out

    arrived = {}
    done = {}
    zero = jnp.zeros((BLOCK, piece), jnp.bfloat16)
    for tick in range(chunks + LAG * (sections - 1)):
        active = [s for s in range(sections) if 0 <= tick - LAG * s < chunks]
        mine = jnp.clip(tick - LAG * section, 0, chunks - 1)
        adapter = lax.dynamic_index_in_dim(adapters, mine, 0, keepdims=True)
        scalars = jnp.concatenate([adapter, section[None].astype(jnp.int32), order])
        sources, blocks = [], []
        if 0 in active:
            m, b = divmod(tick, per_micro)
            sources.append(feeds[m])
            blocks.append(b)
        if active != [0]:
            sources.append(arrived.pop(tick, zero))
            blocks.append(0)
        x, message = prep(scalars, sources, blocks, section_norm_gain, table, rank, copies)
        parts = gathered(message)
        h = layer(scalars, parts, weight, x, table, rank)
        onward = [(s, s + 1) for s in active if s + 1 < sections]
        if onward:
            arrived[tick + LAG] = lax.ppermute(h, "section", onward)
        if sections - 1 in active:
            done[tick - LAG * (sections - 1)] = h

    slots = []
    for slot in range(batches_here):
        value = None
        for home in range(sections):
            m = home * batches_here + slot
            block = jnp.concatenate([done[m * per_micro + b] for b in range(per_micro)], axis=0)
            if home != sections - 1:
                block = lax.ppermute(block, "section", [(sections - 1, home)])
            value = block if value is None else jnp.where(section == home, block, value)
        slots.append(value)
    hidden_out = jnp.stack(slots)
    partial_score = jnp.sum(
        hidden_out.astype(jnp.float32) * reward_head.astype(jnp.float32)[None, None, :], axis=2
    )
    raw = lax.psum(partial_score, everyone)
    place = jnp.arange(rows, dtype=jnp.int32) % BLOCK
    limits = jnp.repeat(live_block_rows, BLOCK, axis=1)
    scores = jnp.where(place[None, :] < limits, raw, jnp.float32(0.0))
    return (hidden_out, scores)


def solution(mesh):
    sections, owners = mesh.shape["section"], mesh.shape["mp"]
    cores = 2 if owners % 2 == 0 else 1
    fine = jax.sharding.Mesh(
        mesh.devices.reshape(sections, owners // cores, cores), ("section", "chip", "core")
    )
    mp = ("chip", "core")
    placed = (
        P("section", None, mp),
        P("section", None, mp),
        P("section", mp),
        P("section", mp, None, None),
        P("section", mp, None, None),
        P(mp),
        P(),
        P("section", None),
    )
    return jax.shard_map(
        shards,
        mesh=fine,
        in_specs=placed,
        out_specs=(P("section", None, mp), P("section", None)),
        check_vma=False,
    )
```

```python
import functools

import jax
import jax.numpy as jnp
from jax import lax
from jax.experimental import pallas as pl
from jax.experimental.pallas import tpu as pltpu
from jax.sharding import PartitionSpec as P

BLOCK = 128
SIDE = 128
LAG = 2


def prep_kernel(rank, block, s_ref, *refs):
    *sources, gain_ref, table_ref, x_ref, m_ref = refs
    copies = m_ref.shape[0]
    rows, piece = x_ref.shape
    picked = [source[b * rows : (b + 1) * rows, :] for source, b in zip(sources, block)]
    if len(picked) == 2:
        x = jnp.where(s_ref[1] == 0, picked[0].astype(jnp.float32), picked[1].astype(jnp.float32))
    else:
        x = picked[0].astype(jnp.float32)
    x_ref[...] = x.astype(jnp.bfloat16)
    scaled = (x * gain_ref[...].astype(jnp.float32)).astype(jnp.bfloat16)
    squares = jnp.sum(x * x, axis=1, keepdims=True)
    high = squares.astype(jnp.bfloat16).astype(jnp.float32)
    low = squares - high
    inner = lax.dot_general(
        scaled, table_ref[s_ref[0]], (((1,), (1,)), ((), ())), preferred_element_type=jnp.float32
    )
    lane = lax.broadcasted_iota(jnp.int32, inner.shape, 1)
    side = jnp.where(lane < rank, inner, jnp.where(lane == rank, high, jnp.where(lane == rank + 1, low, 0.0)))
    side = side[:, :SIDE].astype(jnp.bfloat16)
    for copy in range(copies):
        m_ref[copy, :, :piece] = scaled
        m_ref[copy, :, piece:] = side


VMEM = pl.BlockSpec(memory_space=pltpu.VMEM)
SMEM = pl.BlockSpec(memory_space=pltpu.SMEM)


def near(x):
    return pltpu.with_memory_space_constraint(x, pltpu.VMEM)


def prep(scalars, sources, block, gain, table, rank, copies):
    piece = gain.shape[1]
    rows = BLOCK
    return pl.pallas_call(
        functools.partial(prep_kernel, rank, block),
        out_shape=(
            pltpu.VMEM((rows, piece), jnp.bfloat16),
            pltpu.VMEM((copies, rows, piece + SIDE), jnp.bfloat16),
        ),
        in_specs=[SMEM] + [VMEM] * (len(sources) + 2),
        out_specs=(VMEM, VMEM),
        compiler_params=pltpu.CompilerParams(vmem_limit_bytes=8 << 20),
        cost_estimate=pl.CostEstimate(
            flops=2 * rows * piece * SIDE, bytes_accessed=rows * piece * 8, transcendentals=0
        ),
        name="prep",
    )(scalars, *map(near, sources), near(gain), near(table))


def stage_kernel(w_ref, o_ref, sem):
    copy = pltpu.make_async_copy(w_ref, o_ref, sem)
    copy.start()
    copy.wait()


def staged(weight):
    return pl.pallas_call(
        stage_kernel,
        out_shape=pltpu.VMEM(weight.shape, weight.dtype),
        in_specs=[pl.BlockSpec(memory_space=pl.ANY)],
        out_specs=VMEM,
        scratch_shapes=[pltpu.SemaphoreType.DMA],
        compiler_params=pltpu.CompilerParams(vmem_limit_bytes=4 << 20),
        cost_estimate=pl.CostEstimate(flops=0, bytes_accessed=2 * weight.size, transcendentals=0),
        name="stage",
    )(weight)


def layer_kernel(rank, counts, s_ref, *refs):
    *parts, w_ref, x_ref, table_ref, o_ref = refs
    rows, piece = x_ref.shape
    width = w_ref.shape[0]
    side = jnp.zeros((rows, SIDE), jnp.float32)
    for part, count in zip(parts, counts):
        for k in range(count):
            side = side + part[k, :, piece:].astype(jnp.float32)
    squares = side[:, rank : rank + 1] + side[:, rank + 1 : rank + 2]
    scale = lax.rsqrt(squares / width + 1e-05)
    inner = (2.0 * side[:, :rank]).astype(jnp.bfloat16)
    tile = min(piece, 256)

    @pl.loop(0, piece // tile)
    def _(n):
        columns = pl.ds(pl.multiple_of(n * tile, tile), tile)
        total = jnp.dot(
            inner, table_ref[s_ref[0], rank : 2 * rank, columns], preferred_element_type=jnp.float32
        )
        i = 0
        for part, count in zip(parts, counts):
            for k in range(count):
                depth = pl.ds(pl.multiple_of(s_ref[2 + i] * piece, piece), piece)
                total += jnp.dot(
                    part[k, :, :piece], w_ref[depth, columns], preferred_element_type=jnp.float32
                )
                i += 1
        h = x_ref[:, columns].astype(jnp.float32)
        o_ref[:, columns] = (h + scale * total).astype(jnp.bfloat16)


def layer(scalars, parts, weight, x, table, rank):
    rows, piece = x.shape
    width = weight.shape[0]
    counts = tuple(part.shape[0] for part in parts)
    return pl.pallas_call(
        functools.partial(layer_kernel, rank, counts),
        out_shape=pltpu.VMEM((rows, piece), jnp.bfloat16),
        in_specs=[SMEM] + [VMEM] * (len(parts) + 3),
        out_specs=VMEM,
        compiler_params=pltpu.CompilerParams(vmem_limit_bytes=8 << 20),
        cost_estimate=pl.CostEstimate(
            flops=2 * rows * width * piece, bytes_accessed=2 * width * piece // 4, transcendentals=0
        ),
        name="layer",
    )(scalars, *map(near, parts), near(weight), near(x), near(table))


def shards(
    entering_hidden,
    section_weight,
    section_norm_gain,
    plugin_narrowing_factors,
    plugin_widening_factors,
    reward_head,
    adapter_of_block,
    live_block_rows,
):
    sections = lax.axis_size("section")
    section = lax.axis_index("section")
    chips = lax.axis_size("chip")
    cores = lax.axis_size("core")
    owners = chips * cores
    everyone = ("chip", "core")
    batches_here, rows, piece = entering_hidden.shape
    micro = batches_here * sections
    per_micro = rows // BLOCK
    owned = plugin_narrowing_factors.shape[1]
    rank = plugin_narrowing_factors.shape[3]
    weight = staged(section_weight[0])
    chunks = micro * per_micro

    down = jnp.swapaxes(plugin_narrowing_factors[0], 1, 2)
    maps = jnp.concatenate([down, plugin_widening_factors[0]], axis=1)
    maps = jnp.moveaxis(maps.reshape(owned, 2 * rank, owners, piece), 2, 0)
    table = lax.all_to_all(maps, everyone, split_axis=0, concat_axis=0, tiled=True)
    table = table.reshape(owners * owned, 2 * rank, piece)

    feeds = []
    for m in range(micro):
        home, slot = divmod(m, batches_here)
        block = entering_hidden[slot]
        feeds.append(block if home == 0 else lax.ppermute(block, "section", [(home, 0)]))

    adapters = adapter_of_block.reshape(-1)
    chip, core = lax.axis_index("chip"), lax.axis_index("core")
    base = jnp.arange(chips, dtype=jnp.int32) * cores
    order = jnp.concatenate([base + (core + k) % cores for k in range(cores)])

    def gathered(message):
        parts = lax.all_to_all(message, "chip", split_axis=0, concat_axis=0, tiled=True)
        out = [parts]
        for k in range(1, cores):
            out.append(lax.ppermute(parts, "core", [((c + k) % cores, c) for c in range(cores)]))
        return out

    arrived = {}
    done = {}
    zero = jnp.zeros((BLOCK, piece), jnp.bfloat16)
    for tick in range(chunks + LAG * (sections - 1)):
        active = [s for s in range(sections) if 0 <= tick - LAG * s < chunks]
        mine = jnp.clip(tick - LAG * section, 0, chunks - 1)
        adapter = lax.dynamic_index_in_dim(adapters, mine, 0, keepdims=True)
        scalars = jnp.concatenate([adapter, section[None].astype(jnp.int32), order])
        sources, blocks = [], []
        if 0 in active:
            m, b = divmod(tick, per_micro)
            sources.append(feeds[m])
            blocks.append(b)
        if active != [0]:
            sources.append(arrived.pop(tick, zero))
            blocks.append(0)
        x, message = prep(scalars, sources, blocks, section_norm_gain, table, rank, chips)
        parts = gathered(message)
        h = layer(scalars, parts, weight, x, table, rank)
        onward = [(s, s + 1) for s in active if s + 1 < sections]
        if onward:
            arrived[tick + LAG] = lax.ppermute(h, "section", onward)
        if sections - 1 in active:
            done[tick - LAG * (sections - 1)] = h

    slots = []
    for slot in range(batches_here):
        value = None
        for home in range(sections):
            m = home * batches_here + slot
            block = jnp.concatenate([done[m * per_micro + b] for b in range(per_micro)], axis=0)
            if home != sections - 1:
                block = lax.ppermute(block, "section", [(sections - 1, home)])
            value = block if value is None else jnp.where(section == home, block, value)
        slots.append(value)
    hidden_out = jnp.stack(slots)
    partial_score = jnp.sum(
        hidden_out.astype(jnp.float32) * reward_head.astype(jnp.float32)[None, None, :], axis=2
    )
    raw = lax.psum(partial_score, everyone)
    place = jnp.arange(rows, dtype=jnp.int32) % BLOCK
    limits = jnp.repeat(live_block_rows, BLOCK, axis=1)
    scores = jnp.where(place[None, :] < limits, raw, jnp.float32(0.0))
    return (hidden_out, scores)


def solution(mesh):
    sections, owners = mesh.shape["section"], mesh.shape["mp"]
    cores = 2 if owners % 2 == 0 else 1
    fine = jax.sharding.Mesh(
        mesh.devices.reshape(sections, owners // cores, cores), ("section", "chip", "core")
    )
    mp = ("chip", "core")
    placed = (
        P("section", None, mp),
        P("section", None, mp),
        P("section", mp),
        P("section", mp, None, None),
        P("section", mp, None, None),
        P(mp),
        P(),
        P("section", None),
    )
    return jax.shard_map(
        shards,
        mesh=fine,
        in_specs=placed,
        out_specs=(P("section", None, mp), P("section", None)),
        check_vma=False,
    )
```

```python
import functools

import jax
import jax.numpy as jnp
from jax import lax
from jax.experimental import pallas as pl
from jax.experimental.pallas import tpu as pltpu
from jax.sharding import PartitionSpec as P

BLOCK = 128
SIDE = 128
LAG = 2
SPAN = 1

VMEM = pl.BlockSpec(memory_space=pltpu.VMEM)
SMEM = pl.BlockSpec(memory_space=pltpu.SMEM)


def near(x):
    return pltpu.with_memory_space_constraint(x, pltpu.VMEM)


def call(kernel, out_shape, args, name, flops, moved, limit=8, scratch=()):
    info, *arrays = args
    return pl.pallas_call(
        kernel,
        out_shape=out_shape,
        in_specs=[SMEM] + [VMEM] * len(arrays),
        out_specs=jax.tree.map(lambda _: VMEM, out_shape),
        scratch_shapes=scratch,
        compiler_params=pltpu.CompilerParams(vmem_limit_bytes=limit << 20),
        cost_estimate=pl.CostEstimate(flops=flops, bytes_accessed=moved, transcendentals=0),
        name=name,
    )(info, *map(near, arrays))


def adapter_at(info_ref, owners, tick, chunks, block):
    mine = jnp.clip(tick - LAG * info_ref[0], 0, chunks - 1)
    return info_ref[1 + owners + mine * SPAN + block]


def prep_kernel(rank, owners, tick, chunks, block, info_ref, *refs):
    *sources, gain_ref, down_ref, x_ref, m_ref = refs
    copies = m_ref.shape[0]
    rows, piece = x_ref.shape
    picked = [source[b * rows : (b + 1) * rows, :].astype(jnp.float32) for source, b in zip(sources, block)]
    x = jnp.where(info_ref[0] == 0, *picked) if len(picked) == 2 else picked[0]
    x_ref[...] = x.astype(jnp.bfloat16)
    scaled = (x * gain_ref[...].astype(jnp.float32)).astype(jnp.bfloat16)
    squares = jnp.sum(x * x, axis=1, keepdims=True)
    high = squares.astype(jnp.bfloat16).astype(jnp.float32)
    low = squares - high
    lane = lax.broadcasted_iota(jnp.int32, (rows, SIDE), 1)
    inner = []
    for b in range(SPAN):
        product = lax.dot_general(
            scaled[b * BLOCK : (b + 1) * BLOCK],
            down_ref[adapter_at(info_ref, owners, tick, chunks, b)],
            (((1,), (1,)), ((), ())),
            preferred_element_type=jnp.float32,
        )
        inner.append(jnp.concatenate([product, jnp.zeros((BLOCK, SIDE - rank), jnp.float32)], axis=1))
    inner = jnp.concatenate(inner, axis=0) if SPAN > 1 else inner[0]
    side = jnp.where(lane == rank, high, jnp.where(lane == rank + 1, low, inner)).astype(jnp.bfloat16)
    for copy in range(copies):
        m_ref[copy, :, :piece] = scaled
        m_ref[copy, :, piece:] = side


def stage_kernel(w_ref, o_ref, sem):
    copy = pltpu.make_async_copy(w_ref, o_ref, sem)
    copy.start()
    copy.wait()


def staged(weight):
    return pl.pallas_call(
        stage_kernel,
        out_shape=pltpu.VMEM(weight.shape, weight.dtype),
        in_specs=[pl.BlockSpec(memory_space=pl.ANY)],
        out_specs=VMEM,
        scratch_shapes=[pltpu.SemaphoreType.DMA],
        compiler_params=pltpu.CompilerParams(vmem_limit_bytes=4 << 20),
        cost_estimate=pl.CostEstimate(flops=0, bytes_accessed=2 * weight.size, transcendentals=0),
        name="stage",
    )(weight)


def layer_kernel(rank, owners, tick, chunks, counts, info_ref, *refs):
    *parts, w_ref, x_ref, up_ref, o_ref = refs
    rows, piece = x_ref.shape
    width = w_ref.shape[0]
    side = jnp.zeros((rows, SIDE), jnp.float32)
    for part, count in zip(parts, counts):
        for k in range(count):
            side = side + part[k, :, piece:].astype(jnp.float32)
    squares = side[:, rank : rank + 1] + side[:, rank + 1 : rank + 2]
    scale = lax.rsqrt(squares / width + 1e-05)
    inner = (2.0 * side[:, :rank]).astype(jnp.bfloat16)
    tile = min(piece, 256)

    @pl.loop(0, piece // tile)
    def _(n):
        columns = pl.ds(pl.multiple_of(n * tile, tile), tile)
        delta = [
            jnp.dot(
                inner[b * BLOCK : (b + 1) * BLOCK],
                up_ref[adapter_at(info_ref, owners, tick, chunks, b), :, columns],
                preferred_element_type=jnp.float32,
            )
            for b in range(SPAN)
        ]
        total = jnp.concatenate(delta, axis=0) if SPAN > 1 else delta[0]
        i = 0
        for part, count in zip(parts, counts):
            for k in range(count):
                depth = pl.ds(pl.multiple_of(info_ref[1 + i] * piece, piece), piece)
                total += jnp.dot(
                    part[k, :, :piece], w_ref[depth, columns], preferred_element_type=jnp.float32
                )
                i += 1
        h = x_ref[:, columns].astype(jnp.float32)
        o_ref[:, columns] = (h + scale * total).astype(jnp.bfloat16)


def join_kernel(info_ref, *refs):
    *blocks, o_ref = refs
    rows = blocks[0].shape[0]
    for i, block in enumerate(blocks):
        o_ref[i * rows : (i + 1) * rows, :] = block[...]


def finish_kernel(sections, info_ref, *refs):
    *blocks, head_ref, o_ref, score_ref = refs
    for section in range(sections):

        @pl.when(info_ref[0] == section)
        def _():
            h = blocks[section][...]
            o_ref[...] = h
            score_ref[...] = jnp.sum(
                h.astype(jnp.float32) * head_ref[...].astype(jnp.float32), axis=1, keepdims=True
            )


def shards(
    entering_hidden,
    section_weight,
    section_norm_gain,
    plugin_narrowing_factors,
    plugin_widening_factors,
    reward_head,
    adapter_of_block,
    live_block_rows,
):
    sections = lax.axis_size("section")
    section = lax.axis_index("section")
    chips = lax.axis_size("chip")
    cores = lax.axis_size("core")
    owners = chips * cores
    everyone = ("chip", "core")
    batches_here, rows, piece = entering_hidden.shape
    micro = batches_here * sections
    span = BLOCK * SPAN
    per_micro = rows // span
    owned = plugin_narrowing_factors.shape[1]
    rank = plugin_narrowing_factors.shape[3]
    chunks = micro * per_micro
    weight = staged(section_weight[0])
    pairwise = chips == 4

    chip, core = lax.axis_index("chip"), lax.axis_index("core")
    base = jnp.arange(chips, dtype=jnp.int32)
    base = (chip ^ base if pairwise else base) * cores
    order = jnp.concatenate([base + (core + k) % cores for k in range(cores)])
    info = jnp.concatenate([section[None], order, adapter_of_block.reshape(-1)]).astype(jnp.int32)

    def spread(maps):
        maps = jnp.moveaxis(maps.reshape(owned, rank, owners, piece), 2, 0)
        maps = lax.all_to_all(maps, everyone, split_axis=0, concat_axis=0, tiled=True)
        return maps.reshape(owners * owned, rank, piece)

    down = spread(jnp.swapaxes(plugin_narrowing_factors[0], 1, 2))
    up = spread(plugin_widening_factors[0])

    feeds = []
    for m in range(micro):
        home, slot = divmod(m, batches_here)
        block = entering_hidden[slot]
        feeds.append(block if home == 0 else lax.ppermute(block, "section", [(home, 0)]))

    def gathered(message):
        if pairwise:
            parts = [message]
            for k in (1, 2, 3):
                parts.append(lax.ppermute(message, "chip", [(i, i ^ k) for i in range(chips)]))
        else:
            parts = [lax.all_to_all(message, "chip", split_axis=0, concat_axis=0, tiled=True)]
        out = list(parts)
        for k in range(1, cores):
            for part in parts:
                out.append(lax.ppermute(part, "core", [((c + k) % cores, c) for c in range(cores)]))
        return out

    def prep(tick, sources, blocks):
        out_shape = (
            pltpu.VMEM((span, piece), jnp.bfloat16),
            pltpu.VMEM((1 if pairwise else chips, span, piece + SIDE), jnp.bfloat16),
        )
        kernel = functools.partial(prep_kernel, rank, owners, tick, chunks, blocks)
        args = (info, *sources, section_norm_gain, down)
        return call(kernel, out_shape, args, "prep", 2 * span * piece * SIDE, span * piece * 8)

    def layer(tick, parts, x):
        counts = tuple(part.shape[0] for part in parts)
        width = piece * owners
        kernel = functools.partial(layer_kernel, rank, owners, tick, chunks, counts)
        args = (info, *parts, weight, x, up)
        out_shape = pltpu.VMEM((span, piece), jnp.bfloat16)
        return call(kernel, out_shape, args, "layer", 2 * span * width * piece, 2 * span * width)

    arrived = {}
    done = {}
    home_blocks = {}
    for tick in range(chunks + LAG * (sections - 1)):
        active = [s for s in range(sections) if 0 <= tick - LAG * s < chunks]
        sources, blocks = [], []
        if 0 in active:
            m, b = divmod(tick, per_micro)
            sources.append(feeds[m])
            blocks.append(b)
        if active != [0]:
            sources.append(arrived.pop(tick))
            blocks.append(0)
        x, message = prep(tick, sources, blocks)
        h = layer(tick, gathered(message), x)
        onward = [(s, s + 1) for s in active if s + 1 < sections]
        if onward:
            arrived[tick + LAG] = lax.ppermute(h, "section", onward)
        if sections - 1 in active:
            last = tick - LAG * (sections - 1)
            done[last] = h
            if last % per_micro == per_micro - 1:
                m = last // per_micro
                block = [done[m * per_micro + b] for b in range(per_micro)]
                if per_micro > 1:
                    out_shape = pltpu.VMEM((rows, piece), jnp.bfloat16)
                    block = call(join_kernel, out_shape, (info, *block), "join", 0, rows * piece * 4)
                else:
                    block = block[0]
                home = m // batches_here
                if home != sections - 1:
                    block = lax.ppermute(block, "section", [(sections - 1, home)])
                home_blocks[m] = block

    hidden, partial_score = [], []
    for slot in range(batches_here):
        out_shape = (
            jax.ShapeDtypeStruct((rows, piece), jnp.bfloat16),
            jax.ShapeDtypeStruct((rows, 1), jnp.float32),
        )
        block = [home_blocks[home * batches_here + slot] for home in range(sections)]
        kernel = functools.partial(finish_kernel, sections)
        args = (info, *block, reward_head[None])
        h, s = call(kernel, out_shape, args, "finish", 2 * rows * piece, rows * piece * 4)
        hidden.append(h)
        partial_score.append(s[:, 0])
    raw = lax.psum(jnp.stack(partial_score), everyone)
    place = jnp.arange(rows, dtype=jnp.int32) % BLOCK
    limits = jnp.repeat(live_block_rows, BLOCK, axis=1)
    scores = jnp.where(place[None, :] < limits, raw, jnp.float32(0.0))
    return (jnp.stack(hidden), scores)


def solution(mesh):
    sections, owners = mesh.shape["section"], mesh.shape["mp"]
    cores = 2 if owners % 2 == 0 else 1
    fine = jax.sharding.Mesh(
        mesh.devices.reshape(sections, owners // cores, cores), ("section", "chip", "core")
    )
    mp = ("chip", "core")
    placed = (
        P("section", None, mp),
        P("section", None, mp),
        P("section", mp),
        P("section", mp, None, None),
        P("section", mp, None, None),
        P(mp),
        P(),
        P("section", None),
    )
    return jax.shard_map(
        shards,
        mesh=fine,
        in_specs=placed,
        out_specs=(P("section", None, mp), P("section", None)),
        check_vma=False,
    )
```

```python
import functools

import jax
import jax.numpy as jnp
from jax import lax
from jax.experimental import pallas as pl
from jax.experimental.pallas import tpu as pltpu
from jax.sharding import PartitionSpec as P

BLOCK = 128
SIDE = 128
LAG = 2
SPAN = 1

VMEM = pl.BlockSpec(memory_space=pltpu.VMEM)
SMEM = pl.BlockSpec(memory_space=pltpu.SMEM)


def near(x):
    return pltpu.with_memory_space_constraint(x, pltpu.VMEM)


def call(kernel, out_shape, args, name, flops, moved, limit=8, after=()):
    info, *arrays = args
    count = len(arrays)

    def body(info_ref, *refs):
        kernel(info_ref, *refs[:count], *refs[count + len(after) :])

    return pl.pallas_call(
        body,
        out_shape=out_shape,
        in_specs=[SMEM] + [VMEM] * count + [pl.BlockSpec(memory_space=pl.ANY)] * len(after),
        out_specs=jax.tree.map(lambda _: VMEM, out_shape),
        compiler_params=pltpu.CompilerParams(vmem_limit_bytes=limit << 20),
        cost_estimate=pl.CostEstimate(flops=flops, bytes_accessed=moved, transcendentals=0),
        name=name,
    )(info, *map(near, arrays), *after)


def tie(x, after):
    def body(*_):
        pass

    return pl.pallas_call(
        body,
        out_shape=pltpu.VMEM(x.shape, x.dtype),
        in_specs=[VMEM] + [pl.BlockSpec(memory_space=pl.ANY)] * len(after),
        out_specs=VMEM,
        input_output_aliases={0: 0},
        compiler_params=pltpu.CompilerParams(vmem_limit_bytes=1 << 20),
        cost_estimate=pl.CostEstimate(flops=0, bytes_accessed=0, transcendentals=0),
        name="tie",
    )(near(x), *after)


def adapter_at(info_ref, owners, owned, tick, chunks, block):
    mine = jnp.clip(tick - LAG * info_ref[0], 0, chunks - 1)
    adapter = info_ref[2 + owners + mine * SPAN + block]
    if owned == 1:
        return adapter ^ info_ref[1]
    return (lax.div(adapter, owned) ^ info_ref[1]) * owned + lax.rem(adapter, owned)


def prep_kernel(rank, owners, owned, tick, chunks, block, info_ref, *refs):
    *sources, gain_ref, down_ref, x_ref, m_ref = refs
    copies = m_ref.shape[0]
    rows, piece = x_ref.shape
    picked = [source[b * rows : (b + 1) * rows, :].astype(jnp.float32) for source, b in zip(sources, block)]
    x = jnp.where(info_ref[0] == 0, *picked) if len(picked) == 2 else picked[0]
    x_ref[...] = x.astype(jnp.bfloat16)
    scaled = (x * gain_ref[...].astype(jnp.float32)).astype(jnp.bfloat16)
    squares = jnp.sum(x * x, axis=1, keepdims=True)
    high = squares.astype(jnp.bfloat16).astype(jnp.float32)
    low = squares - high
    lane = lax.broadcasted_iota(jnp.int32, (rows, SIDE), 1)
    inner = []
    for b in range(SPAN):
        product = lax.dot_general(
            scaled[b * BLOCK : (b + 1) * BLOCK],
            down_ref[adapter_at(info_ref, owners, owned, tick, chunks, b)],
            (((1,), (1,)), ((), ())),
            preferred_element_type=jnp.float32,
        )
        inner.append(jnp.concatenate([product, jnp.zeros((BLOCK, SIDE - rank), jnp.float32)], axis=1))
    inner = jnp.concatenate(inner, axis=0) if SPAN > 1 else inner[0]
    side = jnp.where(lane == rank, high, jnp.where(lane == rank + 1, low, inner)).astype(jnp.bfloat16)
    for copy in range(copies):
        m_ref[copy, :, :piece] = scaled
        m_ref[copy, :, piece:] = side


def stage_kernel(w_ref, *refs):
    *_, o_ref, sem = refs
    copy = pltpu.make_async_copy(w_ref, o_ref, sem)
    copy.start()
    copy.wait()


def staged(weight, after):
    return pl.pallas_call(
        stage_kernel,
        out_shape=pltpu.VMEM(weight.shape, weight.dtype),
        in_specs=[pl.BlockSpec(memory_space=pl.ANY)] * (1 + len(after)),
        out_specs=VMEM,
        scratch_shapes=[pltpu.SemaphoreType.DMA],
        compiler_params=pltpu.CompilerParams(vmem_limit_bytes=4 << 20),
        cost_estimate=pl.CostEstimate(flops=0, bytes_accessed=2 * weight.size, transcendentals=0),
        name="stage",
    )(pltpu.with_memory_space_constraint(weight, pltpu.HBM), *after)


def layer_kernel(rank, owners, owned, tick, chunks, counts, info_ref, *refs):
    *parts, w_ref, x_ref, up_ref, o_ref = refs
    rows, piece = x_ref.shape
    width = w_ref.shape[0]
    side = jnp.zeros((rows, SIDE), jnp.float32)
    for part, count in zip(parts, counts):
        for k in range(count):
            side = side + part[k, :, piece:].astype(jnp.float32)
    squares = side[:, rank : rank + 1] + side[:, rank + 1 : rank + 2]
    scale = lax.rsqrt(squares / width + 1e-05)
    inner = (2.0 * side[:, :rank]).astype(jnp.bfloat16)
    tile = min(piece, 256)

    @pl.loop(0, piece // tile)
    def _(n):
        columns = pl.ds(pl.multiple_of(n * tile, tile), tile)
        delta = [
            jnp.dot(
                inner[b * BLOCK : (b + 1) * BLOCK],
                up_ref[adapter_at(info_ref, owners, owned, tick, chunks, b), :, columns],
                preferred_element_type=jnp.float32,
            )
            for b in range(SPAN)
        ]
        total = jnp.concatenate(delta, axis=0) if SPAN > 1 else delta[0]
        i = 0
        for part, count in zip(parts, counts):
            for k in range(count):
                depth = pl.ds(pl.multiple_of(info_ref[2 + i] * piece, piece), piece)
                total += jnp.dot(
                    part[k, :, :piece], w_ref[depth, columns], preferred_element_type=jnp.float32
                )
                i += 1
        h = x_ref[:, columns].astype(jnp.float32)
        o_ref[:, columns] = (h + scale * total).astype(jnp.bfloat16)


def cut_kernel(owners, info_ref, maps_ref, *outs):
    piece = outs[0].shape[2]
    for k, out in enumerate(outs):
        out[...] = maps_ref[:, :, pl.ds(pl.multiple_of((info_ref[1] ^ k) * piece, piece), piece)]


def stack_kernel(info_ref, *refs):
    *blocks, o_ref = refs
    owned = blocks[0].shape[0]
    for i, block in enumerate(blocks):
        o_ref[i * owned : (i + 1) * owned] = block[...]


def join_kernel(info_ref, *refs):
    *blocks, o_ref = refs
    rows = blocks[0].shape[0]
    for i, block in enumerate(blocks):
        o_ref[i * rows : (i + 1) * rows, :] = block[...]


def finish_kernel(sections, info_ref, *refs):
    *blocks, head_ref, o_ref, score_ref = refs
    for section in range(sections):

        @pl.when(info_ref[0] == section)
        def _():
            h = blocks[section][...]
            o_ref[...] = h
            score_ref[...] = jnp.sum(
                h.astype(jnp.float32) * head_ref[...].astype(jnp.float32), axis=1, keepdims=True
            )


def shards(
    entering_hidden,
    section_weight,
    section_norm_gain,
    plugin_narrowing_factors,
    plugin_widening_factors,
    reward_head,
    adapter_of_block,
    live_block_rows,
):
    sections = lax.axis_size("section")
    section = lax.axis_index("section")
    chips = lax.axis_size("chip")
    cores = lax.axis_size("core")
    owners = chips * cores
    everyone = ("chip", "core")
    batches_here, rows, piece = entering_hidden.shape
    micro = batches_here * sections
    span = BLOCK * SPAN
    per_micro = rows // span
    owned = plugin_narrowing_factors.shape[1]
    rank = plugin_narrowing_factors.shape[3]
    chunks = micro * per_micro
    pairwise = chips == 4 and cores == 2

    chip, core = lax.axis_index("chip"), lax.axis_index("core")
    if pairwise:
        near_by, far = jnp.where(core == 0, 1, 2), jnp.where(core == 0, 2, 1)
        place = chip * cores + core
        parts = [(0, 0), (0, 1), (near_by, 0), (near_by, 1), (3, 0), (far, 1), (far, 0), (3, 1)]
        order = [(chip ^ there) * cores + (core ^ other) for there, other in parts]
    else:
        place = jnp.zeros_like(core)
        order = [i * cores + (core + k) % cores for k in range(cores) for i in range(chips)]
    info = jnp.concatenate([jnp.stack([section, place] + order), adapter_of_block.reshape(-1)])
    info = info.astype(jnp.int32)

    def spread(maps, after):
        if not pairwise:
            maps = jnp.moveaxis(maps.reshape(owned, rank, owners, piece), 2, 0)
            maps = lax.all_to_all(maps, everyone, split_axis=0, concat_axis=0, tiled=True)
            return maps.reshape(owners * owned, rank, piece), after
        out_shape = [pltpu.VMEM((owned, rank, piece), maps.dtype) for _ in range(owners)]
        size = 2 * maps.size
        blocks = list(call(functools.partial(cut_kernel, owners), out_shape, (info, maps), "cut", 0, 2 * size, after=after))
        mine = blocks[:1]
        for k in range(1, owners):
            blocks[k] = lax.ppermute(blocks[k], everyone, [(i, i ^ k) for i in range(owners)])
        out_shape = pltpu.VMEM((owners * owned, rank, piece), maps.dtype)
        return call(stack_kernel, out_shape, (info, *blocks), "stack", 0, 2 * size), mine

    down, cut = spread(jnp.swapaxes(plugin_narrowing_factors[0], 1, 2), ())
    weight = staged(section_weight[0], cut)

    feeds = []
    for m in range(micro):
        home, slot = divmod(m, batches_here)
        block = entering_hidden[slot]
        feeds.append(block if home == 0 else lax.ppermute(block, "section", [(home, 0)]))

    def over_cores(part):
        return [
            lax.ppermute(part, "core", [((c + k) % cores, c) for c in range(cores)]) for k in range(1, cores)
        ]

    def over_chips(part, steps):
        pairs = [(i * cores + c, (i ^ steps[c]) * cores + c) for i in range(chips) for c in range(cores)]
        return lax.ppermute(part, everyone, pairs)

    def gather_start(message):
        if not pairwise:
            parts = lax.all_to_all(message, "chip", split_axis=0, concat_axis=0, tiled=True)
            return [parts] + over_cores(parts)
        first = over_chips(message, (1, 2))
        (other,) = over_cores(message)
        second = over_chips(other, (1, 2))
        return [message, other, first, second]

    def gather_end(parts, after):
        if not pairwise:
            return parts
        message, other, first, second = parts
        first = tie(first, after) if after else first
        third = over_chips(first, (2, 1))
        return [message, other, first, second, third] + [
            swapped for part in (first, second, third) for swapped in over_cores(part)
        ]

    def prep(tick, sources, blocks, after):
        out_shape = (
            pltpu.VMEM((span, piece), jnp.bfloat16),
            pltpu.VMEM((1 if pairwise else chips, span, piece + SIDE), jnp.bfloat16),
        )
        kernel = functools.partial(prep_kernel, rank, owners, owned, tick, chunks, blocks)
        args = (info, *sources, section_norm_gain, down)
        return call(kernel, out_shape, args, "prep", 2 * span * piece * SIDE, span * piece * 8, after=after)

    def layer(tick, parts, x, after):
        counts = tuple(part.shape[0] for part in parts)
        width = piece * owners
        kernel = functools.partial(layer_kernel, rank, owners, owned, tick, chunks, counts)
        args = (info, *parts, weight, x, up)
        out_shape = pltpu.VMEM((span, piece), jnp.bfloat16)
        return call(kernel, out_shape, args, "layer", 2 * span * width * piece, 2 * width * piece, after=after)

    arrived, state, hs, done, home_blocks, returned = {}, {}, {}, {}, {}, {}
    ticks = chunks + LAG * (sections - 1)

    def active(tick):
        return [s for s in range(sections) if 0 <= tick - LAG * s < chunks]

    def begin(tick):
        sources, blocks = [], []
        if 0 in active(tick):
            m, b = divmod(tick, per_micro)
            sources.append(feeds[m])
            blocks.append(b)
        if active(tick) != [0]:
            sources.append(arrived.pop(tick))
            blocks.append(0)
        if tick == 0:
            after = [weight]
        elif LAG == 2:
            after = [state[tick - 1][2][4 if pairwise else 0]]
        else:
            after = [hs[tick - 2]] if tick >= 2 else []
        x, message = prep(tick, sources, blocks, after)
        state[tick] = [x, message, gather_start(message)]

    begin(0)
    state[0][2] = gather_end(state[0][2], [])
    up, _ = spread(plugin_widening_factors[0], (state[0][1],))
    for tick in range(ticks):
        after = []
        if tick + 1 < ticks:
            begin(tick + 1)
            after.append(state[tick + 1][1])
        if tick in returned:
            after.append(returned.pop(tick))
        x, _, parts = state.pop(tick)
        h = hs[tick] = layer(tick, parts, x, after)
        if tick + 1 < ticks:
            state[tick + 1][2] = gather_end(state[tick + 1][2], [h])
        onward = [(s, s + 1) for s in active(tick) if s + 1 < sections]
        if onward:
            arrived[tick + LAG] = lax.ppermute(h, "section", onward)
        if sections - 1 in active(tick):
            last = tick - LAG * (sections - 1)
            done[last] = h
            if last % per_micro == per_micro - 1:
                m = last // per_micro
                block = [done[m * per_micro + b] for b in range(per_micro)]
                if per_micro > 1:
                    out_shape = pltpu.VMEM((rows, piece), jnp.bfloat16)
                    block = call(join_kernel, out_shape, (info, *block), "join", 0, rows * piece * 4)
                else:
                    block = block[0]
                home = m // batches_here
                if home != sections - 1:
                    block = lax.ppermute(block, "section", [(sections - 1, home)])
                    returned[tick + 2] = block
                home_blocks[m] = block

    hidden, partial_score = [], []
    for slot in range(batches_here):
        out_shape = (
            jax.ShapeDtypeStruct((rows, piece), jnp.bfloat16),
            jax.ShapeDtypeStruct((rows, 1), jnp.float32),
        )
        block = [home_blocks[home * batches_here + slot] for home in range(sections)]
        kernel = functools.partial(finish_kernel, sections)
        args = (info, *block, reward_head[None])
        h, s = call(kernel, out_shape, args, "finish", 2 * rows * piece, rows * piece * 4)
        hidden.append(h)
        partial_score.append(s[:, 0])
    raw = lax.psum(jnp.stack(partial_score), everyone)
    place = jnp.arange(rows, dtype=jnp.int32) % BLOCK
    limits = jnp.repeat(live_block_rows, BLOCK, axis=1)
    scores = jnp.where(place[None, :] < limits, raw, jnp.float32(0.0))
    return (jnp.stack(hidden), scores)


def solution(mesh):
    sections, owners = mesh.shape["section"], mesh.shape["mp"]
    cores = 2 if owners % 2 == 0 else 1
    fine = jax.sharding.Mesh(
        mesh.devices.reshape(sections, owners // cores, cores), ("section", "chip", "core")
    )
    mp = ("chip", "core")
    placed = (
        P("section", None, mp),
        P("section", None, mp),
        P("section", mp),
        P("section", mp, None, None),
        P("section", mp, None, None),
        P(mp),
        P(),
        P("section", None),
    )
    return jax.shard_map(
        shards,
        mesh=fine,
        in_specs=placed,
        out_specs=(P("section", None, mp), P("section", None)),
        check_vma=False,
    )
```

```python
import functools

import jax
import jax.numpy as jnp
from jax import lax
from jax.experimental import pallas as pl
from jax.experimental.pallas import tpu as pltpu
from jax.sharding import PartitionSpec as P

BLOCK = 128
SIDE = 128
LAG = 2
SPAN = 1

VMEM = pl.BlockSpec(memory_space=pltpu.VMEM)
SMEM = pl.BlockSpec(memory_space=pltpu.SMEM)


def near(x):
    return pltpu.with_memory_space_constraint(x, pltpu.VMEM)


def call(kernel, out_shape, args, name, flops, moved, limit=8, after=()):
    info, *arrays = args
    count = len(arrays)

    def body(info_ref, *refs):
        kernel(info_ref, *refs[:count], *refs[count + len(after) :])

    return pl.pallas_call(
        body,
        out_shape=out_shape,
        in_specs=[SMEM] + [VMEM] * count + [pl.BlockSpec(memory_space=pl.ANY)] * len(after),
        out_specs=jax.tree.map(lambda _: VMEM, out_shape),
        compiler_params=pltpu.CompilerParams(vmem_limit_bytes=limit << 20),
        cost_estimate=pl.CostEstimate(flops=flops, bytes_accessed=moved, transcendentals=0),
        name=name,
    )(info, *map(near, arrays), *after)


def tie(x, after):
    def body(*_):
        pass

    return pl.pallas_call(
        body,
        out_shape=pltpu.VMEM(x.shape, x.dtype),
        in_specs=[VMEM] + [pl.BlockSpec(memory_space=pl.ANY)] * len(after),
        out_specs=VMEM,
        input_output_aliases={0: 0},
        compiler_params=pltpu.CompilerParams(vmem_limit_bytes=1 << 20),
        cost_estimate=pl.CostEstimate(flops=0, bytes_accessed=0, transcendentals=0),
        name="tie",
    )(near(x), *after)


def adapter_at(info_ref, owners, owned, tick, chunks, block):
    mine = jnp.clip(tick - LAG * info_ref[0], 0, chunks - 1)
    adapter = info_ref[2 + owners + mine * SPAN + block]
    if owned == 1:
        return adapter ^ info_ref[1]
    return (lax.div(adapter, owned) ^ info_ref[1]) * owned + lax.rem(adapter, owned)


def prep_kernel(rank, owners, owned, tick, chunks, block, info_ref, *refs):
    *sources, gain_ref, down_ref, x_ref, m_ref = refs
    copies = m_ref.shape[0]
    rows, piece = x_ref.shape
    picked = [source[b * rows : (b + 1) * rows, :].astype(jnp.float32) for source, b in zip(sources, block)]
    x = jnp.where(info_ref[0] == 0, *picked) if len(picked) == 2 else picked[0]
    x_ref[...] = x.astype(jnp.bfloat16)
    scaled = (x * gain_ref[...].astype(jnp.float32)).astype(jnp.bfloat16)
    squares = jnp.sum(x * x, axis=1, keepdims=True)
    high = squares.astype(jnp.bfloat16).astype(jnp.float32)
    low = squares - high
    lane = lax.broadcasted_iota(jnp.int32, (rows, SIDE), 1)
    inner = []
    for b in range(SPAN):
        product = lax.dot_general(
            scaled[b * BLOCK : (b + 1) * BLOCK],
            down_ref[adapter_at(info_ref, owners, owned, tick, chunks, b)],
            (((1,), (1,)), ((), ())),
            preferred_element_type=jnp.float32,
        )
        inner.append(jnp.concatenate([product, jnp.zeros((BLOCK, SIDE - rank), jnp.float32)], axis=1))
    inner = jnp.concatenate(inner, axis=0) if SPAN > 1 else inner[0]
    side = jnp.where(lane == rank, high, jnp.where(lane == rank + 1, low, inner)).astype(jnp.bfloat16)
    for copy in range(copies):
        m_ref[copy, :, :piece] = scaled
        m_ref[copy, :, piece:] = side


def stage_kernel(w_ref, *refs):
    *_, o_ref, sem = refs
    copy = pltpu.make_async_copy(w_ref, o_ref, sem)
    copy.start()
    copy.wait()


def staged(weight, after):
    return pl.pallas_call(
        stage_kernel,
        out_shape=pltpu.VMEM(weight.shape, weight.dtype),
        in_specs=[pl.BlockSpec(memory_space=pl.ANY)] * (1 + len(after)),
        out_specs=VMEM,
        scratch_shapes=[pltpu.SemaphoreType.DMA],
        compiler_params=pltpu.CompilerParams(vmem_limit_bytes=4 << 20),
        cost_estimate=pl.CostEstimate(flops=0, bytes_accessed=2 * weight.size, transcendentals=0),
        name="stage",
    )(pltpu.with_memory_space_constraint(weight, pltpu.HBM), *after)


def piece_dots(info_ref, w_ref, parts, starts, columns):
    total = None
    for part, start in zip(parts, starts):
        piece = w_ref.shape[1]
        for k in range(part.shape[0]):
            depth = pl.ds(pl.multiple_of(info_ref[2 + start + k] * piece, piece), piece)
            term = jnp.dot(part[k, :, :piece], w_ref[depth, columns], preferred_element_type=jnp.float32)
            total = term if total is None else total + term
    return total


def side_sum(parts, piece):
    return sum(part[k, :, piece:].astype(jnp.float32) for part in parts for k in range(part.shape[0]))


def layer_a_kernel(starts, seeded, info_ref, *refs):
    *parts, w_ref, total_ref, side_ref = refs
    if seeded:
        *parts, old_total, old_side = parts
    piece = w_ref.shape[1]
    side = side_sum(parts, piece)
    side_ref[...] = old_side[...] + side if seeded else side
    tile = min(piece, 256)

    @pl.loop(0, piece // tile)
    def _(n):
        columns = pl.ds(pl.multiple_of(n * tile, tile), tile)
        total = piece_dots(info_ref, w_ref, parts, starts, columns)
        total_ref[:, columns] = old_total[:, columns] + total if seeded else total


def layer_b_kernel(rank, owners, owned, tick, chunks, starts, info_ref, *refs):
    *parts, w_ref, x_ref, up_ref, total_ref, side_ref, o_ref = refs
    piece = x_ref.shape[1]
    width = w_ref.shape[0]
    side = side_ref[...] + side_sum(parts, piece)
    squares = side[:, rank : rank + 1] + side[:, rank + 1 : rank + 2]
    scale = lax.rsqrt(squares / width + 1e-05)
    inner = (2.0 * side[:, :rank]).astype(jnp.bfloat16)
    tile = min(piece, 256)

    @pl.loop(0, piece // tile)
    def _(n):
        columns = pl.ds(pl.multiple_of(n * tile, tile), tile)
        delta = [
            jnp.dot(
                inner[b * BLOCK : (b + 1) * BLOCK],
                up_ref[adapter_at(info_ref, owners, owned, tick, chunks, b), :, columns],
                preferred_element_type=jnp.float32,
            )
            for b in range(SPAN)
        ]
        total = jnp.concatenate(delta, axis=0) if SPAN > 1 else delta[0]
        total += total_ref[:, columns] + piece_dots(info_ref, w_ref, parts, starts, columns)
        h = x_ref[:, columns].astype(jnp.float32)
        o_ref[:, columns] = (h + scale * total).astype(jnp.bfloat16)


def join_kernel(info_ref, *refs):
    *blocks, o_ref = refs
    rows = blocks[0].shape[0]
    for i, block in enumerate(blocks):
        o_ref[i * rows : (i + 1) * rows, :] = block[...]


def finish_kernel(sections, counts, info_ref, *refs):
    *blocks, head_ref, o_ref, score_ref = refs
    taken = 0
    for section, count in zip(range(sections), counts):
        own = blocks[taken : taken + count]
        taken += count

        @pl.when(info_ref[0] == section)
        def _():
            row = 0
            for block in own:
                span = block.shape[0]
                h = block[...]
                o_ref[row : row + span, :] = h
                score_ref[:, row : row + span] = lax.dot_general(
                    head_ref[...], h, (((1,), (1,)), ((), ())), preferred_element_type=jnp.float32
                )
                row += span


def add_kernel(info_ref, *refs):
    *terms, o_ref = refs
    o_ref[...] = sum(term[...] for term in terms)


def score_kernel(info_ref, limits_ref, *refs):
    *terms, o_ref = refs
    total = sum(term[...] for term in terms)
    lane = lax.broadcasted_iota(jnp.int32, (1, BLOCK), 1)
    for b in range(total.shape[1] // BLOCK):
        columns = slice(b * BLOCK, (b + 1) * BLOCK)
        o_ref[:, columns] = jnp.where(lane < limits_ref[:, b : b + 1], total[:, columns], 0.0)


def cut_kernel(owners, info_ref, maps_ref, *outs):
    piece = outs[0].shape[2]
    for k, out in enumerate(outs):
        out[...] = maps_ref[:, :, pl.ds(pl.multiple_of((info_ref[1] ^ k) * piece, piece), piece)]


def stack_kernel(info_ref, *refs):
    *blocks, o_ref = refs
    owned = blocks[0].shape[0]
    for i, block in enumerate(blocks):
        o_ref[i * owned : (i + 1) * owned] = block[...]


def shards(
    entering_hidden,
    section_weight,
    section_norm_gain,
    plugin_narrowing_factors,
    plugin_widening_factors,
    reward_head,
    adapter_of_block,
    live_block_rows,
):
    sections = lax.axis_size("section")
    section = lax.axis_index("section")
    chips = lax.axis_size("chip")
    cores = lax.axis_size("core")
    owners = chips * cores
    everyone = ("chip", "core")
    batches_here, rows, piece = entering_hidden.shape
    micro = batches_here * sections
    span = BLOCK * SPAN
    per_micro = rows // span
    owned = plugin_narrowing_factors.shape[1]
    rank = plugin_narrowing_factors.shape[3]
    chunks = micro * per_micro
    pairwise = chips == 4 and cores == 2

    chip, core = lax.axis_index("chip"), lax.axis_index("core")
    if pairwise:
        near_by, far = jnp.where(core == 0, 1, 2), jnp.where(core == 0, 2, 1)
        place = chip * cores + core
        parts = [(0, 0), (0, 1), (near_by, 0), (near_by, 1), (3, 0), (far, 1), (far, 0), (3, 1)]
        order = [(chip ^ there) * cores + (core ^ other) for there, other in parts]
    else:
        place = jnp.zeros_like(core)
        order = [i * cores + (core + k) % cores for k in range(cores) for i in range(chips)]
    info = jnp.concatenate([jnp.stack([section, place] + order), adapter_of_block.reshape(-1)])
    info = info.astype(jnp.int32)

    def spread(maps, after):
        if not pairwise:
            maps = jnp.moveaxis(maps.reshape(owned, rank, owners, piece), 2, 0)
            maps = lax.all_to_all(maps, everyone, split_axis=0, concat_axis=0, tiled=True)
            return maps.reshape(owners * owned, rank, piece), after
        out_shape = [pltpu.VMEM((owned, rank, piece), maps.dtype) for _ in range(owners)]
        size = 2 * maps.size
        blocks = list(call(functools.partial(cut_kernel, owners), out_shape, (info, maps), "cut", 0, 2 * size, after=after))
        mine = blocks[:1]
        for k in range(1, owners):
            blocks[k] = lax.ppermute(blocks[k], everyone, [(i, i ^ k) for i in range(owners)])
        out_shape = pltpu.VMEM((owners * owned, rank, piece), maps.dtype)
        return call(stack_kernel, out_shape, (info, *blocks), "stack", 0, 2 * size), mine

    down, cut = spread(jnp.swapaxes(plugin_narrowing_factors[0], 1, 2), ())
    weight = staged(section_weight[0], cut)

    feeds = []
    for m in range(micro):
        home, slot = divmod(m, batches_here)
        block = entering_hidden[slot]
        feeds.append(block if home == 0 else lax.ppermute(block, "section", [(home, 0)]))

    def over_cores(part):
        return [
            lax.ppermute(part, "core", [((c + k) % cores, c) for c in range(cores)]) for k in range(1, cores)
        ]

    def over_chips(part, steps):
        pairs = [(i * cores + c, (i ^ steps[c]) * cores + c) for i in range(chips) for c in range(cores)]
        return lax.ppermute(part, everyone, pairs)

    def gather_start(message):
        if not pairwise:
            parts = lax.all_to_all(message, "chip", split_axis=0, concat_axis=0, tiled=True)
            return [parts] + over_cores(parts)
        first = over_chips(message, (1, 2))
        (other,) = over_cores(message)
        second = over_chips(other, (1, 2))
        return [message, other, first, second]

    def gather_end(parts, after):
        if not pairwise:
            return [], [(part, chips * (1 + k)) for k, part in enumerate(parts[1:])]
        _, _, first, second = parts
        first = tie(first, after) if after else first
        third = over_chips(first, (2, 1))
        swapped = [over_cores(part)[0] for part in (first, second, third)]
        return [(first, 2), (second, 3), (swapped[0], 5), (swapped[1], 6)], [(third, 4), (swapped[2], 7)]

    def prep(tick, sources, blocks, after):
        out_shape = (
            pltpu.VMEM((span, piece), jnp.bfloat16),
            pltpu.VMEM((1 if pairwise else chips, span, piece + SIDE), jnp.bfloat16),
        )
        kernel = functools.partial(prep_kernel, rank, owners, owned, tick, chunks, blocks)
        args = (info, *sources, section_norm_gain, down)
        return call(kernel, out_shape, args, "prep", 2 * span * piece * SIDE, span * piece * 8, after=after)

    def layer_a(parts, seed, after):
        width = piece * owners
        kernel = functools.partial(layer_a_kernel, [start for _, start in parts], bool(seed))
        out_shape = (pltpu.VMEM((span, piece), jnp.float32), pltpu.VMEM((span, SIDE), jnp.float32))
        args = (info, *[part for part, _ in parts], *seed, weight)
        return call(kernel, out_shape, args, "layer_a", span * width * piece, width * piece, after=after)

    def layer_b(tick, parts, x, sums, after):
        width = piece * owners
        kernel = functools.partial(
            layer_b_kernel, rank, owners, owned, tick, chunks, [start for _, start in parts]
        )
        args = (info, *[part for part, _ in parts], weight, x, up, *sums)
        out_shape = pltpu.VMEM((span, piece), jnp.bfloat16)
        return call(kernel, out_shape, args, "layer_b", span * width * piece // 2, width * piece // 2, after=after)

    arrived, state, sums, done, home_blocks, returned = {}, {}, {}, {}, {}, {}
    ticks = chunks + LAG * (sections - 1)

    def active(tick):
        return [s for s in range(sections) if 0 <= tick - LAG * s < chunks]

    def begin(tick):
        sources, blocks = [], []
        if 0 in active(tick):
            m, b = divmod(tick, per_micro)
            sources.append(feeds[m])
            blocks.append(b)
        if active(tick) != [0]:
            sources.append(arrived.pop(tick))
            blocks.append(0)
        if tick == 0:
            after = [weight]
        else:
            after = [sums[tick - 1][1]]
        x, message = prep(tick, sources, blocks, after)
        state[tick] = [x, message, gather_start(message)]

    def own_chip(tick, after):
        parts = state[tick][2]
        own = [(parts[0], 0), (parts[1], 1)] if pairwise else [(parts[0], 0)]
        sums[tick] = layer_a(own, (), after)
        state[tick][2:] = gather_end(parts, [sums[tick][1]] if after else [])

    def near_chips(tick, after):
        if state[tick][2]:
            sums[tick] = layer_a(state[tick][2], sums[tick], after)

    up, _ = spread(plugin_widening_factors[0], (weight,))
    begin(0)
    own_chip(0, [])
    for tick in range(ticks):
        after = []
        if tick + 1 < ticks:
            begin(tick + 1)
            after.append(state[tick + 1][1])
        near_chips(tick, after)
        after = []
        if tick in returned:
            after.append(returned.pop(tick))
        x, _, _, parts = state.pop(tick)
        h = layer_b(tick, parts, x, sums[tick], after)
        if tick + 1 < ticks:
            own_chip(tick + 1, [h])
        onward = [(s, s + 1) for s in active(tick) if s + 1 < sections]
        if onward:
            arrived[tick + LAG] = lax.ppermute(h, "section", onward)
        if sections - 1 in active(tick):
            last = tick - LAG * (sections - 1)
            done[last] = h
            if last % per_micro == per_micro - 1:
                m = last // per_micro
                block = [done[m * per_micro + b] for b in range(per_micro)]
                home = m // batches_here
                if home != sections - 1:
                    if per_micro > 1:
                        out_shape = pltpu.VMEM((rows, piece), jnp.bfloat16)
                        block = [call(join_kernel, out_shape, (info, *block), "join", 0, rows * piece * 4)]
                    block = [lax.ppermute(block[0], "section", [(sections - 1, home)])]
                    returned[tick + 2] = block[0]
                home_blocks[m] = block

    hidden, scores = [], []
    for slot in range(batches_here):
        blocks = [home_blocks[home * batches_here + slot] for home in range(sections)]
        out_shape = (
            jax.ShapeDtypeStruct((rows, piece), jnp.bfloat16),
            pltpu.VMEM((1, rows), jnp.float32),
        )
        kernel = functools.partial(finish_kernel, sections, [len(block) for block in blocks])
        args = (info, *[part for block in blocks for part in block], reward_head[None])
        h, score = call(kernel, out_shape, args, "finish", 2 * rows * piece, rows * piece * 4)
        hidden.append(h)
        near_by = pltpu.VMEM((1, rows), jnp.float32)
        if pairwise:
            score = call(add_kernel, near_by, (info, score, *over_cores(score)), "add", 0, rows * 4)
            terms = [score] + [over_chips(score, (k, k)) for k in (1, 2, 3)]
        else:
            terms = [lax.psum(score, everyone)]
        limits = live_block_rows[slot : slot + 1]
        out_shape = jax.ShapeDtypeStruct((1, rows), jnp.float32)
        scores.append(call(score_kernel, out_shape, (info, limits, *terms), "score", 0, rows * 4))
    if batches_here == 1:
        return (hidden[0][None], scores[0])
    return (jnp.stack(hidden), jnp.concatenate(scores, axis=0))


def solution(mesh):
    sections, owners = mesh.shape["section"], mesh.shape["mp"]
    cores = 2 if owners % 2 == 0 else 1
    fine = jax.sharding.Mesh(
        mesh.devices.reshape(sections, owners // cores, cores), ("section", "chip", "core")
    )
    mp = ("chip", "core")
    placed = (
        P("section", None, mp),
        P("section", None, mp),
        P("section", mp),
        P("section", mp, None, None),
        P("section", mp, None, None),
        P(mp),
        P(),
        P("section", None),
    )
    return jax.shard_map(
        shards,
        mesh=fine,
        in_specs=placed,
        out_specs=(P("section", None, mp), P("section", None)),
        check_vma=False,
    )
```

```python
import functools

import jax
import jax.numpy as jnp
from jax import lax
from jax.experimental import pallas as pl
from jax.experimental.pallas import tpu as pltpu
from jax.sharding import PartitionSpec as P

BLOCK = 128
SIDE = 128
LAG = 2
SPAN = 1

VMEM = pl.BlockSpec(memory_space=pltpu.VMEM)
SMEM = pl.BlockSpec(memory_space=pltpu.SMEM)


def near(x):
    return pltpu.with_memory_space_constraint(x, pltpu.VMEM)


def call(kernel, out_shape, args, name, flops, moved, limit=8, after=()):
    info, *arrays = args
    count = len(arrays)

    def body(info_ref, *refs):
        kernel(info_ref, *refs[:count], *refs[count + len(after) :])

    return pl.pallas_call(
        body,
        out_shape=out_shape,
        in_specs=[SMEM] + [VMEM] * count + [pl.BlockSpec(memory_space=pl.ANY)] * len(after),
        out_specs=jax.tree.map(lambda _: VMEM, out_shape),
        compiler_params=pltpu.CompilerParams(vmem_limit_bytes=limit << 20),
        cost_estimate=pl.CostEstimate(flops=flops, bytes_accessed=moved, transcendentals=0),
        name=name,
    )(info, *map(near, arrays), *after)


def tie(x, after, flops=0, moved=0):
    def body(*_):
        pass

    return pl.pallas_call(
        body,
        out_shape=pltpu.VMEM(x.shape, x.dtype),
        in_specs=[VMEM] + [pl.BlockSpec(memory_space=pl.ANY)] * len(after),
        out_specs=VMEM,
        input_output_aliases={0: 0},
        compiler_params=pltpu.CompilerParams(vmem_limit_bytes=1 << 20),
        cost_estimate=pl.CostEstimate(flops=flops, bytes_accessed=moved, transcendentals=0),
        name="tie",
    )(near(x), *after)


def adapter_at(info_ref, owners, owned, tick, chunks, block):
    mine = jnp.clip(tick - LAG * info_ref[0], 0, chunks - 1)
    adapter = info_ref[2 + owners + mine * SPAN + block]
    if owned == 1:
        return adapter ^ info_ref[1]
    return (lax.div(adapter, owned) ^ info_ref[1]) * owned + lax.rem(adapter, owned)


def prep_kernel(rank, owners, owned, tick, chunks, block, info_ref, *refs):
    *sources, gain_ref, down_ref, x_ref, m_ref = refs
    copies = m_ref.shape[0]
    rows, piece = x_ref.shape
    picked = [source[b * rows : (b + 1) * rows, :].astype(jnp.float32) for source, b in zip(sources, block)]
    x = jnp.where(info_ref[0] == 0, *picked) if len(picked) == 2 else picked[0]
    x_ref[...] = x.astype(jnp.bfloat16)
    scaled = (x * gain_ref[...].astype(jnp.float32)).astype(jnp.bfloat16)
    squares = jnp.sum(x * x, axis=1, keepdims=True)
    high = squares.astype(jnp.bfloat16).astype(jnp.float32)
    low = squares - high
    lane = lax.broadcasted_iota(jnp.int32, (rows, SIDE), 1)
    inner = []
    for b in range(SPAN):
        product = lax.dot_general(
            scaled[b * BLOCK : (b + 1) * BLOCK],
            down_ref[adapter_at(info_ref, owners, owned, tick, chunks, b)],
            (((1,), (1,)), ((), ())),
            preferred_element_type=jnp.float32,
        )
        inner.append(jnp.concatenate([product, jnp.zeros((BLOCK, SIDE - rank), jnp.float32)], axis=1))
    inner = jnp.concatenate(inner, axis=0) if SPAN > 1 else inner[0]
    side = jnp.where(lane == rank, high, jnp.where(lane == rank + 1, low, inner)).astype(jnp.bfloat16)
    for copy in range(copies):
        m_ref[copy, :, :piece] = scaled
        m_ref[copy, :, piece:] = side


def stage_kernel(w_ref, *refs):
    *_, o_ref, sem = refs
    copy = pltpu.make_async_copy(w_ref, o_ref, sem)
    copy.start()
    copy.wait()


def staged(weight, after):
    return pl.pallas_call(
        stage_kernel,
        out_shape=pltpu.VMEM(weight.shape, weight.dtype),
        in_specs=[pl.BlockSpec(memory_space=pl.ANY)] * (1 + len(after)),
        out_specs=VMEM,
        scratch_shapes=[pltpu.SemaphoreType.DMA],
        compiler_params=pltpu.CompilerParams(vmem_limit_bytes=4 << 20),
        cost_estimate=pl.CostEstimate(flops=0, bytes_accessed=2 * weight.size, transcendentals=0),
        name="stage",
    )(pltpu.with_memory_space_constraint(weight, pltpu.HBM), *after)


def piece_dots(info_ref, w_ref, parts, starts, columns):
    total = None
    for part, start in zip(parts, starts):
        piece = w_ref.shape[1]
        for k in range(part.shape[0]):
            depth = pl.ds(pl.multiple_of(info_ref[2 + start + k] * piece, piece), piece)
            term = jnp.dot(part[k, :, :piece], w_ref[depth, columns], preferred_element_type=jnp.float32)
            total = term if total is None else total + term
    return total


def side_sum(parts, piece):
    return sum(part[k, :, piece:].astype(jnp.float32) for part in parts for k in range(part.shape[0]))


def own_kernel(starts, info_ref, *refs):
    *parts, w_ref, total_ref, side_ref = refs
    piece = w_ref.shape[1]
    side_ref[...] = side_sum(parts, piece)
    tile = min(piece, 256)
    for n in range(piece // tile):
        columns = slice(n * tile, (n + 1) * tile)
        total_ref[:, columns] = piece_dots(info_ref, w_ref, parts, starts, columns)


def layer_kernel(rank, owners, owned, tick, chunks, starts, info_ref, *refs):
    *parts, w_ref, x_ref, up_ref, total_ref, side_ref, o_ref = refs
    piece = x_ref.shape[1]
    width = w_ref.shape[0]
    side = side_ref[...] + side_sum(parts, piece)
    squares = side[:, rank : rank + 1] + side[:, rank + 1 : rank + 2]
    scale = lax.rsqrt(squares / width + 1e-05)
    inner = (2.0 * side[:, :rank]).astype(jnp.bfloat16)
    rows_of = [adapter_at(info_ref, owners, owned, tick, chunks, b) for b in range(SPAN)]
    tile = min(piece, 256)
    for n in range(piece // tile):
        columns = slice(n * tile, (n + 1) * tile)
        delta = [
            jnp.dot(
                inner[b * BLOCK : (b + 1) * BLOCK], up_ref[row, :, columns], preferred_element_type=jnp.float32
            )
            for b, row in enumerate(rows_of)
        ]
        total = jnp.concatenate(delta, axis=0) if SPAN > 1 else delta[0]
        total += total_ref[:, columns] + piece_dots(info_ref, w_ref, parts, starts, columns)
        h = x_ref[:, columns].astype(jnp.float32)
        o_ref[:, columns] = (h + scale * total).astype(jnp.bfloat16)


def join_kernel(info_ref, *refs):
    *blocks, o_ref = refs
    rows = blocks[0].shape[0]
    for i, block in enumerate(blocks):
        o_ref[i * rows : (i + 1) * rows, :] = block[...]


def finish_kernel(sections, counts, info_ref, *refs):
    *blocks, head_ref, o_ref, score_ref = refs
    taken = 0
    for section, count in zip(range(sections), counts):
        own = blocks[taken : taken + count]
        taken += count

        @pl.when(info_ref[0] == section)
        def _():
            row = 0
            for block in own:
                span = block.shape[0]
                h = block[...]
                o_ref[row : row + span, :] = h
                score_ref[:, row : row + span] = lax.dot_general(
                    head_ref[...], h, (((1,), (1,)), ((), ())), preferred_element_type=jnp.float32
                )
                row += span


def add_kernel(info_ref, *refs):
    *terms, o_ref = refs
    o_ref[...] = sum(term[...] for term in terms)


def score_kernel(info_ref, limits_ref, *refs):
    *terms, o_ref = refs
    total = sum(term[...] for term in terms)
    lane = lax.broadcasted_iota(jnp.int32, (1, BLOCK), 1)
    for b in range(total.shape[1] // BLOCK):
        columns = slice(b * BLOCK, (b + 1) * BLOCK)
        o_ref[:, columns] = jnp.where(lane < limits_ref[:, b : b + 1], total[:, columns], 0.0)


def cut_kernel(owners, info_ref, maps_ref, *outs):
    piece = outs[0].shape[2]
    for k, out in enumerate(outs):
        out[...] = maps_ref[:, :, pl.ds(pl.multiple_of((info_ref[1] ^ k) * piece, piece), piece)]


def stack_kernel(info_ref, *refs):
    *blocks, o_ref = refs
    owned = blocks[0].shape[0]
    for i, block in enumerate(blocks):
        o_ref[i * owned : (i + 1) * owned] = block[...]


def shards(
    entering_hidden,
    section_weight,
    section_norm_gain,
    plugin_narrowing_factors,
    plugin_widening_factors,
    reward_head,
    adapter_of_block,
    live_block_rows,
):
    sections = lax.axis_size("section")
    section = lax.axis_index("section")
    chips = lax.axis_size("chip")
    cores = lax.axis_size("core")
    owners = chips * cores
    everyone = ("chip", "core")
    batches_here, rows, piece = entering_hidden.shape
    micro = batches_here * sections
    span = BLOCK * SPAN
    per_micro = rows // span
    owned = plugin_narrowing_factors.shape[1]
    rank = plugin_narrowing_factors.shape[3]
    chunks = micro * per_micro
    pairwise = chips == 4 and cores == 2

    chip, core = lax.axis_index("chip"), lax.axis_index("core")
    if pairwise:
        near_by, far = jnp.where(core == 0, 1, 2), jnp.where(core == 0, 2, 1)
        place = chip * cores + core
        parts = [(0, 0), (0, 1), (near_by, 0), (near_by, 1), (3, 0), (far, 1), (far, 0), (3, 1)]
        order = [(chip ^ there) * cores + (core ^ other) for there, other in parts]
    else:
        place = jnp.zeros_like(core)
        order = [i * cores + (core + k) % cores for k in range(cores) for i in range(chips)]
    info = jnp.concatenate([jnp.stack([section, place] + order), adapter_of_block.reshape(-1)])
    info = info.astype(jnp.int32)

    def spread(maps, after):
        if not pairwise:
            maps = jnp.moveaxis(maps.reshape(owned, rank, owners, piece), 2, 0)
            maps = lax.all_to_all(maps, everyone, split_axis=0, concat_axis=0, tiled=True)
            return maps.reshape(owners * owned, rank, piece), after
        out_shape = [pltpu.VMEM((owned, rank, piece), maps.dtype) for _ in range(owners)]
        size = 2 * maps.size
        blocks = list(call(functools.partial(cut_kernel, owners), out_shape, (info, maps), "cut", 0, 2 * size, after=after))
        mine = blocks[:1]
        for k in range(1, owners):
            blocks[k] = lax.ppermute(blocks[k], everyone, [(i, i ^ k) for i in range(owners)])
        out_shape = pltpu.VMEM((owners * owned, rank, piece), maps.dtype)
        return call(stack_kernel, out_shape, (info, *blocks), "stack", 0, 2 * size), mine

    down, cut = spread(jnp.swapaxes(plugin_narrowing_factors[0], 1, 2), ())
    weight = staged(section_weight[0], cut)

    feeds = []
    for m in range(micro):
        home, slot = divmod(m, batches_here)
        block = entering_hidden[slot]
        feeds.append(block if home == 0 else lax.ppermute(block, "section", [(home, 0)]))

    def over_cores(part):
        return [
            lax.ppermute(part, "core", [((c + k) % cores, c) for c in range(cores)]) for k in range(1, cores)
        ]

    def over_chips(part, steps):
        pairs = [(i * cores + c, (i ^ steps[c]) * cores + c) for i in range(chips) for c in range(cores)]
        return lax.ppermute(part, everyone, pairs)

    def gather_start(message):
        if not pairwise:
            parts = lax.all_to_all(message, "chip", split_axis=0, concat_axis=0, tiled=True)
            return [parts] + over_cores(parts)
        first = over_chips(message, (1, 2))
        (other,) = over_cores(message)
        second = over_chips(other, (1, 2))
        return [message, other, first, second]

    def gather_end(parts, after):
        if not pairwise:
            return [(part, chips * (1 + k)) for k, part in enumerate(parts[1:])]
        _, _, first, second = parts
        first = tie(first, after) if after else first
        third = over_chips(first, (2, 1))
        late = [first, second, third] + [over_cores(part)[0] for part in (first, second, third)]
        return list(zip(late, range(2, 8)))

    def prep(tick, sources, blocks, after):
        out_shape = (
            pltpu.VMEM((span, piece), jnp.bfloat16),
            pltpu.VMEM((1 if pairwise else chips, span, piece + SIDE), jnp.bfloat16),
        )
        kernel = functools.partial(prep_kernel, rank, owners, owned, tick, chunks, blocks)
        args = (info, *sources, section_norm_gain, down)
        return call(kernel, out_shape, args, "prep", 2 * span * piece * SIDE, span * piece * 8, after=after)

    def own_layer(parts, after):
        width = piece * owners
        kernel = functools.partial(own_kernel, [start for _, start in parts])
        out_shape = (pltpu.VMEM((span, piece), jnp.float32), pltpu.VMEM((span, SIDE), jnp.float32))
        args = (info, *[part for part, _ in parts], weight)
        return call(kernel, out_shape, args, "own", span * width * piece // 2, width * piece // 2, after=after)

    def layer(tick, parts, x, sums, after):
        width = piece * owners
        kernel = functools.partial(layer_kernel, rank, owners, owned, tick, chunks, [start for _, start in parts])
        args = (info, *[part for part, _ in parts], weight, x, up, *sums)
        out_shape = pltpu.VMEM((span, piece), jnp.bfloat16)
        return call(kernel, out_shape, args, "layer", 2 * span * width * piece, 2 * width * piece, after=after)

    arrived, state, sums, done, home_blocks, returned = {}, {}, {}, {}, {}, {}
    ticks = chunks + LAG * (sections - 1)

    def active(tick):
        return [s for s in range(sections) if 0 <= tick - LAG * s < chunks]

    def begin(tick):
        sources, blocks = [], []
        if 0 in active(tick):
            m, b = divmod(tick, per_micro)
            sources.append(feeds[m])
            blocks.append(b)
        if active(tick) != [0]:
            sources.append(arrived.pop(tick))
            blocks.append(0)
        if tick == 0:
            after = [weight]
        else:
            after = [sums[tick - 1][1]]
        x, message = prep(tick, sources, blocks, after)
        state[tick] = [x, message, gather_start(message)]

    def own_chip(tick, after):
        parts = state[tick][2]
        own = [(parts[0], 0), (parts[1], 1)] if pairwise else [(parts[0], 0)]
        sums[tick] = own_layer(own, after)
        state[tick][2] = gather_end(parts, [sums[tick][1]] if after else [])

    up, _ = spread(plugin_widening_factors[0], (weight,))
    begin(0)
    own_chip(0, [])
    for tick in range(ticks):
        after = []
        if tick + 1 < ticks:
            begin(tick + 1)
            after.append(state[tick + 1][1])
        if tick in returned:
            after.append(returned.pop(tick))
        x, _, parts = state.pop(tick)
        if pairwise:
            size = piece * piece * owners
            x = tie(x, [part for part, _ in parts[3:5]] + after, span * size, size)
        h = layer(tick, parts, x, sums[tick], after)
        if tick + 1 < ticks:
            own_chip(tick + 1, [h])
        if any(s + 1 < sections for s in active(tick)):
            ring = [(s, (s + 1) % sections) for s in range(sections)]
            arrived[tick + LAG] = lax.ppermute(h, "section", ring)
        if sections - 1 in active(tick):
            last = tick - LAG * (sections - 1)
            done[last] = h
            if last % per_micro == per_micro - 1:
                m = last // per_micro
                block = [done[m * per_micro + b] for b in range(per_micro)]
                home = m // batches_here
                if home != sections - 1:
                    if per_micro > 1:
                        out_shape = pltpu.VMEM((rows, piece), jnp.bfloat16)
                        block = [call(join_kernel, out_shape, (info, *block), "join", 0, rows * piece * 4)]
                    block = [lax.ppermute(block[0], "section", [(sections - 1, home)])]
                    returned[tick + 2] = block[0]
                home_blocks[m] = block

    hidden, scores = [], []
    for slot in range(batches_here):
        blocks = [home_blocks[home * batches_here + slot] for home in range(sections)]
        out_shape = (
            jax.ShapeDtypeStruct((rows, piece), jnp.bfloat16),
            pltpu.VMEM((1, rows), jnp.float32),
        )
        kernel = functools.partial(finish_kernel, sections, [len(block) for block in blocks])
        args = (info, *[part for block in blocks for part in block], reward_head[None])
        h, score = call(kernel, out_shape, args, "finish", 2 * rows * piece, rows * piece * 4)
        hidden.append(h)
        near_by = pltpu.VMEM((1, rows), jnp.float32)
        if pairwise:
            score = call(add_kernel, near_by, (info, score, *over_cores(score)), "add", 0, rows * 4)
            terms = [score] + [over_chips(score, (k, k)) for k in (1, 2, 3)]
        else:
            terms = [lax.psum(score, everyone)]
        limits = live_block_rows[slot : slot + 1]
        out_shape = jax.ShapeDtypeStruct((1, rows), jnp.float32)
        scores.append(call(score_kernel, out_shape, (info, limits, *terms), "score", 0, rows * 4))
    if batches_here == 1:
        return (hidden[0][None], scores[0])
    return (jnp.stack(hidden), jnp.concatenate(scores, axis=0))


def solution(mesh):
    sections, owners = mesh.shape["section"], mesh.shape["mp"]
    cores = 2 if owners % 2 == 0 else 1
    fine = jax.sharding.Mesh(
        mesh.devices.reshape(sections, owners // cores, cores), ("section", "chip", "core")
    )
    mp = ("chip", "core")
    placed = (
        P("section", None, mp),
        P("section", None, mp),
        P("section", mp),
        P("section", mp, None, None),
        P("section", mp, None, None),
        P(mp),
        P(),
        P("section", None),
    )
    return jax.shard_map(
        shards,
        mesh=fine,
        in_specs=placed,
        out_specs=(P("section", None, mp), P("section", None)),
        check_vma=False,
    )
```

```python
import functools

import jax
import jax.numpy as jnp
from jax import lax
from jax.experimental import pallas as pl
from jax.experimental.pallas import tpu as pltpu
from jax.sharding import PartitionSpec as P

BLOCK = 128
SIDE = 128
LAG = 2
SPAN = 1

VMEM = pl.BlockSpec(memory_space=pltpu.VMEM)
SMEM = pl.BlockSpec(memory_space=pltpu.SMEM)


def near(x):
    return pltpu.with_memory_space_constraint(x, pltpu.VMEM)


def call(kernel, out_shape, args, name, flops, moved, limit=8, after=()):
    info, *arrays = args
    count = len(arrays)

    def body(info_ref, *refs):
        kernel(info_ref, *refs[:count], *refs[count + len(after) :])

    return pl.pallas_call(
        body,
        out_shape=out_shape,
        in_specs=[SMEM] + [VMEM] * count + [pl.BlockSpec(memory_space=pl.ANY)] * len(after),
        out_specs=jax.tree.map(lambda _: VMEM, out_shape),
        compiler_params=pltpu.CompilerParams(vmem_limit_bytes=limit << 20),
        cost_estimate=pl.CostEstimate(flops=flops, bytes_accessed=moved, transcendentals=0),
        name=name,
    )(info, *map(near, arrays), *after)


def tie(x, after, flops=0, moved=0):
    def body(*_):
        pass

    return pl.pallas_call(
        body,
        out_shape=pltpu.VMEM(x.shape, x.dtype),
        in_specs=[VMEM] + [pl.BlockSpec(memory_space=pl.ANY)] * len(after),
        out_specs=VMEM,
        input_output_aliases={0: 0},
        compiler_params=pltpu.CompilerParams(vmem_limit_bytes=1 << 20),
        cost_estimate=pl.CostEstimate(flops=flops, bytes_accessed=moved, transcendentals=0),
        name="tie",
    )(near(x), *after)


def adapter_at(info_ref, owners, owned, tick, chunks, block):
    mine = jnp.clip(tick - LAG * info_ref[0], 0, chunks - 1)
    adapter = info_ref[2 + owners + mine * SPAN + block]
    if owned == 1:
        return adapter ^ info_ref[1]
    return (lax.div(adapter, owned) ^ info_ref[1]) * owned + lax.rem(adapter, owned)


def prep_kernel(rank, owners, owned, tick, chunks, block, info_ref, *refs):
    *sources, gain_ref, down_ref, x_ref, m_ref = refs
    copies = m_ref.shape[0]
    rows, piece = x_ref.shape
    picked = [source[b * rows : (b + 1) * rows, :].astype(jnp.float32) for source, b in zip(sources, block)]
    x = jnp.where(info_ref[0] == 0, *picked) if len(picked) == 2 else picked[0]
    x_ref[...] = x.astype(jnp.bfloat16)
    scaled = (x * gain_ref[...].astype(jnp.float32)).astype(jnp.bfloat16)
    squares = jnp.sum(x * x, axis=1, keepdims=True)
    high = squares.astype(jnp.bfloat16).astype(jnp.float32)
    low = squares - high
    lane = lax.broadcasted_iota(jnp.int32, (rows, SIDE), 1)
    inner = []
    for b in range(SPAN):
        product = lax.dot_general(
            scaled[b * BLOCK : (b + 1) * BLOCK],
            down_ref[adapter_at(info_ref, owners, owned, tick, chunks, b)],
            (((1,), (1,)), ((), ())),
            preferred_element_type=jnp.float32,
        )
        inner.append(jnp.concatenate([product, jnp.zeros((BLOCK, SIDE - rank), jnp.float32)], axis=1))
    inner = jnp.concatenate(inner, axis=0) if SPAN > 1 else inner[0]
    side = jnp.where(lane == rank, high, jnp.where(lane == rank + 1, low, inner)).astype(jnp.bfloat16)
    for copy in range(copies):
        m_ref[copy, :, :piece] = scaled
        m_ref[copy, :, piece:] = side


def stage_kernel(w_ref, *refs):
    *_, o_ref, sem = refs
    copy = pltpu.make_async_copy(w_ref, o_ref, sem)
    copy.start()
    copy.wait()


def staged(weight, after):
    return pl.pallas_call(
        stage_kernel,
        out_shape=pltpu.VMEM(weight.shape, weight.dtype),
        in_specs=[pl.BlockSpec(memory_space=pl.ANY)] * (1 + len(after)),
        out_specs=VMEM,
        scratch_shapes=[pltpu.SemaphoreType.DMA],
        compiler_params=pltpu.CompilerParams(vmem_limit_bytes=4 << 20),
        cost_estimate=pl.CostEstimate(flops=0, bytes_accessed=2 * weight.size, transcendentals=0),
        name="stage",
    )(pltpu.with_memory_space_constraint(weight, pltpu.HBM), *after)


def piece_dots(info_ref, w_ref, parts, starts, columns):
    total = None
    for part, start in zip(parts, starts):
        piece = w_ref.shape[1]
        for k in range(part.shape[0]):
            depth = pl.ds(pl.multiple_of(info_ref[2 + start + k] * piece, piece), piece)
            term = jnp.dot(part[k, :, :piece], w_ref[depth, columns], preferred_element_type=jnp.float32)
            total = term if total is None else total + term
    return total


def side_sum(parts, piece):
    return sum(part[k, :, piece:].astype(jnp.float32) for part in parts for k in range(part.shape[0]))


def own_kernel(starts, info_ref, *refs):
    *parts, w_ref, total_ref, side_ref = refs
    piece = w_ref.shape[1]
    side_ref[...] = side_sum(parts, piece)
    tile = min(piece, 256)
    for n in range(piece // tile):
        columns = slice(n * tile, (n + 1) * tile)
        total_ref[:, columns] = piece_dots(info_ref, w_ref, parts, starts, columns)


def layer_kernel(rank, owners, owned, tick, chunks, starts, info_ref, *refs):
    *parts, w_ref, x_ref, up_ref, total_ref, side_ref, o_ref = refs
    piece = x_ref.shape[1]
    width = w_ref.shape[0]
    side = side_ref[...] + side_sum(parts, piece)
    squares = side[:, rank : rank + 1] + side[:, rank + 1 : rank + 2]
    scale = lax.rsqrt(squares / width + 1e-05)
    inner = (2.0 * side[:, :rank]).astype(jnp.bfloat16)
    rows_of = [adapter_at(info_ref, owners, owned, tick, chunks, b) for b in range(SPAN)]
    tile = min(piece, 256)
    for n in range(piece // tile):
        columns = slice(n * tile, (n + 1) * tile)
        delta = [
            jnp.dot(
                inner[b * BLOCK : (b + 1) * BLOCK], up_ref[row, :, columns], preferred_element_type=jnp.float32
            )
            for b, row in enumerate(rows_of)
        ]
        total = jnp.concatenate(delta, axis=0) if SPAN > 1 else delta[0]
        total += total_ref[:, columns] + piece_dots(info_ref, w_ref, parts, starts, columns)
        h = x_ref[:, columns].astype(jnp.float32)
        o_ref[:, columns] = (h + scale * total).astype(jnp.bfloat16)


def join_kernel(info_ref, *refs):
    *blocks, o_ref = refs
    rows = blocks[0].shape[0]
    for i, block in enumerate(blocks):
        o_ref[i * rows : (i + 1) * rows, :] = block[...]


def finish_kernel(sections, counts, info_ref, *refs):
    *blocks, head_ref, o_ref, score_ref = refs
    taken = 0
    for section, count in zip(range(sections), counts):
        own = blocks[taken : taken + count]
        taken += count

        @pl.when(info_ref[0] == section)
        def _():
            row = 0
            for block in own:
                span = block.shape[0]
                h = block[...]
                o_ref[row : row + span, :] = h
                score_ref[:, row : row + span] = lax.dot_general(
                    head_ref[...], h, (((1,), (1,)), ((), ())), preferred_element_type=jnp.float32
                )
                row += span


def add_kernel(info_ref, *refs):
    *terms, o_ref = refs
    o_ref[...] = sum(term[...] for term in terms)


def score_kernel(info_ref, limits_ref, *refs):
    *terms, o_ref = refs
    total = sum(term[...] for term in terms)
    lane = lax.broadcasted_iota(jnp.int32, (1, BLOCK), 1)
    for b in range(total.shape[1] // BLOCK):
        columns = slice(b * BLOCK, (b + 1) * BLOCK)
        o_ref[:, columns] = jnp.where(lane < limits_ref[:, b : b + 1], total[:, columns], 0.0)


def cut(maps_ref, info_ref, place, out):
    piece = out.shape[-1]
    out[...] = maps_ref[:, :, pl.ds(pl.multiple_of((info_ref[1] ^ place) * piece, piece), piece)]


def cut_other_kernel(chips, info_ref, maps_ref, o_ref):
    for k in range(chips):
        cut(maps_ref, info_ref, 2 * k + 1, o_ref.at[k])


def cut_own_kernel(chips, info_ref, maps_ref, other_ref, *outs):
    for k, out in enumerate(outs):
        cut(maps_ref, info_ref, 2 * k, out.at[0])
        out[1] = other_ref[k]


def stack_kernel(info_ref, *refs):
    *blocks, o_ref = refs
    count, owned = blocks[0].shape[:2]
    for i, block in enumerate(blocks):
        for j in range(count):
            start = (i * count + j) * owned
            o_ref[start : start + owned] = block[j]


def shards(
    entering_hidden,
    section_weight,
    section_norm_gain,
    plugin_narrowing_factors,
    plugin_widening_factors,
    reward_head,
    adapter_of_block,
    live_block_rows,
):
    sections = lax.axis_size("section")
    section = lax.axis_index("section")
    chips = lax.axis_size("chip")
    cores = lax.axis_size("core")
    owners = chips * cores
    everyone = ("chip", "core")
    batches_here, rows, piece = entering_hidden.shape
    micro = batches_here * sections
    span = BLOCK * SPAN
    per_micro = rows // span
    owned = plugin_narrowing_factors.shape[1]
    rank = plugin_narrowing_factors.shape[3]
    chunks = micro * per_micro
    pairwise = chips == 4 and cores == 2

    chip, core = lax.axis_index("chip"), lax.axis_index("core")
    if pairwise:
        near_by, far = jnp.where(core == 0, 1, 2), jnp.where(core == 0, 2, 1)
        place = chip * cores + core
        parts = [(0, 0), (0, 1), (near_by, 0), (near_by, 1), (3, 0), (far, 1), (far, 0), (3, 1)]
        order = [(chip ^ there) * cores + (core ^ other) for there, other in parts]
    else:
        place = jnp.zeros_like(core)
        order = [i * cores + (core + k) % cores for k in range(cores) for i in range(chips)]
    info = jnp.concatenate([jnp.stack([section, place] + order), adapter_of_block.reshape(-1)])
    info = info.astype(jnp.int32)

    def over_cores(part):
        return [
            lax.ppermute(part, "core", [((c + k) % cores, c) for c in range(cores)]) for k in range(1, cores)
        ]

    def over_chips(part, steps):
        pairs = [(i * cores + c, (i ^ steps[c]) * cores + c) for i in range(chips) for c in range(cores)]
        return lax.ppermute(part, everyone, pairs)

    def spread(maps, after):
        if not pairwise:
            maps = jnp.moveaxis(maps.reshape(owned, rank, owners, piece), 2, 0)
            maps = lax.all_to_all(maps, everyone, split_axis=0, concat_axis=0, tiled=True)
            return maps.reshape(owners * owned, rank, piece), after
        size = 2 * maps.size
        out_shape = pltpu.VMEM((chips, owned, rank, piece), maps.dtype)
        kernel = functools.partial(cut_other_kernel, chips)
        other = call(kernel, out_shape, (info, maps), "cut_other", 0, size, after=after)
        (swapped,) = over_cores(other)
        out_shape = [pltpu.VMEM((cores, owned, rank, piece), maps.dtype) for _ in range(chips)]
        kernel = functools.partial(cut_own_kernel, chips)
        mine, *blocks = call(kernel, out_shape, (info, maps, swapped), "cut_own", 0, 2 * size)
        blocks = [over_chips(block, (k, k)) for k, block in zip(range(1, chips), blocks)]
        out_shape = pltpu.VMEM((owners * owned, rank, piece), maps.dtype)
        return call(stack_kernel, out_shape, (info, mine, *blocks), "stack", 0, 2 * size), [mine]

    down, begun = spread(jnp.swapaxes(plugin_narrowing_factors[0], 1, 2), ())
    up, _ = spread(plugin_widening_factors[0], begun)
    weight = staged(section_weight[0], begun)

    feeds = []
    for m in range(micro):
        home, slot = divmod(m, batches_here)
        block = entering_hidden[slot]
        feeds.append(block if home == 0 else lax.ppermute(block, "section", [(home, 0)]))

    def gather_start(message):
        if not pairwise:
            parts = lax.all_to_all(message, "chip", split_axis=0, concat_axis=0, tiled=True)
            return [parts] + over_cores(parts)
        first = over_chips(message, (1, 2))
        (other,) = over_cores(message)
        second = over_chips(other, (1, 2))
        return [message, other, first, second]

    def gather_end(parts, after):
        if not pairwise:
            return [(part, chips * (1 + k)) for k, part in enumerate(parts[1:])]
        _, _, first, second = parts
        first = tie(first, after) if after else first
        third = over_chips(first, (2, 1))
        late = [first, second, third] + [over_cores(part)[0] for part in (first, second, third)]
        return list(zip(late, range(2, 8)))

    def prep(tick, sources, blocks, after):
        out_shape = (
            pltpu.VMEM((span, piece), jnp.bfloat16),
            pltpu.VMEM((1 if pairwise else chips, span, piece + SIDE), jnp.bfloat16),
        )
        kernel = functools.partial(prep_kernel, rank, owners, owned, tick, chunks, blocks)
        args = (info, *sources, section_norm_gain, down)
        return call(kernel, out_shape, args, "prep", 2 * span * piece * SIDE, span * piece * 8, after=after)

    def own_layer(parts, after):
        width = piece * owners
        kernel = functools.partial(own_kernel, [start for _, start in parts])
        out_shape = (pltpu.VMEM((span, piece), jnp.float32), pltpu.VMEM((span, SIDE), jnp.float32))
        args = (info, *[part for part, _ in parts], weight)
        return call(kernel, out_shape, args, "own", span * width * piece // 2, width * piece // 2, after=after)

    def layer(tick, parts, x, sums, after):
        width = piece * owners
        kernel = functools.partial(layer_kernel, rank, owners, owned, tick, chunks, [start for _, start in parts])
        args = (info, *[part for part, _ in parts], weight, x, up, *sums)
        out_shape = pltpu.VMEM((span, piece), jnp.bfloat16)
        return call(kernel, out_shape, args, "layer", 2 * span * width * piece, 2 * width * piece, after=after)

    arrived, state, sums, done, home_blocks, returned = {}, {}, {}, {}, {}, {}
    ticks = chunks + LAG * (sections - 1)

    def active(tick):
        return [s for s in range(sections) if 0 <= tick - LAG * s < chunks]

    def begin(tick):
        sources, blocks = [], []
        if 0 in active(tick):
            m, b = divmod(tick, per_micro)
            sources.append(feeds[m])
            blocks.append(b)
        if active(tick) != [0]:
            sources.append(arrived.pop(tick))
            blocks.append(0)
        if tick == 0:
            after = [weight]
        else:
            after = [sums[tick - 1][1]]
        x, message = prep(tick, sources, blocks, after)
        state[tick] = [x, message, gather_start(message)]

    def own_chip(tick, after):
        parts = state[tick][2]
        own = [(parts[0], 0), (parts[1], 1)] if pairwise else [(parts[0], 0)]
        sums[tick] = own_layer(own, after)
        state[tick][2] = gather_end(parts, [sums[tick][1]] if after else [])

    begin(0)
    own_chip(0, [])
    for tick in range(ticks):
        after = []
        if tick + 1 < ticks:
            begin(tick + 1)
            after.append(state[tick + 1][1])
        if tick in returned:
            after.append(returned.pop(tick))
        x, _, parts = state.pop(tick)
        if pairwise:
            size = piece * piece * owners
            x = tie(x, [part for part, _ in parts[3:5]] + after, span * size, size)
        h = layer(tick, parts, x, sums[tick], after)
        if tick + 1 < ticks:
            own_chip(tick + 1, [h])
        onward = [(s, s + 1) for s in active(tick) if s + 1 < sections]
        if onward:
            arrived[tick + LAG] = lax.ppermute(h, "section", onward)
        if sections - 1 in active(tick):
            last = tick - LAG * (sections - 1)
            done[last] = h
            if last % per_micro == per_micro - 1:
                m = last // per_micro
                block = [done[m * per_micro + b] for b in range(per_micro)]
                home = m // batches_here
                if home != sections - 1:
                    if per_micro > 1:
                        out_shape = pltpu.VMEM((rows, piece), jnp.bfloat16)
                        block = [call(join_kernel, out_shape, (info, *block), "join", 0, rows * piece * 4)]
                    block = [lax.ppermute(block[0], "section", [(sections - 1, home)])]
                    returned[tick + 2] = block[0]
                home_blocks[m] = block

    hidden, scores = [], []
    for slot in range(batches_here):
        blocks = [home_blocks[home * batches_here + slot] for home in range(sections)]
        out_shape = (
            jax.ShapeDtypeStruct((rows, piece), jnp.bfloat16),
            pltpu.VMEM((1, rows), jnp.float32),
        )
        kernel = functools.partial(finish_kernel, sections, [len(block) for block in blocks])
        args = (info, *[part for block in blocks for part in block], reward_head[None])
        h, score = call(kernel, out_shape, args, "finish", 2 * rows * piece, rows * piece * 4)
        hidden.append(h)
        near_by = pltpu.VMEM((1, rows), jnp.float32)
        if pairwise:
            score = call(add_kernel, near_by, (info, score, *over_cores(score)), "add", 0, rows * 4)
            terms = [score] + [over_chips(score, (k, k)) for k in (1, 2, 3)]
        else:
            terms = [lax.psum(score, everyone)]
        limits = live_block_rows[slot : slot + 1]
        out_shape = jax.ShapeDtypeStruct((1, rows), jnp.float32)
        scores.append(call(score_kernel, out_shape, (info, limits, *terms), "score", 0, rows * 4))
    if batches_here == 1:
        return (hidden[0][None], scores[0])
    return (jnp.stack(hidden), jnp.concatenate(scores, axis=0))


def solution(mesh):
    sections, owners = mesh.shape["section"], mesh.shape["mp"]
    cores = 2 if owners % 2 == 0 else 1
    fine = jax.sharding.Mesh(
        mesh.devices.reshape(sections, owners // cores, cores), ("section", "chip", "core")
    )
    mp = ("chip", "core")
    placed = (
        P("section", None, mp),
        P("section", None, mp),
        P("section", mp),
        P("section", mp, None, None),
        P("section", mp, None, None),
        P(mp),
        P(),
        P("section", None),
    )
    return jax.shard_map(
        shards,
        mesh=fine,
        in_specs=placed,
        out_specs=(P("section", None, mp), P("section", None)),
        check_vma=False,
    )
```

```python
import functools

import jax
import jax.numpy as jnp
from jax import lax
from jax.experimental import pallas as pl
from jax.experimental.pallas import tpu as pltpu
from jax.sharding import PartitionSpec as P

BLOCK = 128
SIDE = 128
LAG = 2
SPAN = 1

VMEM = pl.BlockSpec(memory_space=pltpu.VMEM)
SMEM = pl.BlockSpec(memory_space=pltpu.SMEM)


def near(x):
    return pltpu.with_memory_space_constraint(x, pltpu.VMEM)


def call(kernel, out_shape, args, name, flops, moved, limit=8, after=()):
    info, *arrays = args
    count = len(arrays)

    def body(info_ref, *refs):
        kernel(info_ref, *refs[:count], *refs[count + len(after) :])

    return pl.pallas_call(
        body,
        out_shape=out_shape,
        in_specs=[SMEM] + [VMEM] * count + [pl.BlockSpec(memory_space=pl.ANY)] * len(after),
        out_specs=jax.tree.map(lambda _: VMEM, out_shape),
        compiler_params=pltpu.CompilerParams(vmem_limit_bytes=limit << 20),
        cost_estimate=pl.CostEstimate(flops=flops, bytes_accessed=moved, transcendentals=0),
        name=name,
    )(info, *map(near, arrays), *after)


def tie(x, after, flops=0, moved=0):
    def body(*_):
        pass

    return pl.pallas_call(
        body,
        out_shape=pltpu.VMEM(x.shape, x.dtype),
        in_specs=[VMEM] + [pl.BlockSpec(memory_space=pl.ANY)] * len(after),
        out_specs=VMEM,
        input_output_aliases={0: 0},
        compiler_params=pltpu.CompilerParams(vmem_limit_bytes=1 << 20),
        cost_estimate=pl.CostEstimate(flops=flops, bytes_accessed=moved, transcendentals=0),
        name="tie",
    )(near(x), *after)


def adapter_at(info_ref, owners, owned, tick, chunks, block):
    mine = jnp.clip(tick - LAG * info_ref[0], 0, chunks - 1)
    adapter = info_ref[2 + owners + mine * SPAN + block]
    if owned == 1:
        return adapter ^ info_ref[1]
    return (lax.div(adapter, owned) ^ info_ref[1]) * owned + lax.rem(adapter, owned)


def prep_kernel(rank, owners, owned, tick, chunks, block, info_ref, *refs):
    *sources, gain_ref, down_ref, x_ref, m_ref = refs
    copies = m_ref.shape[0]
    rows, piece = x_ref.shape
    picked = [source[b * rows : (b + 1) * rows, :].astype(jnp.float32) for source, b in zip(sources, block)]
    x = jnp.where(info_ref[0] == 0, *picked) if len(picked) == 2 else picked[0]
    x_ref[...] = x.astype(jnp.bfloat16)
    scaled = (x * gain_ref[...].astype(jnp.float32)).astype(jnp.bfloat16)
    squares = jnp.sum(x * x, axis=1, keepdims=True)
    high = squares.astype(jnp.bfloat16).astype(jnp.float32)
    low = squares - high
    lane = lax.broadcasted_iota(jnp.int32, (rows, SIDE), 1)
    inner = []
    for b in range(SPAN):
        product = lax.dot_general(
            scaled[b * BLOCK : (b + 1) * BLOCK],
            down_ref[adapter_at(info_ref, owners, owned, tick, chunks, b)],
            (((1,), (1,)), ((), ())),
            preferred_element_type=jnp.float32,
        )
        inner.append(jnp.concatenate([product, jnp.zeros((BLOCK, SIDE - rank), jnp.float32)], axis=1))
    inner = jnp.concatenate(inner, axis=0) if SPAN > 1 else inner[0]
    side = jnp.where(lane == rank, high, jnp.where(lane == rank + 1, low, inner)).astype(jnp.bfloat16)
    for copy in range(copies):
        m_ref[copy, :, :piece] = scaled
        m_ref[copy, :, piece:] = side


def stage_kernel(w_ref, *refs):
    *_, o_ref, sem = refs
    copy = pltpu.make_async_copy(w_ref, o_ref, sem)
    copy.start()
    copy.wait()


def staged(weight, after):
    return pl.pallas_call(
        stage_kernel,
        out_shape=pltpu.VMEM(weight.shape, weight.dtype),
        in_specs=[pl.BlockSpec(memory_space=pl.ANY)] * (1 + len(after)),
        out_specs=VMEM,
        scratch_shapes=[pltpu.SemaphoreType.DMA],
        compiler_params=pltpu.CompilerParams(vmem_limit_bytes=4 << 20),
        cost_estimate=pl.CostEstimate(flops=0, bytes_accessed=0, transcendentals=0),
        name="stage",
    )(pltpu.with_memory_space_constraint(weight, pltpu.HBM), *after)


def piece_dots(info_ref, w_ref, parts, starts, columns):
    total = None
    for part, start in zip(parts, starts):
        piece = w_ref.shape[1]
        for k in range(part.shape[0]):
            depth = pl.ds(pl.multiple_of(info_ref[2 + start + k] * piece, piece), piece)
            term = jnp.dot(part[k, :, :piece], w_ref[depth, columns], preferred_element_type=jnp.float32)
            total = term if total is None else total + term
    return total


def side_sum(parts, piece):
    return sum(part[k, :, piece:].astype(jnp.float32) for part in parts for k in range(part.shape[0]))


def own_kernel(starts, info_ref, *refs):
    *parts, w_ref, total_ref, side_ref = refs
    piece = w_ref.shape[1]
    side_ref[...] = side_sum(parts, piece)
    tile = min(piece, 256)
    for n in range(piece // tile):
        columns = slice(n * tile, (n + 1) * tile)
        total_ref[:, columns] = piece_dots(info_ref, w_ref, parts, starts, columns)


def layer_kernel(rank, owners, owned, tick, chunks, starts, info_ref, *refs):
    *parts, w_ref, x_ref, up_ref, total_ref, side_ref, o_ref = refs
    piece = x_ref.shape[1]
    width = w_ref.shape[0]
    side = side_ref[...] + side_sum(parts, piece)
    squares = side[:, rank : rank + 1] + side[:, rank + 1 : rank + 2]
    scale = lax.rsqrt(squares / width + 1e-05)
    inner = (2.0 * side[:, :rank]).astype(jnp.bfloat16)
    rows_of = [adapter_at(info_ref, owners, owned, tick, chunks, b) for b in range(SPAN)]
    tile = min(piece, 256)
    for n in range(piece // tile):
        columns = slice(n * tile, (n + 1) * tile)
        delta = [
            jnp.dot(
                inner[b * BLOCK : (b + 1) * BLOCK], up_ref[row, :, columns], preferred_element_type=jnp.float32
            )
            for b, row in enumerate(rows_of)
        ]
        total = jnp.concatenate(delta, axis=0) if SPAN > 1 else delta[0]
        total += total_ref[:, columns] + piece_dots(info_ref, w_ref, parts, starts, columns)
        h = x_ref[:, columns].astype(jnp.float32)
        o_ref[:, columns] = (h + scale * total).astype(jnp.bfloat16)


def join_kernel(info_ref, *refs):
    *blocks, o_ref = refs
    rows = blocks[0].shape[0]
    for i, block in enumerate(blocks):
        o_ref[i * rows : (i + 1) * rows, :] = block[...]


def home_kernel(sections, counts, info_ref, *refs):
    *blocks, o_ref = refs
    taken = 0
    for section, count in zip(range(sections), counts):
        own = blocks[taken : taken + count]
        taken += count

        @pl.when(info_ref[0] == section)
        def _():
            row = 0
            for block in own:
                span = block.shape[0]
                o_ref[row : row + span, :] = block[...]
                row += span


def reward_kernel(sections, counts, info_ref, *refs):
    *blocks, head_ref, score_ref = refs
    taken = 0
    for section, count in zip(range(sections), counts):
        own = blocks[taken : taken + count]
        taken += count

        @pl.when(info_ref[0] == section)
        def _():
            row = 0
            for block in own:
                span = block.shape[0]
                score_ref[:, row : row + span] = lax.dot_general(
                    head_ref[...], block[...], (((1,), (1,)), ((), ())), preferred_element_type=jnp.float32
                )
                row += span


def add_kernel(info_ref, *refs):
    *terms, o_ref = refs
    o_ref[...] = sum(term[...] for term in terms)


def score_kernel(info_ref, limits_ref, *refs):
    *terms, o_ref = refs
    total = sum(term[...] for term in terms)
    lane = lax.broadcasted_iota(jnp.int32, (1, BLOCK), 1)
    for b in range(total.shape[1] // BLOCK):
        columns = slice(b * BLOCK, (b + 1) * BLOCK)
        o_ref[:, columns] = jnp.where(lane < limits_ref[:, b : b + 1], total[:, columns], 0.0)


def cut(maps_ref, info_ref, place, out):
    piece = out.shape[-1]
    out[...] = maps_ref[:, :, pl.ds(pl.multiple_of((info_ref[1] ^ place) * piece, piece), piece)]


def cut_other_kernel(chips, info_ref, maps_ref, o_ref):
    for k in range(chips):
        cut(maps_ref, info_ref, 2 * k + 1, o_ref.at[k])


def cut_own_kernel(chips, info_ref, maps_ref, other_ref, *outs):
    for k, out in enumerate(outs):
        cut(maps_ref, info_ref, 2 * k, out.at[0])
        out[1] = other_ref[k]


def stack_kernel(info_ref, *refs):
    *blocks, o_ref = refs
    count, owned = blocks[0].shape[:2]
    for i, block in enumerate(blocks):
        for j in range(count):
            start = (i * count + j) * owned
            o_ref[start : start + owned] = block[j]


def shards(
    entering_hidden,
    section_weight,
    section_norm_gain,
    plugin_narrowing_factors,
    plugin_widening_factors,
    reward_head,
    adapter_of_block,
    live_block_rows,
):
    sections = lax.axis_size("section")
    section = lax.axis_index("section")
    chips = lax.axis_size("chip")
    cores = lax.axis_size("core")
    owners = chips * cores
    everyone = ("chip", "core")
    batches_here, rows, piece = entering_hidden.shape
    micro = batches_here * sections
    span = BLOCK * SPAN
    per_micro = rows // span
    owned = plugin_narrowing_factors.shape[1]
    rank = plugin_narrowing_factors.shape[3]
    chunks = micro * per_micro
    pairwise = chips == 4 and cores == 2

    chip, core = lax.axis_index("chip"), lax.axis_index("core")
    if pairwise:
        near_by, far = jnp.where(core == 0, 1, 2), jnp.where(core == 0, 2, 1)
        place = chip * cores + core
        parts = [(0, 0), (0, 1), (near_by, 0), (near_by, 1), (3, 0), (far, 1), (far, 0), (3, 1)]
        order = [(chip ^ there) * cores + (core ^ other) for there, other in parts]
    else:
        place = jnp.zeros_like(core)
        order = [i * cores + (core + k) % cores for k in range(cores) for i in range(chips)]
    info = jnp.concatenate([jnp.stack([section, place] + order), adapter_of_block.reshape(-1)])
    info = info.astype(jnp.int32)

    def over_cores(part):
        return [
            lax.ppermute(part, "core", [((c + k) % cores, c) for c in range(cores)]) for k in range(1, cores)
        ]

    def over_chips(part, steps):
        pairs = [(i * cores + c, (i ^ steps[c]) * cores + c) for i in range(chips) for c in range(cores)]
        return lax.ppermute(part, everyone, pairs)

    def spread(maps, after):
        if not pairwise:
            maps = jnp.moveaxis(maps.reshape(owned, rank, owners, piece), 2, 0)
            maps = lax.all_to_all(maps, everyone, split_axis=0, concat_axis=0, tiled=True)
            return maps.reshape(owners * owned, rank, piece), after
        size = 2 * maps.size
        out_shape = pltpu.VMEM((chips, owned, rank, piece), maps.dtype)
        kernel = functools.partial(cut_other_kernel, chips)
        other = call(kernel, out_shape, (info, maps), "cut_other", 0, 0, after=after)
        (swapped,) = over_cores(other)
        out_shape = [pltpu.VMEM((cores, owned, rank, piece), maps.dtype) for _ in range(chips)]
        kernel = functools.partial(cut_own_kernel, chips)
        mine, *blocks = call(kernel, out_shape, (info, maps, swapped), "cut_own", 0, 0)
        blocks = [over_chips(block, (k, k)) for k, block in zip(range(1, chips), blocks)]
        out_shape = pltpu.VMEM((owners * owned, rank, piece), maps.dtype)
        return call(stack_kernel, out_shape, (info, mine, *blocks), "stack", 0, 0), [mine]

    down, begun = spread(jnp.swapaxes(plugin_narrowing_factors[0], 1, 2), ())
    up, begun = spread(plugin_widening_factors[0], begun)
    weight = staged(section_weight[0], begun)

    feeds = []
    for m in range(micro):
        home, slot = divmod(m, batches_here)
        block = entering_hidden[slot]
        feeds.append(block if home == 0 else lax.ppermute(block, "section", [(home, 0)]))

    def gather_start(message):
        if not pairwise:
            parts = lax.all_to_all(message, "chip", split_axis=0, concat_axis=0, tiled=True)
            return [parts] + over_cores(parts)
        first = over_chips(message, (1, 2))
        (other,) = over_cores(message)
        second = over_chips(other, (1, 2))
        return [message, other, first, second]

    def gather_end(parts, after):
        if not pairwise:
            return [(part, chips * (1 + k)) for k, part in enumerate(parts[1:])]
        _, _, first, second = parts
        first = tie(first, after) if after else first
        third = over_chips(first, (2, 1))
        late = [first, second, third] + [over_cores(part)[0] for part in (first, second, third)]
        return list(zip(late, range(2, 8)))

    def prep(tick, sources, blocks, after):
        out_shape = (
            pltpu.VMEM((span, piece), jnp.bfloat16),
            pltpu.VMEM((1 if pairwise else chips, span, piece + SIDE), jnp.bfloat16),
        )
        kernel = functools.partial(prep_kernel, rank, owners, owned, tick, chunks, blocks)
        args = (info, *sources, section_norm_gain, down)
        return call(kernel, out_shape, args, "prep", 2 * span * piece * SIDE * bool(tick), span * piece * 8 * bool(tick), after=after)

    def own_layer(parts, after):
        width = piece * owners
        kernel = functools.partial(own_kernel, [start for _, start in parts])
        out_shape = (pltpu.VMEM((span, piece), jnp.float32), pltpu.VMEM((span, SIDE), jnp.float32))
        args = (info, *[part for part, _ in parts], weight)
        return call(kernel, out_shape, args, "own", span * width * piece // 2 * bool(after), width * piece // 2 * bool(after), after=after)

    def layer(tick, parts, x, sums, after):
        width = piece * owners
        kernel = functools.partial(layer_kernel, rank, owners, owned, tick, chunks, [start for _, start in parts])
        args = (info, *[part for part, _ in parts], weight, x, up, *sums)
        out_shape = pltpu.VMEM((span, piece), jnp.bfloat16)
        return call(kernel, out_shape, args, "layer", 2 * span * width * piece, 2 * width * piece, after=after)

    arrived, state, sums, done, home_blocks, returned = {}, {}, {}, {}, {}, {}
    ticks = chunks + LAG * (sections - 1)

    def active(tick):
        return [s for s in range(sections) if 0 <= tick - LAG * s < chunks]

    def begin(tick):
        sources, blocks = [], []
        if 0 in active(tick):
            m, b = divmod(tick, per_micro)
            sources.append(feeds[m])
            blocks.append(b)
        if active(tick) != [0]:
            sources.append(arrived.pop(tick))
            blocks.append(0)
        if tick == 0:
            after = [weight, up]
        else:
            after = [sums[tick - 1][1]]
        x, message = prep(tick, sources, blocks, after)
        state[tick] = [x, message, gather_start(message)]

    def own_chip(tick, after):
        parts = state[tick][2]
        own = [(parts[0], 0), (parts[1], 1)] if pairwise else [(parts[0], 0)]
        sums[tick] = own_layer(own, after)
        state[tick][2] = gather_end(parts, [sums[tick][1]] if after else [])

    begin(0)
    own_chip(0, [])
    for tick in range(ticks):
        after = []
        if tick + 1 < ticks:
            begin(tick + 1)
            after.append(state[tick + 1][1])
        if tick in returned:
            after.append(returned.pop(tick))
        x, _, parts = state.pop(tick)
        if pairwise:
            size = piece * piece * owners
            x = tie(x, [part for part, _ in parts[3:5]] + after, span * size, size)
        h = layer(tick, parts, x, sums[tick], after)
        if tick + 1 < ticks:
            own_chip(tick + 1, [h])
        onward = [(s, s + 1) for s in active(tick) if s + 1 < sections]
        if onward:
            arrived[tick + LAG] = lax.ppermute(h, "section", onward)
        if sections - 1 in active(tick):
            last = tick - LAG * (sections - 1)
            done[last] = h
            if last % per_micro == per_micro - 1:
                m = last // per_micro
                block = [done[m * per_micro + b] for b in range(per_micro)]
                home = m // batches_here
                if home != sections - 1:
                    if per_micro > 1:
                        out_shape = pltpu.VMEM((rows, piece), jnp.bfloat16)
                        block = [call(join_kernel, out_shape, (info, *block), "join", 0, rows * piece * 4)]
                    block = [lax.ppermute(block[0], "section", [(sections - 1, home)])]
                    returned[tick + 2] = block[0]
                home_blocks[m] = block

    hidden, scores = [], []
    for slot in range(batches_here):
        blocks = [home_blocks[home * batches_here + slot] for home in range(sections)]
        counts = [len(block) for block in blocks]
        parts = [part for block in blocks for part in block]
        out_shape = pltpu.VMEM((1, rows), jnp.float32)
        kernel = functools.partial(reward_kernel, sections, counts)
        score = call(kernel, out_shape, (info, *parts, reward_head[None]), "reward", 0, 0)
        out_shape = jax.ShapeDtypeStruct((rows, piece), jnp.bfloat16)
        kernel = functools.partial(home_kernel, sections, counts)
        hidden.append(call(kernel, out_shape, (info, *parts), "home", 2 * rows * piece, rows * piece * 4, after=[score]))
        near_by = pltpu.VMEM((1, rows), jnp.float32)
        if pairwise:
            score = call(add_kernel, near_by, (info, score, *over_cores(score)), "add", 0, rows * 4)
            terms = [score] + [over_chips(score, (k, k)) for k in (1, 2, 3)]
        else:
            terms = [lax.psum(score, everyone)]
        limits = live_block_rows[slot : slot + 1]
        out_shape = jax.ShapeDtypeStruct((1, rows), jnp.float32)
        scores.append(call(score_kernel, out_shape, (info, limits, *terms), "score", 0, rows * 4))
    if batches_here == 1:
        return (hidden[0][None], scores[0])
    return (jnp.stack(hidden), jnp.concatenate(scores, axis=0))


def solution(mesh):
    sections, owners = mesh.shape["section"], mesh.shape["mp"]
    cores = 2 if owners % 2 == 0 else 1
    fine = jax.sharding.Mesh(
        mesh.devices.reshape(sections, owners // cores, cores), ("section", "chip", "core")
    )
    mp = ("chip", "core")
    placed = (
        P("section", None, mp),
        P("section", None, mp),
        P("section", mp),
        P("section", mp, None, None),
        P("section", mp, None, None),
        P(mp),
        P(),
        P("section", None),
    )
    return jax.shard_map(
        shards,
        mesh=fine,
        in_specs=placed,
        out_specs=(P("section", None, mp), P("section", None)),
        check_vma=False,
    )
```

```python
import functools

import jax
import jax.numpy as jnp
from jax import lax
from jax.experimental import pallas as pl
from jax.experimental.pallas import tpu as pltpu
from jax.sharding import PartitionSpec as P

BLOCK = 128
SIDE = 128
LAG = 2
SPAN = 1

VMEM = pl.BlockSpec(memory_space=pltpu.VMEM)
SMEM = pl.BlockSpec(memory_space=pltpu.SMEM)


def near(x):
    return pltpu.with_memory_space_constraint(x, pltpu.VMEM)


def call(kernel, out_shape, args, name, flops, moved, limit=8, after=()):
    info, *arrays = args
    count = len(arrays)

    def body(info_ref, *refs):
        kernel(info_ref, *refs[:count], *refs[count + len(after) :])

    return pl.pallas_call(
        body,
        out_shape=out_shape,
        in_specs=[SMEM] + [VMEM] * count + [pl.BlockSpec(memory_space=pl.ANY)] * len(after),
        out_specs=jax.tree.map(lambda _: VMEM, out_shape),
        compiler_params=pltpu.CompilerParams(vmem_limit_bytes=limit << 20),
        cost_estimate=pl.CostEstimate(flops=flops, bytes_accessed=moved, transcendentals=0),
        name=name,
    )(info, *map(near, arrays), *after)


def tie(x, after, flops=0, moved=0):
    def body(*_):
        pass

    return pl.pallas_call(
        body,
        out_shape=pltpu.VMEM(x.shape, x.dtype),
        in_specs=[VMEM] + [pl.BlockSpec(memory_space=pl.ANY)] * len(after),
        out_specs=VMEM,
        input_output_aliases={0: 0},
        compiler_params=pltpu.CompilerParams(vmem_limit_bytes=1 << 20),
        cost_estimate=pl.CostEstimate(flops=flops, bytes_accessed=moved, transcendentals=0),
        name="tie",
    )(near(x), *after)


def adapter_at(info_ref, owners, owned, tick, chunks, block):
    mine = jnp.clip(tick - LAG * info_ref[0], 0, chunks - 1)
    adapter = info_ref[2 + owners + mine * SPAN + block]
    if owned == 1:
        return adapter ^ info_ref[1]
    return (lax.div(adapter, owned) ^ info_ref[1]) * owned + lax.rem(adapter, owned)


def prep_kernel(rank, owners, owned, tick, chunks, block, info_ref, *refs):
    *sources, gain_ref, down_ref, x_ref, m_ref = refs
    copies = m_ref.shape[0]
    rows, piece = x_ref.shape
    picked = [source[b * rows : (b + 1) * rows, :].astype(jnp.float32) for source, b in zip(sources, block)]
    x = jnp.where(info_ref[0] == 0, *picked) if len(picked) == 2 else picked[0]
    x_ref[...] = x.astype(jnp.bfloat16)
    scaled = (x * gain_ref[...].astype(jnp.float32)).astype(jnp.bfloat16)
    squares = jnp.sum(x * x, axis=1, keepdims=True)
    high = squares.astype(jnp.bfloat16).astype(jnp.float32)
    low = squares - high
    lane = lax.broadcasted_iota(jnp.int32, (rows, SIDE), 1)
    inner = []
    for b in range(SPAN):
        product = lax.dot_general(
            scaled[b * BLOCK : (b + 1) * BLOCK],
            down_ref[adapter_at(info_ref, owners, owned, tick, chunks, b)],
            (((1,), (1,)), ((), ())),
            preferred_element_type=jnp.float32,
        )
        inner.append(jnp.concatenate([product, jnp.zeros((BLOCK, SIDE - rank), jnp.float32)], axis=1))
    inner = jnp.concatenate(inner, axis=0) if SPAN > 1 else inner[0]
    side = jnp.where(lane == rank, high, jnp.where(lane == rank + 1, low, inner)).astype(jnp.bfloat16)
    for copy in range(copies):
        m_ref[copy, :, :piece] = scaled
        m_ref[copy, :, piece:] = side


def stage_kernel(w_ref, *refs):
    *_, o_ref, sem = refs
    copy = pltpu.make_async_copy(w_ref, o_ref, sem)
    copy.start()
    copy.wait()


def staged(weight, after):
    return pl.pallas_call(
        stage_kernel,
        out_shape=pltpu.VMEM(weight.shape, weight.dtype),
        in_specs=[pl.BlockSpec(memory_space=pl.ANY)] * (1 + len(after)),
        out_specs=VMEM,
        scratch_shapes=[pltpu.SemaphoreType.DMA],
        compiler_params=pltpu.CompilerParams(vmem_limit_bytes=4 << 20),
        cost_estimate=pl.CostEstimate(flops=0, bytes_accessed=0, transcendentals=0),
        name="stage",
    )(pltpu.with_memory_space_constraint(weight, pltpu.HBM), *after)


def piece_dots(info_ref, w_ref, parts, starts, columns):
    total = None
    for part, start in zip(parts, starts):
        piece = w_ref.shape[1]
        for k in range(part.shape[0]):
            depth = pl.ds(pl.multiple_of(info_ref[2 + start + k] * piece, piece), piece)
            term = jnp.dot(part[k, :, :piece], w_ref[depth, columns], preferred_element_type=jnp.float32)
            total = term if total is None else total + term
    return total


def side_sum(parts, piece):
    return sum(part[k, :, piece:].astype(jnp.float32) for part in parts for k in range(part.shape[0]))


def own_kernel(starts, info_ref, *refs):
    *parts, w_ref, total_ref, side_ref = refs
    piece = w_ref.shape[1]
    side_ref[...] = side_sum(parts, piece)
    tile = min(piece, 256)
    for n in range(piece // tile):
        columns = slice(n * tile, (n + 1) * tile)
        total_ref[:, columns] = piece_dots(info_ref, w_ref, parts, starts, columns)


def layer_kernel(rank, owners, owned, tick, chunks, starts, info_ref, *refs):
    *parts, w_ref, x_ref, up_ref, total_ref, side_ref, o_ref = refs
    piece = x_ref.shape[1]
    width = w_ref.shape[0]
    side = side_ref[...] + side_sum(parts, piece)
    squares = side[:, rank : rank + 1] + side[:, rank + 1 : rank + 2]
    scale = lax.rsqrt(squares / width + 1e-05)
    inner = (2.0 * side[:, :rank]).astype(jnp.bfloat16)
    rows_of = [adapter_at(info_ref, owners, owned, tick, chunks, b) for b in range(SPAN)]
    tile = min(piece, 256)
    for n in range(piece // tile):
        columns = slice(n * tile, (n + 1) * tile)
        delta = [
            jnp.dot(
                inner[b * BLOCK : (b + 1) * BLOCK], up_ref[row, :, columns], preferred_element_type=jnp.float32
            )
            for b, row in enumerate(rows_of)
        ]
        total = jnp.concatenate(delta, axis=0) if SPAN > 1 else delta[0]
        total += total_ref[:, columns] + piece_dots(info_ref, w_ref, parts, starts, columns)
        h = x_ref[:, columns].astype(jnp.float32)
        o_ref[:, columns] = (h + scale * total).astype(jnp.bfloat16)


def home_kernel(sections, counts, info_ref, *refs):
    *blocks, o_ref = refs
    taken = 0
    for section, count in zip(range(sections), counts):
        own = blocks[taken : taken + count]
        taken += count

        @pl.when(info_ref[0] == section)
        def _():
            row = 0
            for block in own:
                span = block.shape[0]
                o_ref[row : row + span, :] = block[...]
                row += span


def reward_kernel(sections, counts, info_ref, *refs):
    *blocks, head_ref, score_ref = refs
    taken = 0
    for section, count in zip(range(sections), counts):
        own = blocks[taken : taken + count]
        taken += count

        @pl.when(info_ref[0] == section)
        def _():
            row = 0
            for block in own:
                span = block.shape[0]
                score_ref[:, row : row + span] = lax.dot_general(
                    head_ref[...], block[...], (((1,), (1,)), ((), ())), preferred_element_type=jnp.float32
                )
                row += span


def add_kernel(info_ref, *refs):
    *terms, o_ref = refs
    o_ref[...] = sum(term[...] for term in terms)


def score_kernel(info_ref, limits_ref, *refs):
    *terms, o_ref = refs
    total = sum(term[...] for term in terms)
    lane = lax.broadcasted_iota(jnp.int32, (1, BLOCK), 1)
    for b in range(total.shape[1] // BLOCK):
        columns = slice(b * BLOCK, (b + 1) * BLOCK)
        o_ref[:, columns] = jnp.where(lane < limits_ref[:, b : b + 1], total[:, columns], 0.0)


def cut(maps_ref, info_ref, place, out):
    piece = out.shape[-1]
    out[...] = maps_ref[:, :, pl.ds(pl.multiple_of((info_ref[1] ^ place) * piece, piece), piece)]


def cut_other_kernel(chips, info_ref, maps_ref, o_ref):
    for k in range(chips):
        cut(maps_ref, info_ref, 2 * k + 1, o_ref.at[k])


def cut_own_kernel(chips, info_ref, maps_ref, other_ref, *outs):
    for k, out in enumerate(outs):
        cut(maps_ref, info_ref, 2 * k, out.at[0])
        out[1] = other_ref[k]


def stack_kernel(info_ref, *refs):
    *blocks, o_ref = refs
    count, owned = blocks[0].shape[:2]
    for i, block in enumerate(blocks):
        for j in range(count):
            start = (i * count + j) * owned
            o_ref[start : start + owned] = block[j]


def shards(
    entering_hidden,
    section_weight,
    section_norm_gain,
    plugin_narrowing_factors,
    plugin_widening_factors,
    reward_head,
    adapter_of_block,
    live_block_rows,
):
    sections = lax.axis_size("section")
    section = lax.axis_index("section")
    chips = lax.axis_size("chip")
    cores = lax.axis_size("core")
    owners = chips * cores
    everyone = ("chip", "core")
    batches_here, rows, piece = entering_hidden.shape
    micro = batches_here * sections
    span = BLOCK * SPAN
    per_micro = rows // span
    owned = plugin_narrowing_factors.shape[1]
    rank = plugin_narrowing_factors.shape[3]
    chunks = micro * per_micro
    pairwise = chips == 4 and cores == 2

    chip, core = lax.axis_index("chip"), lax.axis_index("core")
    if pairwise:
        near_by, far = jnp.where(core == 0, 1, 2), jnp.where(core == 0, 2, 1)
        place = chip * cores + core
        parts = [(0, 0), (0, 1), (near_by, 0), (near_by, 1), (3, 0), (far, 1), (far, 0), (3, 1)]
        order = [(chip ^ there) * cores + (core ^ other) for there, other in parts]
    else:
        place = jnp.zeros_like(core)
        order = [i * cores + (core + k) % cores for k in range(cores) for i in range(chips)]
    info = jnp.concatenate([jnp.stack([section, place] + order), adapter_of_block.reshape(-1)])
    info = info.astype(jnp.int32)

    def over_cores(part):
        return [
            lax.ppermute(part, "core", [((c + k) % cores, c) for c in range(cores)]) for k in range(1, cores)
        ]

    def over_chips(part, steps):
        pairs = [(i * cores + c, (i ^ steps[c]) * cores + c) for i in range(chips) for c in range(cores)]
        return lax.ppermute(part, everyone, pairs)

    def spread(maps, after):
        if not pairwise:
            maps = jnp.moveaxis(maps.reshape(owned, rank, owners, piece), 2, 0)
            maps = lax.all_to_all(maps, everyone, split_axis=0, concat_axis=0, tiled=True)
            table = maps.reshape(owners * owned, rank, piece)
            return lambda after: table, after
        size = 2 * maps.size
        out_shape = pltpu.VMEM((chips, owned, rank, piece), maps.dtype)
        kernel = functools.partial(cut_other_kernel, chips)
        other = call(kernel, out_shape, (info, maps), "cut_other", 0, 0, after=after)
        (swapped,) = over_cores(other)
        out_shape = [pltpu.VMEM((cores, owned, rank, piece), maps.dtype) for _ in range(chips)]
        kernel = functools.partial(cut_own_kernel, chips)
        mine, *blocks = call(kernel, out_shape, (info, maps, swapped), "cut_own", 0, 0)
        blocks = [over_chips(block, (k, k)) for k, block in zip(range(1, chips), blocks)]
        out_shape = pltpu.VMEM((owners * owned, rank, piece), maps.dtype)
        return functools.partial(call, stack_kernel, out_shape, (info, mine, *blocks), "stack", 0, 0), [mine]

    down, begun = spread(jnp.swapaxes(plugin_narrowing_factors[0], 1, 2), ())
    up, begun = spread(plugin_widening_factors[0], begun)
    weight = staged(section_weight[0], begun)
    down, up = down(after=[weight]), up(after=[weight])

    feeds = []
    for m in range(micro):
        home, slot = divmod(m, batches_here)
        block = entering_hidden[slot]
        feeds.append(block if home == 0 else lax.ppermute(block, "section", [(home, 0)]))

    def gather_start(message):
        if not pairwise:
            parts = lax.all_to_all(message, "chip", split_axis=0, concat_axis=0, tiled=True)
            return [parts] + over_cores(parts)
        first = over_chips(message, (1, 2))
        (other,) = over_cores(message)
        second = over_chips(other, (1, 2))
        return [message, other, first, second]

    def gather_end(parts, after):
        if not pairwise:
            return [(part, chips * (1 + k)) for k, part in enumerate(parts[1:])]
        _, _, first, second = parts
        first = tie(first, after) if after else first
        third = over_chips(first, (2, 1))
        late = [first, second, third] + [over_cores(part)[0] for part in (first, second, third)]
        return list(zip(late, range(2, 8)))

    def prep(tick, sources, blocks, after):
        out_shape = (
            pltpu.VMEM((span, piece), jnp.bfloat16),
            pltpu.VMEM((1 if pairwise else chips, span, piece + SIDE), jnp.bfloat16),
        )
        kernel = functools.partial(prep_kernel, rank, owners, owned, tick, chunks, blocks)
        args = (info, *sources, section_norm_gain, down)
        return call(kernel, out_shape, args, "prep", 2 * span * piece * SIDE * bool(tick), span * piece * 8 * bool(tick), after=after)

    def own_layer(parts, after):
        width = piece * owners
        kernel = functools.partial(own_kernel, [start for _, start in parts])
        out_shape = (pltpu.VMEM((span, piece), jnp.float32), pltpu.VMEM((span, SIDE), jnp.float32))
        args = (info, *[part for part, _ in parts], weight)
        return call(kernel, out_shape, args, "own", span * width * piece // 2 * bool(after), width * piece // 2 * bool(after), after=after)

    def layer(tick, parts, x, sums, after):
        width = piece * owners
        kernel = functools.partial(layer_kernel, rank, owners, owned, tick, chunks, [start for _, start in parts])
        args = (info, *[part for part, _ in parts], weight, x, up, *sums)
        out_shape = pltpu.VMEM((span, piece), jnp.bfloat16)
        return call(kernel, out_shape, args, "layer", 2 * span * width * piece, 2 * width * piece, after=after)

    arrived, state, sums, home_blocks, returned = {}, {}, {}, {}, {}
    ticks = chunks + LAG * (sections - 1)

    def active(tick):
        return [s for s in range(sections) if 0 <= tick - LAG * s < chunks]

    def begin(tick):
        sources, blocks = [], []
        if 0 in active(tick):
            m, b = divmod(tick, per_micro)
            sources.append(feeds[m])
            blocks.append(b)
        if active(tick) != [0]:
            sources.append(arrived.pop(tick))
            blocks.append(0)
        if tick == 0:
            after = [weight, up]
        else:
            after = [sums[tick - 1][1]]
        if tick in returned:
            after.append(returned.pop(tick))
        x, message = prep(tick, sources, blocks, after)
        state[tick] = [x, message, gather_start(message)]

    def own_chip(tick, after):
        parts = state[tick][2]
        own = [(parts[0], 0), (parts[1], 1)] if pairwise else [(parts[0], 0)]
        sums[tick] = own_layer(own, after)
        state[tick][2] = gather_end(parts, [sums[tick][1]] if after else [])

    begin(0)
    own_chip(0, [])
    for tick in range(ticks):
        after = []
        if tick + 1 < ticks:
            begin(tick + 1)
            after.append(state[tick + 1][1])
        x, _, parts = state.pop(tick)
        if pairwise:
            size = piece * piece * owners
            x = tie(x, [part for part, _ in parts[3:5]] + after, span * size, size)
        h = layer(tick, parts, x, sums[tick], after)
        if tick + 1 < ticks:
            own_chip(tick + 1, [h])
        onward = [(s, s + 1) for s in active(tick) if s + 1 < sections]
        if onward:
            arrived[tick + LAG] = lax.ppermute(h, "section", onward)
        if sections - 1 in active(tick):
            last = tick - LAG * (sections - 1)
            m = last // per_micro
            home = m // batches_here
            if home != sections - 1:
                h = returned[tick + 2] = lax.ppermute(h, "section", [(sections - 1, home)])
            home_blocks.setdefault(m, []).append(h)

    hidden, scores = [], []
    for slot in range(batches_here):
        blocks = [home_blocks[home * batches_here + slot] for home in range(sections)]
        counts = [len(block) for block in blocks]
        parts = [part for block in blocks for part in block]
        out_shape = pltpu.VMEM((1, rows), jnp.float32)
        kernel = functools.partial(reward_kernel, sections, counts)
        score = call(kernel, out_shape, (info, *parts, reward_head[None]), "reward", 0, 0)
        out_shape = jax.ShapeDtypeStruct((rows, piece), jnp.bfloat16)
        kernel = functools.partial(home_kernel, sections, counts)
        hidden.append(call(kernel, out_shape, (info, *parts), "home", 2 * rows * piece, rows * piece * 4, after=[score]))
        near_by = pltpu.VMEM((1, rows), jnp.float32)
        if pairwise:
            score = call(add_kernel, near_by, (info, score, *over_cores(score)), "add", 0, rows * 4)
            terms = [score] + [over_chips(score, (k, k)) for k in (1, 2, 3)]
        else:
            terms = [lax.psum(score, everyone)]
        limits = live_block_rows[slot : slot + 1]
        out_shape = jax.ShapeDtypeStruct((1, rows), jnp.float32)
        scores.append(call(score_kernel, out_shape, (info, limits, *terms), "score", 0, rows * 4))
    if batches_here == 1:
        return (hidden[0][None], scores[0])
    return (jnp.stack(hidden), jnp.concatenate(scores, axis=0))


def solution(mesh):
    sections, owners = mesh.shape["section"], mesh.shape["mp"]
    cores = 2 if owners % 2 == 0 else 1
    fine = jax.sharding.Mesh(
        mesh.devices.reshape(sections, owners // cores, cores), ("section", "chip", "core")
    )
    mp = ("chip", "core")
    placed = (
        P("section", None, mp),
        P("section", None, mp),
        P("section", mp),
        P("section", mp, None, None),
        P("section", mp, None, None),
        P(mp),
        P(),
        P("section", None),
    )
    return jax.shard_map(
        shards,
        mesh=fine,
        in_specs=placed,
        out_specs=(P("section", None, mp), P("section", None)),
        check_vma=False,
    )
```

```python
import functools

import jax
import jax.numpy as jnp
from jax import lax
from jax.experimental import pallas as pl
from jax.experimental.pallas import tpu as pltpu
from jax.sharding import PartitionSpec as P

BLOCK = 128
SIDE = 128
LAG = 2
SPAN = 1

VMEM = pl.BlockSpec(memory_space=pltpu.VMEM)
SMEM = pl.BlockSpec(memory_space=pltpu.SMEM)


def near(x):
    return pltpu.with_memory_space_constraint(x, pltpu.VMEM)


def call(kernel, out_shape, args, name, flops, moved, limit=8, after=()):
    info, *arrays = args
    count = len(arrays)

    def body(info_ref, *refs):
        kernel(info_ref, *refs[:count], *refs[count + len(after) :])

    return pl.pallas_call(
        body,
        out_shape=out_shape,
        in_specs=[SMEM] + [VMEM] * count + [pl.BlockSpec(memory_space=pl.ANY)] * len(after),
        out_specs=jax.tree.map(lambda _: VMEM, out_shape),
        compiler_params=pltpu.CompilerParams(vmem_limit_bytes=limit << 20),
        cost_estimate=pl.CostEstimate(flops=flops, bytes_accessed=moved, transcendentals=0),
        name=name,
    )(info, *map(near, arrays), *after)


def tie(x, after, flops=0, moved=0):
    def body(*_):
        pass

    return pl.pallas_call(
        body,
        out_shape=pltpu.VMEM(x.shape, x.dtype),
        in_specs=[VMEM] + [pl.BlockSpec(memory_space=pl.ANY)] * len(after),
        out_specs=VMEM,
        input_output_aliases={0: 0},
        compiler_params=pltpu.CompilerParams(vmem_limit_bytes=1 << 20),
        cost_estimate=pl.CostEstimate(flops=flops, bytes_accessed=moved, transcendentals=0),
        name="tie",
    )(near(x), *after)


def adapter_at(info_ref, owners, owned, tick, chunks, block):
    mine = jnp.clip(tick - LAG * info_ref[0], 0, chunks - 1)
    adapter = info_ref[2 + owners + mine * SPAN + block]
    if owned == 1:
        return adapter ^ info_ref[1]
    return (lax.div(adapter, owned) ^ info_ref[1]) * owned + lax.rem(adapter, owned)


def prep_kernel(rank, owners, owned, tick, chunks, block, info_ref, *refs):
    *sources, gain_ref, down_ref, x_ref, m_ref = refs
    copies = m_ref.shape[0]
    rows, piece = x_ref.shape
    picked = [source[b * rows : (b + 1) * rows, :].astype(jnp.float32) for source, b in zip(sources, block)]
    x = jnp.where(info_ref[0] == 0, *picked) if len(picked) == 2 else picked[0]
    x_ref[...] = x.astype(jnp.bfloat16)
    scaled = (x * gain_ref[...].astype(jnp.float32)).astype(jnp.bfloat16)
    squares = jnp.sum(x * x, axis=1, keepdims=True)
    high = squares.astype(jnp.bfloat16).astype(jnp.float32)
    low = squares - high
    lane = lax.broadcasted_iota(jnp.int32, (rows, SIDE), 1)
    inner = []
    for b in range(SPAN):
        product = lax.dot_general(
            scaled[b * BLOCK : (b + 1) * BLOCK],
            down_ref[adapter_at(info_ref, owners, owned, tick, chunks, b)],
            (((1,), (1,)), ((), ())),
            preferred_element_type=jnp.float32,
        )
        inner.append(jnp.concatenate([product, jnp.zeros((BLOCK, SIDE - rank), jnp.float32)], axis=1))
    inner = jnp.concatenate(inner, axis=0) if SPAN > 1 else inner[0]
    side = jnp.where(lane == rank, high, jnp.where(lane == rank + 1, low, inner)).astype(jnp.bfloat16)
    for copy in range(copies):
        m_ref[copy, :, :piece] = scaled
        m_ref[copy, :, piece:] = side


def stage_kernel(w_ref, *refs):
    *_, o_ref, sem = refs
    copy = pltpu.make_async_copy(w_ref, o_ref, sem)
    copy.start()
    copy.wait()


def staged(weight, after):
    return pl.pallas_call(
        stage_kernel,
        out_shape=pltpu.VMEM(weight.shape, weight.dtype),
        in_specs=[pl.BlockSpec(memory_space=pl.ANY)] * (1 + len(after)),
        out_specs=VMEM,
        scratch_shapes=[pltpu.SemaphoreType.DMA],
        compiler_params=pltpu.CompilerParams(vmem_limit_bytes=4 << 20),
        cost_estimate=pl.CostEstimate(flops=0, bytes_accessed=0, transcendentals=0),
        name="stage",
    )(pltpu.with_memory_space_constraint(weight, pltpu.HBM), *after)


def piece_dots(info_ref, w_ref, parts, starts, columns):
    total = None
    for part, start in zip(parts, starts):
        piece = w_ref.shape[1]
        for k in range(part.shape[0]):
            depth = pl.ds(pl.multiple_of(info_ref[2 + start + k] * piece, piece), piece)
            term = jnp.dot(part[k, :, :piece], w_ref[depth, columns], preferred_element_type=jnp.float32)
            total = term if total is None else total + term
    return total


def side_sum(parts, piece):
    return sum(part[k, :, piece:].astype(jnp.float32) for part in parts for k in range(part.shape[0]))


def own_kernel(starts, info_ref, *refs):
    *parts, w_ref, total_ref, side_ref = refs
    piece = w_ref.shape[1]
    side_ref[...] = side_sum(parts, piece)
    tile = min(piece, 256)
    for n in range(piece // tile):
        columns = slice(n * tile, (n + 1) * tile)
        total_ref[:, columns] = piece_dots(info_ref, w_ref, parts, starts, columns)


def layer_kernel(rank, owners, owned, tick, chunks, starts, info_ref, *refs):
    *parts, w_ref, x_ref, up_ref, total_ref, side_ref, o_ref = refs
    piece = x_ref.shape[1]
    width = w_ref.shape[0]
    side = side_ref[...] + side_sum(parts, piece)
    squares = side[:, rank : rank + 1] + side[:, rank + 1 : rank + 2]
    scale = lax.rsqrt(squares / width + 1e-05)
    inner = (2.0 * side[:, :rank]).astype(jnp.bfloat16)
    rows_of = [adapter_at(info_ref, owners, owned, tick, chunks, b) for b in range(SPAN)]
    tile = min(piece, 256)
    for n in range(piece // tile):
        columns = slice(n * tile, (n + 1) * tile)
        delta = [
            jnp.dot(
                inner[b * BLOCK : (b + 1) * BLOCK], up_ref[row, :, columns], preferred_element_type=jnp.float32
            )
            for b, row in enumerate(rows_of)
        ]
        total = jnp.concatenate(delta, axis=0) if SPAN > 1 else delta[0]
        total += total_ref[:, columns] + piece_dots(info_ref, w_ref, parts, starts, columns)
        h = x_ref[:, columns].astype(jnp.float32)
        o_ref[:, columns] = (h + scale * total).astype(jnp.bfloat16)


def home_kernel(sections, counts, info_ref, *refs):
    *blocks, o_ref = refs
    taken = 0
    for section, count in zip(range(sections), counts):
        own = blocks[taken : taken + count]
        taken += count

        @pl.when(info_ref[0] == section)
        def _():
            row = 0
            for block in own:
                span = block.shape[0]
                o_ref[row : row + span, :] = block[...]
                row += span


def reward_kernel(sections, counts, info_ref, *refs):
    *blocks, head_ref, score_ref = refs
    taken = 0
    for section, count in zip(range(sections), counts):
        own = blocks[taken : taken + count]
        taken += count

        @pl.when(info_ref[0] == section)
        def _():
            row = 0
            for block in own:
                span = block.shape[0]
                score_ref[:, row : row + span] = lax.dot_general(
                    head_ref[...], block[...], (((1,), (1,)), ((), ())), preferred_element_type=jnp.float32
                )
                row += span


def add_kernel(info_ref, *refs):
    *terms, o_ref = refs
    o_ref[...] = sum(term[...] for term in terms)


def score_kernel(info_ref, limits_ref, *refs):
    *terms, o_ref = refs
    total = sum(term[...] for term in terms)
    lane = lax.broadcasted_iota(jnp.int32, (1, BLOCK), 1)
    for b in range(total.shape[1] // BLOCK):
        columns = slice(b * BLOCK, (b + 1) * BLOCK)
        o_ref[:, columns] = jnp.where(lane < limits_ref[:, b : b + 1], total[:, columns], 0.0)


def cut(maps_ref, info_ref, place, out):
    piece = out.shape[-1]
    out[...] = maps_ref[:, :, pl.ds(pl.multiple_of((info_ref[1] ^ place) * piece, piece), piece)]


def cut_other_kernel(chips, info_ref, maps_ref, o_ref):
    for k in range(chips):
        cut(maps_ref, info_ref, 2 * k + 1, o_ref.at[k])


def cut_own_kernel(chips, info_ref, maps_ref, other_ref, *outs):
    for k, out in enumerate(outs):
        cut(maps_ref, info_ref, 2 * k, out.at[0])
        out[1] = other_ref[k]


def stack_kernel(info_ref, *refs):
    *blocks, o_ref = refs
    count, owned = blocks[0].shape[:2]
    for i, block in enumerate(blocks):
        for j in range(count):
            start = (i * count + j) * owned
            o_ref[start : start + owned] = block[j]


def shards(
    entering_hidden,
    section_weight,
    section_norm_gain,
    plugin_narrowing_factors,
    plugin_widening_factors,
    reward_head,
    adapter_of_block,
    live_block_rows,
):
    sections = lax.axis_size("section")
    section = lax.axis_index("section")
    chips = lax.axis_size("chip")
    cores = lax.axis_size("core")
    owners = chips * cores
    everyone = ("chip", "core")
    batches_here, rows, piece = entering_hidden.shape
    micro = batches_here * sections
    span = BLOCK * SPAN
    per_micro = rows // span
    owned = plugin_narrowing_factors.shape[1]
    rank = plugin_narrowing_factors.shape[3]
    chunks = micro * per_micro
    pairwise = chips == 4 and cores == 2

    chip, core = lax.axis_index("chip"), lax.axis_index("core")
    if pairwise:
        near_by, far = jnp.where(core == 0, 1, 2), jnp.where(core == 0, 2, 1)
        place = chip * cores + core
        parts = [(0, 0), (0, 1), (near_by, 0), (near_by, 1), (3, 0), (far, 1), (far, 0), (3, 1)]
        order = [(chip ^ there) * cores + (core ^ other) for there, other in parts]
    else:
        place = jnp.zeros_like(core)
        order = [i * cores + (core + k) % cores for k in range(cores) for i in range(chips)]
    info = jnp.concatenate([jnp.stack([section, place] + order), adapter_of_block.reshape(-1)])
    info = info.astype(jnp.int32)

    def over_cores(part):
        return [
            lax.ppermute(part, "core", [((c + k) % cores, c) for c in range(cores)]) for k in range(1, cores)
        ]

    def over_chips(part, steps):
        pairs = [(i * cores + c, (i ^ steps[c]) * cores + c) for i in range(chips) for c in range(cores)]
        return lax.ppermute(part, everyone, pairs)

    def spread(maps, after):
        if not pairwise:
            maps = jnp.moveaxis(maps.reshape(owned, rank, owners, piece), 2, 0)
            maps = lax.all_to_all(maps, everyone, split_axis=0, concat_axis=0, tiled=True)
            table = maps.reshape(owners * owned, rank, piece)
            return lambda after: table, after
        size = 2 * maps.size
        out_shape = pltpu.VMEM((chips, owned, rank, piece), maps.dtype)
        kernel = functools.partial(cut_other_kernel, chips)
        other = call(kernel, out_shape, (info, maps), "cut_other", 0, 0, after=after)
        (swapped,) = over_cores(other)
        out_shape = [pltpu.VMEM((cores, owned, rank, piece), maps.dtype) for _ in range(chips)]
        kernel = functools.partial(cut_own_kernel, chips)
        mine, *blocks = call(kernel, out_shape, (info, maps, swapped), "cut_own", 0, 0)
        blocks = [over_chips(block, (k, k)) for k, block in zip(range(1, chips), blocks)]
        out_shape = pltpu.VMEM((owners * owned, rank, piece), maps.dtype)
        return functools.partial(call, stack_kernel, out_shape, (info, mine, *blocks), "stack", 0, 0), [mine]

    down, begun = spread(jnp.swapaxes(plugin_narrowing_factors[0], 1, 2), ())
    up, begun = spread(plugin_widening_factors[0], begun)
    weight = staged(section_weight[0], begun)
    down, up = down(after=[weight]), up(after=[weight])

    feeds = []
    for m in range(micro):
        home, slot = divmod(m, batches_here)
        block = entering_hidden[slot]
        feeds.append(block if home == 0 else lax.ppermute(block, "section", [(home, 0)]))

    def gather_start(message):
        if not pairwise:
            parts = lax.all_to_all(message, "chip", split_axis=0, concat_axis=0, tiled=True)
            return [parts] + over_cores(parts)
        first = over_chips(message, (1, 2))
        (other,) = over_cores(message)
        second = over_chips(other, (1, 2))
        return [message, other, first, second]

    def gather_end(parts, after):
        if not pairwise:
            return [(part, chips * (1 + k)) for k, part in enumerate(parts[1:])]
        _, _, first, second = parts
        first = tie(first, after) if after else first
        third = over_chips(first, (2, 1))
        late = [first, second, third] + [over_cores(part)[0] for part in (first, second, third)]
        return list(zip(late, range(2, 8)))

    def prep(tick, sources, blocks, after):
        out_shape = (
            pltpu.VMEM((span, piece), jnp.bfloat16),
            pltpu.VMEM((1 if pairwise else chips, span, piece + SIDE), jnp.bfloat16),
        )
        kernel = functools.partial(prep_kernel, rank, owners, owned, tick, chunks, blocks)
        args = (info, *sources, section_norm_gain, down)
        return call(kernel, out_shape, args, "prep", 2 * span * piece * SIDE * bool(tick), span * piece * 8 * bool(tick), after=after)

    def own_layer(parts, after):
        width = piece * owners
        kernel = functools.partial(own_kernel, [start for _, start in parts])
        out_shape = (pltpu.VMEM((span, piece), jnp.float32), pltpu.VMEM((span, SIDE), jnp.float32))
        args = (info, *[part for part, _ in parts], weight)
        return call(kernel, out_shape, args, "own", span * width * piece // 2 * bool(after), width * piece // 2 * bool(after), after=after)

    def layer(tick, parts, x, sums, after):
        width = piece * owners
        kernel = functools.partial(layer_kernel, rank, owners, owned, tick, chunks, [start for _, start in parts])
        args = (info, *[part for part, _ in parts], weight, x, up, *sums)
        out_shape = pltpu.VMEM((span, piece), jnp.bfloat16)
        return call(kernel, out_shape, args, "layer", 2 * span * width * piece, 2 * width * piece, after=after)

    arrived, state, sums, home_blocks, returned = {}, {}, {}, {}, {}
    ticks = chunks + LAG * (sections - 1)

    def active(tick):
        return [s for s in range(sections) if 0 <= tick - LAG * s < chunks]

    def begin(tick):
        sources, blocks = [], []
        if 0 in active(tick):
            m, b = divmod(tick, per_micro)
            sources.append(feeds[m])
            blocks.append(b)
        if active(tick) != [0]:
            sources.append(arrived.pop(tick))
            if tick in returned:
                sources[-1] = tie(sources[-1], [])
            blocks.append(0)
        if tick == 0:
            after = [weight]
        else:
            after = [sums[tick - 1][1]]
        if tick in returned:
            after.append(returned.pop(tick))
        x, message = prep(tick, sources, blocks, after)
        state[tick] = [x, message, gather_start(message)]

    def own_chip(tick, after):
        parts = state[tick][2]
        own = [(parts[0], 0), (parts[1], 1)] if pairwise else [(parts[0], 0)]
        sums[tick] = own_layer(own, after)
        state[tick][2] = gather_end(parts, [sums[tick][1]] if after else [])

    begin(0)
    own_chip(0, [up])
    for tick in range(ticks):
        after = []
        if tick + 1 < ticks:
            begin(tick + 1)
            after.append(state[tick + 1][1])
        x, _, parts = state.pop(tick)
        if pairwise:
            size = piece * piece * owners
            x = tie(x, [part for part, _ in parts[3:5]] + after, span * size, size)
        h = layer(tick, parts, x, sums[tick], after)
        if tick + 1 < ticks:
            own_chip(tick + 1, [h])
        onward = [(s, s + 1) for s in active(tick) if s + 1 < sections]
        if onward:
            arrived[tick + LAG] = lax.ppermute(h, "section", onward)
        if sections - 1 in active(tick):
            last = tick - LAG * (sections - 1)
            m = last // per_micro
            home = m // batches_here
            if home != sections - 1:
                h = returned[tick + 2] = lax.ppermute(h, "section", [(sections - 1, home)])
            home_blocks.setdefault(m, []).append(h)

    hidden, scores = [], []
    for slot in range(batches_here):
        blocks = [home_blocks[home * batches_here + slot] for home in range(sections)]
        counts = [len(block) for block in blocks]
        parts = [part for block in blocks for part in block]
        out_shape = pltpu.VMEM((1, rows), jnp.float32)
        kernel = functools.partial(reward_kernel, sections, counts)
        score = call(kernel, out_shape, (info, *parts, reward_head[None]), "reward", 0, 0)
        out_shape = jax.ShapeDtypeStruct((rows, piece), jnp.bfloat16)
        kernel = functools.partial(home_kernel, sections, counts)
        hidden.append(call(kernel, out_shape, (info, *parts), "home", 2 * rows * piece, rows * piece * 4, after=[score]))
        near_by = pltpu.VMEM((1, rows), jnp.float32)
        if pairwise:
            score = call(add_kernel, near_by, (info, score, *over_cores(score)), "add", 0, rows * 4)
            terms = [score] + [over_chips(score, (k, k)) for k in (1, 2, 3)]
        else:
            terms = [lax.psum(score, everyone)]
        limits = live_block_rows[slot : slot + 1]
        out_shape = jax.ShapeDtypeStruct((1, rows), jnp.float32)
        scores.append(call(score_kernel, out_shape, (info, limits, *terms), "score", 0, rows * 4))
    if batches_here == 1:
        return (hidden[0][None], scores[0])
    return (jnp.stack(hidden), jnp.concatenate(scores, axis=0))


def solution(mesh):
    sections, owners = mesh.shape["section"], mesh.shape["mp"]
    cores = 2 if owners % 2 == 0 else 1
    fine = jax.sharding.Mesh(
        mesh.devices.reshape(sections, owners // cores, cores), ("section", "chip", "core")
    )
    mp = ("chip", "core")
    placed = (
        P("section", None, mp),
        P("section", None, mp),
        P("section", mp),
        P("section", mp, None, None),
        P("section", mp, None, None),
        P(mp),
        P(),
        P("section", None),
    )
    return jax.shard_map(
        shards,
        mesh=fine,
        in_specs=placed,
        out_specs=(P("section", None, mp), P("section", None)),
        check_vma=False,
    )
```

```python
import functools

import jax
import jax.numpy as jnp
from jax import lax
from jax.experimental import pallas as pl
from jax.experimental.pallas import tpu as pltpu
from jax.sharding import PartitionSpec as P

BLOCK = 128
SIDE = 128
LAG = 2
SPAN = 1

VMEM = pl.BlockSpec(memory_space=pltpu.VMEM)
SMEM = pl.BlockSpec(memory_space=pltpu.SMEM)


def near(x):
    return pltpu.with_memory_space_constraint(x, pltpu.VMEM)


def call(kernel, out_shape, args, name, flops, moved, limit=8, after=()):
    info, *arrays = args
    count = len(arrays)

    def body(info_ref, *refs):
        kernel(info_ref, *refs[:count], *refs[count + len(after) :])

    return pl.pallas_call(
        body,
        out_shape=out_shape,
        in_specs=[SMEM] + [VMEM] * count + [pl.BlockSpec(memory_space=pl.ANY)] * len(after),
        out_specs=jax.tree.map(lambda _: VMEM, out_shape),
        compiler_params=pltpu.CompilerParams(vmem_limit_bytes=limit << 20),
        cost_estimate=pl.CostEstimate(flops=flops, bytes_accessed=moved, transcendentals=0),
        name=name,
    )(info, *map(near, arrays), *after)


def tie(x, after, flops=0, moved=0):
    def body(*_):
        pass

    return pl.pallas_call(
        body,
        out_shape=pltpu.VMEM(x.shape, x.dtype),
        in_specs=[VMEM] + [pl.BlockSpec(memory_space=pl.ANY)] * len(after),
        out_specs=VMEM,
        input_output_aliases={0: 0},
        compiler_params=pltpu.CompilerParams(vmem_limit_bytes=1 << 20),
        cost_estimate=pl.CostEstimate(flops=flops, bytes_accessed=moved, transcendentals=0),
        name="tie",
    )(near(x), *after)


def adapter_at(info_ref, owners, owned, tick, chunks, block):
    mine = jnp.clip(tick - LAG * info_ref[0], 0, chunks - 1)
    adapter = info_ref[2 + owners + mine * SPAN + block]
    if owned == 1:
        return adapter ^ info_ref[1]
    return (lax.div(adapter, owned) ^ info_ref[1]) * owned + lax.rem(adapter, owned)


def prep_kernel(rank, owners, owned, tick, chunks, block, tabled, info_ref, *refs):
    *sources, gain_ref, x_ref, m_ref = refs
    if tabled:
        *sources, gain_ref, down_ref = sources + [gain_ref]
    copies = m_ref.shape[0]
    rows, piece = x_ref.shape
    picked = [source[b * rows : (b + 1) * rows, :].astype(jnp.float32) for source, b in zip(sources, block)]
    x = jnp.where(info_ref[0] == 0, *picked) if len(picked) == 2 else picked[0]
    x_ref[...] = x.astype(jnp.bfloat16)
    scaled = (x * gain_ref[...].astype(jnp.float32)).astype(jnp.bfloat16)
    squares = jnp.sum(x * x, axis=1, keepdims=True)
    high = squares.astype(jnp.bfloat16).astype(jnp.float32)
    low = squares - high
    lane = lax.broadcasted_iota(jnp.int32, (rows, SIDE), 1)
    inner = jnp.zeros((rows, SIDE), jnp.float32)
    if tabled:
        inner = []
        for b in range(SPAN):
            product = lax.dot_general(
                scaled[b * BLOCK : (b + 1) * BLOCK],
                down_ref[adapter_at(info_ref, owners, owned, tick, chunks, b)],
                (((1,), (1,)), ((), ())),
                preferred_element_type=jnp.float32,
            )
            inner.append(jnp.concatenate([product, jnp.zeros((BLOCK, SIDE - rank), jnp.float32)], axis=1))
        inner = jnp.concatenate(inner, axis=0) if SPAN > 1 else inner[0]
    side = jnp.where(lane == rank, high, jnp.where(lane == rank + 1, low, inner)).astype(jnp.bfloat16)
    for copy in range(copies):
        m_ref[copy, :, :piece] = scaled
        m_ref[copy, :, piece:] = side


def owner_kernel(rank, owners, owned, starts, info_ref, *refs):
    *parts, down_ref, o_ref = refs
    rows = o_ref.shape[1]
    piece = parts[0].shape[2] - SIDE
    sums = []
    for o in range(owned):
        total = None
        for part, start in zip(parts, starts):
            columns = pl.ds(pl.multiple_of(info_ref[2 + start] * piece, piece), piece)
            term = lax.dot_general(
                part[0, :, :piece], down_ref[o, :, columns], (((1,), (1,)), ((), ())), preferred_element_type=jnp.float32
            )
            total = term if total is None else total + term
        sums.append(total)
    for b in range(SPAN):
        adapter = info_ref[2 + owners + b]
        block = slice(b * BLOCK, (b + 1) * BLOCK)
        product = jnp.zeros((BLOCK, rank), jnp.float32)
        for o, total in enumerate(sums):
            product = jnp.where(adapter == info_ref[1] * owned + o, total[block], product)
        side = jnp.concatenate([product, jnp.zeros((BLOCK, SIDE - rank), jnp.float32)], axis=1)
        o_ref[0, block, :] = side.astype(jnp.bfloat16)


def stage_kernel(w_ref, *refs):
    *_, o_ref, sem = refs
    copy = pltpu.make_async_copy(w_ref, o_ref, sem)
    copy.start()
    copy.wait()


def staged(weight, after):
    return pl.pallas_call(
        stage_kernel,
        out_shape=pltpu.VMEM(weight.shape, weight.dtype),
        in_specs=[pl.BlockSpec(memory_space=pl.ANY)] * (1 + len(after)),
        out_specs=VMEM,
        scratch_shapes=[pltpu.SemaphoreType.DMA],
        compiler_params=pltpu.CompilerParams(vmem_limit_bytes=4 << 20),
        cost_estimate=pl.CostEstimate(flops=0, bytes_accessed=2 * weight.size, transcendentals=0),
        name="stage",
    )(pltpu.with_memory_space_constraint(weight, pltpu.HBM), *after)


def piece_dots(info_ref, w_ref, parts, starts, columns):
    total = None
    for part, start in zip(parts, starts):
        piece = w_ref.shape[1]
        for k in range(part.shape[0]):
            depth = pl.ds(pl.multiple_of(info_ref[2 + start + k] * piece, piece), piece)
            term = jnp.dot(part[k, :, :piece], w_ref[depth, columns], preferred_element_type=jnp.float32)
            total = term if total is None else total + term
    return total


def side_sum(parts, piece):
    return sum(part[k, :, piece:].astype(jnp.float32) for part in parts for k in range(part.shape[0]))


def own_kernel(starts, info_ref, *refs):
    *parts, w_ref, total_ref, side_ref = refs
    piece = w_ref.shape[1]
    side_ref[...] = side_sum(parts, piece)
    tile = min(piece, 256)
    for n in range(piece // tile):
        columns = slice(n * tile, (n + 1) * tile)
        total_ref[:, columns] = piece_dots(info_ref, w_ref, parts, starts, columns)


def layer_kernel(rank, owners, owned, tick, chunks, starts, extra, info_ref, *refs):
    *parts, w_ref, x_ref, up_ref, total_ref, side_ref, o_ref = refs
    piece = x_ref.shape[1]
    width = w_ref.shape[0]
    *parts, terms = [*parts[: len(parts) - extra], parts[len(parts) - extra :]]
    side = side_ref[...] + side_sum(parts, piece)
    if extra:
        side = side + side_sum(terms, 0)
    squares = side[:, rank : rank + 1] + side[:, rank + 1 : rank + 2]
    scale = lax.rsqrt(squares / width + 1e-05)
    inner = (2.0 * side[:, :rank]).astype(jnp.bfloat16)
    rows_of = [adapter_at(info_ref, owners, owned, tick, chunks, b) for b in range(SPAN)]
    tile = min(piece, 256)
    for n in range(piece // tile):
        columns = slice(n * tile, (n + 1) * tile)
        delta = [
            jnp.dot(
                inner[b * BLOCK : (b + 1) * BLOCK], up_ref[row, :, columns], preferred_element_type=jnp.float32
            )
            for b, row in enumerate(rows_of)
        ]
        total = jnp.concatenate(delta, axis=0) if SPAN > 1 else delta[0]
        total += total_ref[:, columns] + piece_dots(info_ref, w_ref, parts, starts, columns)
        h = x_ref[:, columns].astype(jnp.float32)
        o_ref[:, columns] = (h + scale * total).astype(jnp.bfloat16)


def join_kernel(info_ref, *refs):
    *blocks, o_ref = refs
    rows = blocks[0].shape[0]
    for i, block in enumerate(blocks):
        o_ref[i * rows : (i + 1) * rows, :] = block[...]


def home_kernel(sections, counts, info_ref, *refs):
    *blocks, o_ref = refs
    taken = 0
    for section, count in zip(range(sections), counts):
        own = blocks[taken : taken + count]
        taken += count

        @pl.when(info_ref[0] == section)
        def _():
            row = 0
            for block in own:
                span = block.shape[0]
                o_ref[row : row + span, :] = block[...]
                row += span


def reward_kernel(sections, counts, info_ref, *refs):
    *blocks, head_ref, score_ref = refs
    taken = 0
    for section, count in zip(range(sections), counts):
        own = blocks[taken : taken + count]
        taken += count

        @pl.when(info_ref[0] == section)
        def _():
            row = 0
            for block in own:
                span = block.shape[0]
                score_ref[:, row : row + span] = lax.dot_general(
                    head_ref[...], block[...], (((1,), (1,)), ((), ())), preferred_element_type=jnp.float32
                )
                row += span


def add_kernel(info_ref, *refs):
    *terms, o_ref = refs
    o_ref[...] = sum(term[...] for term in terms)


def score_kernel(info_ref, limits_ref, *refs):
    *terms, o_ref = refs
    total = sum(term[...] for term in terms)
    lane = lax.broadcasted_iota(jnp.int32, (1, BLOCK), 1)
    for b in range(total.shape[1] // BLOCK):
        columns = slice(b * BLOCK, (b + 1) * BLOCK)
        o_ref[:, columns] = jnp.where(lane < limits_ref[:, b : b + 1], total[:, columns], 0.0)


def cut(maps_ref, info_ref, place, out):
    piece = out.shape[-1]
    out[...] = maps_ref[:, :, pl.ds(pl.multiple_of((info_ref[1] ^ place) * piece, piece), piece)]


def cut_other_kernel(chips, info_ref, maps_ref, o_ref):
    for k in range(chips):
        cut(maps_ref, info_ref, 2 * k + 1, o_ref.at[k])


def cut_own_kernel(chips, info_ref, maps_ref, other_ref, *outs):
    for k, out in enumerate(outs):
        cut(maps_ref, info_ref, 2 * k, out.at[0])
        out[1] = other_ref[k]


def stack_kernel(info_ref, *refs):
    *blocks, o_ref = refs
    count, owned = blocks[0].shape[:2]
    for i, block in enumerate(blocks):
        for j in range(count):
            start = (i * count + j) * owned
            o_ref[start : start + owned] = block[j]


def shards(
    entering_hidden,
    section_weight,
    section_norm_gain,
    plugin_narrowing_factors,
    plugin_widening_factors,
    reward_head,
    adapter_of_block,
    live_block_rows,
):
    sections = lax.axis_size("section")
    section = lax.axis_index("section")
    chips = lax.axis_size("chip")
    cores = lax.axis_size("core")
    owners = chips * cores
    everyone = ("chip", "core")
    batches_here, rows, piece = entering_hidden.shape
    micro = batches_here * sections
    span = BLOCK * SPAN
    per_micro = rows // span
    owned = plugin_narrowing_factors.shape[1]
    rank = plugin_narrowing_factors.shape[3]
    chunks = micro * per_micro
    pairwise = chips == 4 and cores == 2

    chip, core = lax.axis_index("chip"), lax.axis_index("core")
    if pairwise:
        near_by, far = jnp.where(core == 0, 1, 2), jnp.where(core == 0, 2, 1)
        place = chip * cores + core
        parts = [(0, 0), (0, 1), (near_by, 0), (near_by, 1), (3, 0), (far, 1), (far, 0), (3, 1)]
        order = [(chip ^ there) * cores + (core ^ other) for there, other in parts]
    else:
        place = jnp.zeros_like(core)
        order = [i * cores + (core + k) % cores for k in range(cores) for i in range(chips)]
    info = jnp.concatenate([jnp.stack([section, place] + order), adapter_of_block.reshape(-1)])
    info = info.astype(jnp.int32)

    def over_cores(part):
        return [
            lax.ppermute(part, "core", [((c + k) % cores, c) for c in range(cores)]) for k in range(1, cores)
        ]

    def over_chips(part, steps):
        pairs = [(i * cores + c, (i ^ steps[c]) * cores + c) for i in range(chips) for c in range(cores)]
        return lax.ppermute(part, everyone, pairs)

    def spread(maps, after):
        if not pairwise:
            maps = jnp.moveaxis(maps.reshape(owned, rank, owners, piece), 2, 0)
            maps = lax.all_to_all(maps, everyone, split_axis=0, concat_axis=0, tiled=True)
            table = maps.reshape(owners * owned, rank, piece)
            return lambda after: table, after
        size = 2 * maps.size
        out_shape = pltpu.VMEM((chips, owned, rank, piece), maps.dtype)
        kernel = functools.partial(cut_other_kernel, chips)
        other = call(kernel, out_shape, (info, maps), "cut_other", 0, 0, after=after)
        (swapped,) = over_cores(other)
        out_shape = [pltpu.VMEM((cores, owned, rank, piece), maps.dtype) for _ in range(chips)]
        kernel = functools.partial(cut_own_kernel, chips)
        mine, *blocks = call(kernel, out_shape, (info, maps, swapped), "cut_own", 0, 0)
        blocks = [over_chips(block, (k, k)) for k, block in zip(range(1, chips), blocks)]
        out_shape = pltpu.VMEM((owners * owned, rank, piece), maps.dtype)
        return functools.partial(call, stack_kernel, out_shape, (info, mine, *blocks), "stack", 0, 0), [mine]

    feeds = []
    for m in range(micro):
        home, slot = divmod(m, batches_here)
        block = entering_hidden[slot]
        feeds.append(block if home == 0 else lax.ppermute(block, "section", [(home, 0)]))

    def gather_start(message):
        if not pairwise:
            parts = lax.all_to_all(message, "chip", split_axis=0, concat_axis=0, tiled=True)
            return [parts] + over_cores(parts)
        first = over_chips(message, (1, 2))
        (other,) = over_cores(message)
        second = over_chips(other, (1, 2))
        return [message, other, first, second]

    def gather_end(parts, after):
        if not pairwise:
            return [(part, chips * (1 + k)) for k, part in enumerate(parts[1:])]
        _, _, first, second = parts
        first = tie(first, after) if after else first
        third = over_chips(first, (2, 1))
        late = [first, second, third] + [over_cores(part)[0] for part in (first, second, third)]
        return list(zip(late, range(2, 8)))

    def prep(tick, sources, blocks, after):
        out_shape = (
            pltpu.VMEM((span, piece), jnp.bfloat16),
            pltpu.VMEM((1 if pairwise else chips, span, piece + SIDE), jnp.bfloat16),
        )
        tabled = tick > 0 or not pairwise
        kernel = functools.partial(prep_kernel, rank, owners, owned, tick, chunks, blocks, tabled)
        args = (info, *sources, section_norm_gain) + ((down,) if tabled else ())
        return call(kernel, out_shape, args, "prep", 2 * span * piece * SIDE * bool(tick), span * piece * 8 * bool(tick), after=after)

    def own_layer(parts, after):
        width = piece * owners
        kernel = functools.partial(own_kernel, [start for _, start in parts])
        out_shape = (pltpu.VMEM((span, piece), jnp.float32), pltpu.VMEM((span, SIDE), jnp.float32))
        args = (info, *[part for part, _ in parts], weight)
        return call(kernel, out_shape, args, "own", span * width * piece // 2 * bool(after), width * piece // 2 * bool(after), after=after)

    def layer(tick, parts, x, sums, terms, after):
        width = piece * owners
        kernel = functools.partial(layer_kernel, rank, owners, owned, tick, chunks, [start for _, start in parts], len(terms))
        args = (info, *[part for part, _ in parts], *terms, weight, x, up, *sums)
        out_shape = pltpu.VMEM((span, piece), jnp.bfloat16)
        return call(kernel, out_shape, args, "layer", 2 * span * width * piece, 2 * width * piece, after=after)

    arrived, state, sums, done, home_blocks, returned = {}, {}, {}, {}, {}, {}
    ticks = chunks + LAG * (sections - 1)

    def active(tick):
        return [s for s in range(sections) if 0 <= tick - LAG * s < chunks]

    def begin(tick):
        sources, blocks = [], []
        if 0 in active(tick):
            m, b = divmod(tick, per_micro)
            sources.append(feeds[m])
            blocks.append(b)
        if active(tick) != [0]:
            sources.append(arrived.pop(tick))
            blocks.append(0)
        if tick == 0:
            after = []
        else:
            after = [sums[tick - 1][1]]
        x, message = prep(tick, sources, blocks, after)
        parts = gather_start(message)
        state[tick] = [x, message, parts, parts[1] if pairwise else None]

    def own_chip(tick, after):
        parts = state[tick][2]
        own = [(parts[0], 0), (parts[1], 1)] if pairwise else [(parts[0], 0)]
        sums[tick] = own_layer(own, after)
        state[tick][2] = gather_end(parts, [sums[tick][1]] if after else [])

    down_maps = jnp.swapaxes(plugin_narrowing_factors[0], 1, 2)
    down = None
    if not pairwise:
        down = spread(down_maps, ())[0](after=[])
    up, begun = spread(plugin_widening_factors[0], ())
    begin(0)
    if pairwise:
        down, also = spread(down_maps, begun)
        begun = begun + also
    weight = staged(section_weight[0], [*begun, state[0][1]])
    up = up(after=[weight])
    own_chip(0, [])
    terms = []
    if pairwise:
        down = down(after=[weight])
        parts = [(state[0][1], 0), (state[0][3], 1)] + state[0][2]
        kernel = functools.partial(owner_kernel, rank, owners, owned, [start for _, start in parts])
        out_shape = pltpu.VMEM((1, span, SIDE), jnp.bfloat16)
        args = (info, *[part for part, _ in parts], down_maps)
        side = call(kernel, out_shape, args, "owner", 2 * span * piece * owners * rank, 0)
        side = call(add_kernel, out_shape, (info, side, *over_cores(side)), "add", 0, 0)
        terms = [side] + [over_chips(side, (k, k)) for k in (1, 2, 3)]
    for tick in range(ticks):
        after = []
        if tick + 1 < ticks:
            begin(tick + 1)
            after.append(state[tick + 1][1])
        if tick in returned:
            after.append(returned.pop(tick))
        x, _, parts, _ = state.pop(tick)
        if pairwise:
            size = piece * piece * owners
            x = tie(x, [part for part, _ in parts[3:5]] + after, span * size, size)
        h = layer(tick, parts, x, sums[tick], terms if tick == 0 else [], after)
        if tick + 1 < ticks:
            own_chip(tick + 1, [h])
        onward = [(s, s + 1) for s in active(tick) if s + 1 < sections]
        if onward:
            arrived[tick + LAG] = lax.ppermute(h, "section", onward)
        if sections - 1 in active(tick):
            last = tick - LAG * (sections - 1)
            m = last // per_micro
            home = m // batches_here
            done[last] = h
            if last % per_micro == per_micro - 1:
                block = [done[m * per_micro + b] for b in range(per_micro)]
                if home != sections - 1:
                    if per_micro > 1:
                        out_shape = pltpu.VMEM((rows, piece), jnp.bfloat16)
                        block = [call(join_kernel, out_shape, (info, *block), "join", 0, rows * piece * 4)]
                    block = [lax.ppermute(block[0], "section", [(sections - 1, home)])]
                    if tick + 2 < ticks:
                        returned[tick + 2] = block[0]
                home_blocks[m] = block

    hidden, scores = [], []
    for slot in range(batches_here):
        blocks = [home_blocks[home * batches_here + slot] for home in range(sections)]
        counts = [len(block) for block in blocks]
        parts = [part for block in blocks for part in block]
        out_shape = pltpu.VMEM((1, rows), jnp.float32)
        kernel = functools.partial(reward_kernel, sections, counts)
        score = call(kernel, out_shape, (info, *parts, reward_head[None]), "reward", 0, 0)
        out_shape = jax.ShapeDtypeStruct((rows, piece), jnp.bfloat16)
        kernel = functools.partial(home_kernel, sections, counts)
        hidden.append(call(kernel, out_shape, (info, *parts), "home", 2 * rows * piece, rows * piece * 4, after=[score]))
        near_by = pltpu.VMEM((1, rows), jnp.float32)
        if pairwise:
            score = call(add_kernel, near_by, (info, score, *over_cores(score)), "add", 0, rows * 4)
            terms = [score] + [over_chips(score, (k, k)) for k in (1, 2, 3)]
        else:
            terms = [lax.psum(score, everyone)]
        limits = live_block_rows[slot : slot + 1]
        out_shape = jax.ShapeDtypeStruct((1, rows), jnp.float32)
        scores.append(call(score_kernel, out_shape, (info, limits, *terms), "score", 0, rows * 4))
    if batches_here == 1:
        return (hidden[0][None], scores[0])
    return (jnp.stack(hidden), jnp.concatenate(scores, axis=0))


def solution(mesh):
    sections, owners = mesh.shape["section"], mesh.shape["mp"]
    cores = 2 if owners % 2 == 0 else 1
    fine = jax.sharding.Mesh(
        mesh.devices.reshape(sections, owners // cores, cores), ("section", "chip", "core")
    )
    mp = ("chip", "core")
    placed = (
        P("section", None, mp),
        P("section", None, mp),
        P("section", mp),
        P("section", mp, None, None),
        P("section", mp, None, None),
        P(mp),
        P(),
        P("section", None),
    )
    return jax.shard_map(
        shards,
        mesh=fine,
        in_specs=placed,
        out_specs=(P("section", None, mp), P("section", None)),
        check_vma=False,
    )
```

```python
import functools

import jax
import jax.numpy as jnp
from jax import lax
from jax.experimental import pallas as pl
from jax.experimental.pallas import tpu as pltpu
from jax.sharding import PartitionSpec as P

BLOCK = 128
SIDE = 128
LAG = 2
SPAN = 1

VMEM = pl.BlockSpec(memory_space=pltpu.VMEM)
SMEM = pl.BlockSpec(memory_space=pltpu.SMEM)


def near(x):
    return pltpu.with_memory_space_constraint(x, pltpu.VMEM)


def call(kernel, out_shape, args, name, flops, moved, limit=8, after=()):
    info, *arrays = args
    count = len(arrays)

    def body(info_ref, *refs):
        kernel(info_ref, *refs[:count], *refs[count + len(after) :])

    return pl.pallas_call(
        body,
        out_shape=out_shape,
        in_specs=[SMEM] + [VMEM] * count + [pl.BlockSpec(memory_space=pl.ANY)] * len(after),
        out_specs=jax.tree.map(lambda _: VMEM, out_shape),
        compiler_params=pltpu.CompilerParams(vmem_limit_bytes=limit << 20),
        cost_estimate=pl.CostEstimate(flops=flops, bytes_accessed=moved, transcendentals=0),
        name=name,
    )(info, *map(near, arrays), *after)


def tie(x, after, flops=0, moved=0):
    def body(*_):
        pass

    return pl.pallas_call(
        body,
        out_shape=pltpu.VMEM(x.shape, x.dtype),
        in_specs=[VMEM] + [pl.BlockSpec(memory_space=pl.ANY)] * len(after),
        out_specs=VMEM,
        input_output_aliases={0: 0},
        compiler_params=pltpu.CompilerParams(vmem_limit_bytes=1 << 20),
        cost_estimate=pl.CostEstimate(flops=flops, bytes_accessed=moved, transcendentals=0),
        name="tie",
    )(near(x), *after)


def adapter_at(info_ref, owners, owned, tick, chunks, block):
    mine = jnp.clip(tick - LAG * info_ref[0], 0, chunks - 1)
    adapter = info_ref[2 + owners + mine * SPAN + block]
    if owned == 1:
        return adapter ^ info_ref[1]
    return (lax.div(adapter, owned) ^ info_ref[1]) * owned + lax.rem(adapter, owned)


def prep_kernel(rank, owners, owned, tick, chunks, block, tabled, info_ref, *refs):
    *sources, gain_ref, x_ref, m_ref = refs
    if tabled:
        *sources, gain_ref, down_ref = sources + [gain_ref]
    copies = m_ref.shape[0]
    rows, piece = x_ref.shape
    picked = [source[b * rows : (b + 1) * rows, :].astype(jnp.float32) for source, b in zip(sources, block)]
    x = jnp.where(info_ref[0] == 0, *picked) if len(picked) == 2 else picked[0]
    x_ref[...] = x.astype(jnp.bfloat16)
    scaled = (x * gain_ref[...].astype(jnp.float32)).astype(jnp.bfloat16)
    squares = jnp.sum(x * x, axis=1, keepdims=True)
    high = squares.astype(jnp.bfloat16).astype(jnp.float32)
    low = squares - high
    lane = lax.broadcasted_iota(jnp.int32, (rows, SIDE), 1)
    inner = jnp.zeros((rows, SIDE), jnp.float32)
    if tabled:
        inner = []
        for b in range(SPAN):
            product = lax.dot_general(
                scaled[b * BLOCK : (b + 1) * BLOCK],
                down_ref[adapter_at(info_ref, owners, owned, tick, chunks, b)],
                (((1,), (1,)), ((), ())),
                preferred_element_type=jnp.float32,
            )
            inner.append(jnp.concatenate([product, jnp.zeros((BLOCK, SIDE - rank), jnp.float32)], axis=1))
        inner = jnp.concatenate(inner, axis=0) if SPAN > 1 else inner[0]
    side = jnp.where(lane == rank, high, jnp.where(lane == rank + 1, low, inner)).astype(jnp.bfloat16)
    for copy in range(copies):
        m_ref[copy, :, :piece] = scaled
        m_ref[copy, :, piece:] = side


def owner_kernel(rank, owners, owned, starts, info_ref, *refs):
    *parts, down_ref, o_ref = refs
    rows = o_ref.shape[1]
    piece = parts[0].shape[2] - SIDE
    sums = []
    for o in range(owned):
        total = None
        for part, start in zip(parts, starts):
            columns = pl.ds(pl.multiple_of(info_ref[2 + start] * piece, piece), piece)
            term = lax.dot_general(
                part[0, :, :piece], down_ref[o, :, columns], (((1,), (1,)), ((), ())), preferred_element_type=jnp.float32
            )
            total = term if total is None else total + term
        sums.append(total)
    for b in range(SPAN):
        adapter = info_ref[2 + owners + b]
        block = slice(b * BLOCK, (b + 1) * BLOCK)
        product = jnp.zeros((BLOCK, rank), jnp.float32)
        for o, total in enumerate(sums):
            product = jnp.where(adapter == info_ref[1] * owned + o, total[block], product)
        side = jnp.concatenate([product, jnp.zeros((BLOCK, SIDE - rank), jnp.float32)], axis=1)
        o_ref[0, block, :] = side.astype(jnp.bfloat16)


def stage_kernel(w_ref, *refs):
    *_, o_ref, sem = refs
    copy = pltpu.make_async_copy(w_ref, o_ref, sem)
    copy.start()
    copy.wait()


def staged(weight, after):
    return pl.pallas_call(
        stage_kernel,
        out_shape=pltpu.VMEM(weight.shape, weight.dtype),
        in_specs=[pl.BlockSpec(memory_space=pl.ANY)] * (1 + len(after)),
        out_specs=VMEM,
        scratch_shapes=[pltpu.SemaphoreType.DMA],
        compiler_params=pltpu.CompilerParams(vmem_limit_bytes=4 << 20),
        cost_estimate=pl.CostEstimate(flops=0, bytes_accessed=2 * weight.size, transcendentals=0),
        name="stage",
    )(pltpu.with_memory_space_constraint(weight, pltpu.HBM), *after)


def piece_dots(info_ref, w_ref, parts, starts, columns):
    total = None
    for part, start in zip(parts, starts):
        piece = w_ref.shape[1]
        for k in range(part.shape[0]):
            depth = pl.ds(pl.multiple_of(info_ref[2 + start + k] * piece, piece), piece)
            term = jnp.dot(part[k, :, :piece], w_ref[depth, columns], preferred_element_type=jnp.float32)
            total = term if total is None else total + term
    return total


def side_sum(parts, piece):
    return sum(part[k, :, piece:].astype(jnp.float32) for part in parts for k in range(part.shape[0]))


def own_kernel(starts, info_ref, *refs):
    *parts, w_ref, total_ref, side_ref = refs
    piece = w_ref.shape[1]
    side_ref[...] = side_sum(parts, piece)
    tile = min(piece, 256)
    for n in range(piece // tile):
        columns = slice(n * tile, (n + 1) * tile)
        total_ref[:, columns] = piece_dots(info_ref, w_ref, parts, starts, columns)


def layer_kernel(rank, owners, owned, tick, chunks, starts, extra, info_ref, *refs):
    *parts, w_ref, x_ref, up_ref, total_ref, side_ref, o_ref = refs
    piece = x_ref.shape[1]
    width = w_ref.shape[0]
    *parts, terms = [*parts[: len(parts) - extra], parts[len(parts) - extra :]]
    side = side_ref[...] + side_sum(parts, piece)
    if extra:
        side = side + side_sum(terms, 0)
    squares = side[:, rank : rank + 1] + side[:, rank + 1 : rank + 2]
    scale = lax.rsqrt(squares / width + 1e-05)
    inner = (2.0 * side[:, :rank]).astype(jnp.bfloat16)
    rows_of = [adapter_at(info_ref, owners, owned, tick, chunks, b) for b in range(SPAN)]
    tile = min(piece, 256)
    for n in range(piece // tile):
        columns = slice(n * tile, (n + 1) * tile)
        delta = [
            jnp.dot(
                inner[b * BLOCK : (b + 1) * BLOCK], up_ref[row, :, columns], preferred_element_type=jnp.float32
            )
            for b, row in enumerate(rows_of)
        ]
        total = jnp.concatenate(delta, axis=0) if SPAN > 1 else delta[0]
        total += total_ref[:, columns] + piece_dots(info_ref, w_ref, parts, starts, columns)
        h = x_ref[:, columns].astype(jnp.float32)
        o_ref[:, columns] = (h + scale * total).astype(jnp.bfloat16)


def join_kernel(info_ref, *refs):
    *blocks, o_ref = refs
    rows = blocks[0].shape[0]
    for i, block in enumerate(blocks):
        o_ref[i * rows : (i + 1) * rows, :] = block[...]


def home_kernel(sections, counts, info_ref, *refs):
    *blocks, o_ref = refs
    taken = 0
    for section, count in zip(range(sections), counts):
        own = blocks[taken : taken + count]
        taken += count

        @pl.when(info_ref[0] == section)
        def _():
            row = 0
            for block in own:
                span = block.shape[0]
                o_ref[row : row + span, :] = block[...]
                row += span


def reward_kernel(sections, counts, info_ref, *refs):
    *blocks, head_ref, score_ref = refs
    taken = 0
    for section, count in zip(range(sections), counts):
        own = blocks[taken : taken + count]
        taken += count

        @pl.when(info_ref[0] == section)
        def _():
            row = 0
            for block in own:
                span = block.shape[0]
                score_ref[:, row : row + span] = lax.dot_general(
                    head_ref[...], block[...], (((1,), (1,)), ((), ())), preferred_element_type=jnp.float32
                )
                row += span


def add_kernel(info_ref, *refs):
    *terms, o_ref = refs
    o_ref[...] = sum(term[...] for term in terms)


def score_kernel(info_ref, limits_ref, *refs):
    *terms, o_ref = refs
    total = sum(term[...] for term in terms)
    lane = lax.broadcasted_iota(jnp.int32, (1, BLOCK), 1)
    for b in range(total.shape[1] // BLOCK):
        columns = slice(b * BLOCK, (b + 1) * BLOCK)
        o_ref[:, columns] = jnp.where(lane < limits_ref[:, b : b + 1], total[:, columns], 0.0)


def cut(maps_ref, info_ref, place, out):
    piece = out.shape[-1]
    out[...] = maps_ref[:, :, pl.ds(pl.multiple_of((info_ref[1] ^ place) * piece, piece), piece)]


def cut_other_kernel(chips, info_ref, maps_ref, o_ref):
    for k in range(chips):
        cut(maps_ref, info_ref, 2 * k + 1, o_ref.at[k])


def cut_own_kernel(chips, info_ref, maps_ref, other_ref, *outs):
    for k, out in enumerate(outs):
        cut(maps_ref, info_ref, 2 * k, out.at[0])
        out[1] = other_ref[k]


def stack_kernel(info_ref, *refs):
    *blocks, o_ref = refs
    count, owned = blocks[0].shape[:2]
    for i, block in enumerate(blocks):
        for j in range(count):
            start = (i * count + j) * owned
            o_ref[start : start + owned] = block[j]


def shards(
    entering_hidden,
    section_weight,
    section_norm_gain,
    plugin_narrowing_factors,
    plugin_widening_factors,
    reward_head,
    adapter_of_block,
    live_block_rows,
):
    sections = lax.axis_size("section")
    section = lax.axis_index("section")
    chips = lax.axis_size("chip")
    cores = lax.axis_size("core")
    owners = chips * cores
    everyone = ("chip", "core")
    batches_here, rows, piece = entering_hidden.shape
    micro = batches_here * sections
    span = BLOCK * SPAN
    per_micro = rows // span
    owned = plugin_narrowing_factors.shape[1]
    rank = plugin_narrowing_factors.shape[3]
    chunks = micro * per_micro
    pairwise = chips == 4 and cores == 2

    chip, core = lax.axis_index("chip"), lax.axis_index("core")
    if pairwise:
        near_by, far = jnp.where(core == 0, 1, 2), jnp.where(core == 0, 2, 1)
        place = chip * cores + core
        parts = [(0, 0), (0, 1), (near_by, 0), (near_by, 1), (3, 0), (far, 1), (far, 0), (3, 1)]
        order = [(chip ^ there) * cores + (core ^ other) for there, other in parts]
    else:
        place = jnp.zeros_like(core)
        order = [i * cores + (core + k) % cores for k in range(cores) for i in range(chips)]
    info = jnp.concatenate([jnp.stack([section, place] + order), adapter_of_block.reshape(-1)])
    info = info.astype(jnp.int32)

    def over_cores(part):
        return [
            lax.ppermute(part, "core", [((c + k) % cores, c) for c in range(cores)]) for k in range(1, cores)
        ]

    def over_chips(part, steps):
        pairs = [(i * cores + c, (i ^ steps[c]) * cores + c) for i in range(chips) for c in range(cores)]
        return lax.ppermute(part, everyone, pairs)

    def spread(maps, after):
        if not pairwise:
            maps = jnp.moveaxis(maps.reshape(owned, rank, owners, piece), 2, 0)
            maps = lax.all_to_all(maps, everyone, split_axis=0, concat_axis=0, tiled=True)
            table = maps.reshape(owners * owned, rank, piece)
            return lambda after: table, after
        size = 2 * maps.size
        out_shape = pltpu.VMEM((chips, owned, rank, piece), maps.dtype)
        kernel = functools.partial(cut_other_kernel, chips)
        other = call(kernel, out_shape, (info, maps), "cut_other", 0, 0, after=after)
        (swapped,) = over_cores(other)
        out_shape = [pltpu.VMEM((cores, owned, rank, piece), maps.dtype) for _ in range(chips)]
        kernel = functools.partial(cut_own_kernel, chips)
        mine, *blocks = call(kernel, out_shape, (info, maps, swapped), "cut_own", 0, 0)
        blocks = [over_chips(block, (k, k)) for k, block in zip(range(1, chips), blocks)]
        out_shape = pltpu.VMEM((owners * owned, rank, piece), maps.dtype)
        return functools.partial(call, stack_kernel, out_shape, (info, mine, *blocks), "stack", 0, 0), [mine]

    feeds = []
    for m in range(micro):
        home, slot = divmod(m, batches_here)
        block = entering_hidden[slot]
        feeds.append(block if home == 0 else lax.ppermute(block, "section", [(home, 0)]))

    def gather_start(message):
        if not pairwise:
            parts = lax.all_to_all(message, "chip", split_axis=0, concat_axis=0, tiled=True)
            return [parts] + over_cores(parts)
        first = over_chips(message, (1, 2))
        (other,) = over_cores(message)
        second = over_chips(other, (1, 2))
        return [message, other, first, second]

    def gather_end(parts, after):
        if not pairwise:
            return [(part, chips * (1 + k)) for k, part in enumerate(parts[1:])]
        _, _, first, second = parts
        if after:
            first = tie(first, after)
        else:
            second = tie(second, [sums[0][1]])
        third = over_chips(first, (2, 1))
        late = [first, second, third] + [over_cores(part)[0] for part in (first, second, third)]
        return list(zip(late, range(2, 8)))

    def prep(tick, sources, blocks, after):
        out_shape = (
            pltpu.VMEM((span, piece), jnp.bfloat16),
            pltpu.VMEM((1 if pairwise else chips, span, piece + SIDE), jnp.bfloat16),
        )
        tabled = tick > 0 or not pairwise
        kernel = functools.partial(prep_kernel, rank, owners, owned, tick, chunks, blocks, tabled)
        args = (info, *sources, section_norm_gain) + ((down,) if tabled else ())
        return call(kernel, out_shape, args, "prep", 2 * span * piece * SIDE * bool(tick), span * piece * 8 * bool(tick), after=after)

    def own_layer(parts, after):
        width = piece * owners
        kernel = functools.partial(own_kernel, [start for _, start in parts])
        out_shape = (pltpu.VMEM((span, piece), jnp.float32), pltpu.VMEM((span, SIDE), jnp.float32))
        args = (info, *[part for part, _ in parts], weight)
        return call(kernel, out_shape, args, "own", span * width * piece // 2 * bool(after), width * piece // 2 * bool(after), after=after)

    def layer(tick, parts, x, sums, terms, after):
        width = piece * owners
        kernel = functools.partial(layer_kernel, rank, owners, owned, tick, chunks, [start for _, start in parts], len(terms))
        args = (info, *[part for part, _ in parts], *terms, weight, x, up, *sums)
        out_shape = pltpu.VMEM((span, piece), jnp.bfloat16)
        return call(kernel, out_shape, args, "layer", 2 * span * width * piece, 2 * width * piece, after=after)

    arrived, state, sums, done, home_blocks, returned = {}, {}, {}, {}, {}, {}
    ticks = chunks + LAG * (sections - 1)

    def active(tick):
        return [s for s in range(sections) if 0 <= tick - LAG * s < chunks]

    def begin(tick):
        sources, blocks = [], []
        if 0 in active(tick):
            m, b = divmod(tick, per_micro)
            sources.append(feeds[m])
            blocks.append(b)
        if active(tick) != [0]:
            sources.append(arrived.pop(tick))
            blocks.append(0)
        if tick == 0:
            after = []
        else:
            after = [sums[tick - 1][1]]
        x, message = prep(tick, sources, blocks, after)
        parts = gather_start(message)
        state[tick] = [x, message, parts, parts[1] if pairwise else None]

    def own_chip(tick, after):
        parts = state[tick][2]
        own = [(parts[0], 0), (parts[1], 1)] if pairwise else [(parts[0], 0)]
        sums[tick] = own_layer(own, after)
        state[tick][2] = gather_end(parts, [sums[tick][1]] if after else [])

    down_maps = jnp.swapaxes(plugin_narrowing_factors[0], 1, 2)
    down = None
    if not pairwise:
        down = spread(down_maps, ())[0](after=[])
    up, begun = spread(plugin_widening_factors[0], ())
    begin(0)
    if pairwise:
        down, also = spread(down_maps, begun)
        begun = begun + also
    weight = staged(section_weight[0], [*begun, state[0][1]])
    up = up(after=[weight])
    own_chip(0, [])
    terms = []
    if pairwise:
        down = down(after=[weight])
        parts = [(state[0][1], 0), (state[0][3], 1)] + state[0][2]
        kernel = functools.partial(owner_kernel, rank, owners, owned, [start for _, start in parts])
        out_shape = pltpu.VMEM((1, span, SIDE), jnp.bfloat16)
        args = (info, *[part for part, _ in parts], down_maps)
        side = call(kernel, out_shape, args, "owner", 2 * span * piece * owners * rank, 0)
        side = call(add_kernel, out_shape, (info, side, *over_cores(side)), "add", 0, 0)
        terms = [side] + [over_chips(side, (k, k)) for k in (1, 2, 3)]
    for tick in range(ticks):
        after = []
        if tick + 1 < ticks:
            begin(tick + 1)
            after.append(state[tick + 1][1])
        if tick in returned:
            after.append(returned.pop(tick))
        x, _, parts, _ = state.pop(tick)
        if pairwise:
            size = piece * piece * owners
            x = tie(x, [part for part, _ in parts[3:5]] + after, span * size, size)
        h = layer(tick, parts, x, sums[tick], terms if tick == 0 else [], after)
        if tick + 1 < ticks:
            own_chip(tick + 1, [h])
        onward = [(s, s + 1) for s in active(tick) if s + 1 < sections]
        if onward:
            arrived[tick + LAG] = lax.ppermute(h, "section", onward)
        if sections - 1 in active(tick):
            last = tick - LAG * (sections - 1)
            m = last // per_micro
            home = m // batches_here
            done[last] = h
            if last % per_micro == per_micro - 1:
                block = [done[m * per_micro + b] for b in range(per_micro)]
                if home != sections - 1:
                    if per_micro > 1:
                        out_shape = pltpu.VMEM((rows, piece), jnp.bfloat16)
                        block = [call(join_kernel, out_shape, (info, *block), "join", 0, rows * piece * 4)]
                    block = [lax.ppermute(block[0], "section", [(sections - 1, home)])]
                    if tick + 2 < ticks:
                        returned[tick + 2] = block[0]
                home_blocks[m] = block

    hidden, scores = [], []
    for slot in range(batches_here):
        blocks = [home_blocks[home * batches_here + slot] for home in range(sections)]
        counts = [len(block) for block in blocks]
        parts = [part for block in blocks for part in block]
        out_shape = pltpu.VMEM((1, rows), jnp.float32)
        kernel = functools.partial(reward_kernel, sections, counts)
        score = call(kernel, out_shape, (info, *parts, reward_head[None]), "reward", 0, 0)
        out_shape = jax.ShapeDtypeStruct((rows, piece), jnp.bfloat16)
        kernel = functools.partial(home_kernel, sections, counts)
        hidden.append(call(kernel, out_shape, (info, *parts), "home", 2 * rows * piece, rows * piece * 4, after=[score]))
        near_by = pltpu.VMEM((1, rows), jnp.float32)
        if pairwise:
            score = call(add_kernel, near_by, (info, score, *over_cores(score)), "add", 0, rows * 4)
            terms = [score] + [over_chips(score, (k, k)) for k in (1, 2, 3)]
        else:
            terms = [lax.psum(score, everyone)]
        limits = live_block_rows[slot : slot + 1]
        out_shape = jax.ShapeDtypeStruct((1, rows), jnp.float32)
        scores.append(call(score_kernel, out_shape, (info, limits, *terms), "score", 0, rows * 4))
    if batches_here == 1:
        return (hidden[0][None], scores[0])
    return (jnp.stack(hidden), jnp.concatenate(scores, axis=0))


def solution(mesh):
    sections, owners = mesh.shape["section"], mesh.shape["mp"]
    cores = 2 if owners % 2 == 0 else 1
    fine = jax.sharding.Mesh(
        mesh.devices.reshape(sections, owners // cores, cores), ("section", "chip", "core")
    )
    mp = ("chip", "core")
    placed = (
        P("section", None, mp),
        P("section", None, mp),
        P("section", mp),
        P("section", mp, None, None),
        P("section", mp, None, None),
        P(mp),
        P(),
        P("section", None),
    )
    return jax.shard_map(
        shards,
        mesh=fine,
        in_specs=placed,
        out_specs=(P("section", None, mp), P("section", None)),
        check_vma=False,
    )
```

```python
import functools

import jax
import jax.numpy as jnp
from jax import lax
from jax.experimental import pallas as pl
from jax.experimental.pallas import tpu as pltpu
from jax.sharding import PartitionSpec as P

BLOCK = 128
SIDE = 128
LAG = 2
SPAN = 1

VMEM = pl.BlockSpec(memory_space=pltpu.VMEM)
SMEM = pl.BlockSpec(memory_space=pltpu.SMEM)


def near(x):
    return pltpu.with_memory_space_constraint(x, pltpu.VMEM)


def call(kernel, out_shape, args, name, flops, moved, limit=8, after=()):
    info, *arrays = args
    count = len(arrays)

    def body(info_ref, *refs):
        kernel(info_ref, *refs[:count], *refs[count + len(after) :])

    return pl.pallas_call(
        body,
        out_shape=out_shape,
        in_specs=[SMEM] + [VMEM] * count + [pl.BlockSpec(memory_space=pl.ANY)] * len(after),
        out_specs=jax.tree.map(lambda _: VMEM, out_shape),
        compiler_params=pltpu.CompilerParams(vmem_limit_bytes=limit << 20),
        cost_estimate=pl.CostEstimate(flops=flops, bytes_accessed=moved, transcendentals=0),
        name=name,
    )(info, *map(near, arrays), *after)


def tie(x, after, flops=0, moved=0):
    def body(*_):
        pass

    return pl.pallas_call(
        body,
        out_shape=pltpu.VMEM(x.shape, x.dtype),
        in_specs=[VMEM] + [pl.BlockSpec(memory_space=pl.ANY)] * len(after),
        out_specs=VMEM,
        input_output_aliases={0: 0},
        compiler_params=pltpu.CompilerParams(vmem_limit_bytes=1 << 20),
        cost_estimate=pl.CostEstimate(flops=flops, bytes_accessed=moved, transcendentals=0),
        name="tie",
    )(near(x), *after)


def adapter_at(info_ref, owners, owned, tick, chunks, block):
    mine = jnp.clip(tick - LAG * info_ref[0], 0, chunks - 1)
    adapter = info_ref[2 + owners + mine * SPAN + block]
    if owned == 1:
        return adapter ^ info_ref[1]
    return (lax.div(adapter, owned) ^ info_ref[1]) * owned + lax.rem(adapter, owned)


def prep_kernel(rank, owners, owned, tick, chunks, block, tabled, info_ref, *refs):
    *sources, gain_ref, x_ref, m_ref = refs
    if tabled:
        *sources, gain_ref, down_ref = sources + [gain_ref]
    copies = m_ref.shape[0]
    rows, piece = x_ref.shape
    picked = [source[b * rows : (b + 1) * rows, :].astype(jnp.float32) for source, b in zip(sources, block)]
    x = jnp.where(info_ref[0] == 0, *picked) if len(picked) == 2 else picked[0]
    x_ref[...] = x.astype(jnp.bfloat16)
    scaled = (x * gain_ref[...].astype(jnp.float32)).astype(jnp.bfloat16)
    squares = jnp.sum(x * x, axis=1, keepdims=True)
    high = squares.astype(jnp.bfloat16).astype(jnp.float32)
    low = squares - high
    lane = lax.broadcasted_iota(jnp.int32, (rows, SIDE), 1)
    inner = jnp.zeros((rows, SIDE), jnp.float32)
    if tabled:
        inner = []
        for b in range(SPAN):
            product = lax.dot_general(
                scaled[b * BLOCK : (b + 1) * BLOCK],
                down_ref[adapter_at(info_ref, owners, owned, tick, chunks, b)],
                (((1,), (1,)), ((), ())),
                preferred_element_type=jnp.float32,
            )
            inner.append(jnp.concatenate([product, jnp.zeros((BLOCK, SIDE - rank), jnp.float32)], axis=1))
        inner = jnp.concatenate(inner, axis=0) if SPAN > 1 else inner[0]
    side = jnp.where(lane == rank, high, jnp.where(lane == rank + 1, low, inner)).astype(jnp.bfloat16)
    for copy in range(copies):
        m_ref[copy, :, :piece] = scaled
        m_ref[copy, :, piece:] = side


def owner_kernel(rank, owners, owned, starts, info_ref, *refs):
    *parts, down_ref, o_ref = refs
    rows = o_ref.shape[1]
    piece = parts[0].shape[2] - SIDE
    sums = []
    for o in range(owned):
        total = None
        for part, start in zip(parts, starts):
            columns = pl.ds(pl.multiple_of(info_ref[2 + start] * piece, piece), piece)
            term = lax.dot_general(
                part[0, :, :piece], down_ref[o, :, columns], (((1,), (1,)), ((), ())), preferred_element_type=jnp.float32
            )
            total = term if total is None else total + term
        sums.append(total)
    for b in range(SPAN):
        adapter = info_ref[2 + owners + b]
        block = slice(b * BLOCK, (b + 1) * BLOCK)
        product = jnp.zeros((BLOCK, rank), jnp.float32)
        for o, total in enumerate(sums):
            product = jnp.where(adapter == info_ref[1] * owned + o, total[block], product)
        side = jnp.concatenate([product, jnp.zeros((BLOCK, SIDE - rank), jnp.float32)], axis=1)
        o_ref[0, block, :] = side.astype(jnp.bfloat16)


def stage_kernel(w_ref, *refs):
    *_, o_ref, sem = refs
    copy = pltpu.make_async_copy(w_ref, o_ref, sem)
    copy.start()
    copy.wait()


def staged(weight, after):
    return pl.pallas_call(
        stage_kernel,
        out_shape=pltpu.VMEM(weight.shape, weight.dtype),
        in_specs=[pl.BlockSpec(memory_space=pl.ANY)] * (1 + len(after)),
        out_specs=VMEM,
        scratch_shapes=[pltpu.SemaphoreType.DMA],
        compiler_params=pltpu.CompilerParams(vmem_limit_bytes=4 << 20),
        cost_estimate=pl.CostEstimate(flops=0, bytes_accessed=2 * weight.size, transcendentals=0),
        name="stage",
    )(pltpu.with_memory_space_constraint(weight, pltpu.HBM), *after)


def piece_dots(info_ref, w_ref, parts, starts, columns):
    total = None
    for part, start in zip(parts, starts):
        piece = w_ref.shape[1]
        for k in range(part.shape[0]):
            depth = pl.ds(pl.multiple_of(info_ref[2 + start + k] * piece, piece), piece)
            term = jnp.dot(part[k, :, :piece], w_ref[depth, columns], preferred_element_type=jnp.float32)
            total = term if total is None else total + term
    return total


def side_sum(parts, piece):
    return sum(part[k, :, piece:].astype(jnp.float32) for part in parts for k in range(part.shape[0]))


def own_kernel(starts, info_ref, *refs):
    *parts, w_ref, total_ref, side_ref = refs
    piece = w_ref.shape[1]
    side_ref[...] = side_sum(parts, piece)
    tile = min(piece, 256)
    for n in range(piece // tile):
        columns = slice(n * tile, (n + 1) * tile)
        total_ref[:, columns] = piece_dots(info_ref, w_ref, parts, starts, columns)


def layer_kernel(rank, owners, owned, tick, chunks, starts, extra, info_ref, *refs):
    *parts, w_ref, x_ref, up_ref, total_ref, side_ref, o_ref = refs
    piece = x_ref.shape[1]
    width = w_ref.shape[0]
    *parts, terms = [*parts[: len(parts) - extra], parts[len(parts) - extra :]]
    side = side_ref[...] + side_sum(parts, piece)
    if extra:
        side = side + side_sum(terms, 0)
    squares = side[:, rank : rank + 1] + side[:, rank + 1 : rank + 2]
    scale = lax.rsqrt(squares / width + 1e-05)
    inner = (2.0 * side[:, :rank]).astype(jnp.bfloat16)
    rows_of = [adapter_at(info_ref, owners, owned, tick, chunks, b) for b in range(SPAN)]
    tile = min(piece, 256)
    for n in range(piece // tile):
        columns = slice(n * tile, (n + 1) * tile)
        delta = [
            jnp.dot(
                inner[b * BLOCK : (b + 1) * BLOCK], up_ref[row, :, columns], preferred_element_type=jnp.float32
            )
            for b, row in enumerate(rows_of)
        ]
        total = jnp.concatenate(delta, axis=0) if SPAN > 1 else delta[0]
        total += total_ref[:, columns] + piece_dots(info_ref, w_ref, parts, starts, columns)
        h = x_ref[:, columns].astype(jnp.float32)
        o_ref[:, columns] = (h + scale * total).astype(jnp.bfloat16)


def join_kernel(info_ref, *refs):
    *blocks, o_ref = refs
    rows = blocks[0].shape[0]
    for i, block in enumerate(blocks):
        o_ref[i * rows : (i + 1) * rows, :] = block[...]


def home_kernel(sections, counts, info_ref, *refs):
    *blocks, o_ref = refs
    taken = 0
    for section, count in zip(range(sections), counts):
        own = blocks[taken : taken + count]
        taken += count

        @pl.when(info_ref[0] == section)
        def _():
            row = 0
            for block in own:
                span = block.shape[0]
                o_ref[row : row + span, :] = block[...]
                row += span


def reward_kernel(sections, counts, info_ref, *refs):
    *blocks, head_ref, score_ref = refs
    taken = 0
    for section, count in zip(range(sections), counts):
        own = blocks[taken : taken + count]
        taken += count

        @pl.when(info_ref[0] == section)
        def _():
            row = 0
            for block in own:
                span = block.shape[0]
                score_ref[:, row : row + span] = lax.dot_general(
                    head_ref[...], block[...], (((1,), (1,)), ((), ())), preferred_element_type=jnp.float32
                )
                row += span


def add_kernel(info_ref, *refs):
    *terms, o_ref = refs
    o_ref[...] = sum(term[...] for term in terms)


def score_kernel(info_ref, limits_ref, *refs):
    *terms, o_ref = refs
    total = sum(term[...] for term in terms)
    lane = lax.broadcasted_iota(jnp.int32, (1, BLOCK), 1)
    for b in range(total.shape[1] // BLOCK):
        columns = slice(b * BLOCK, (b + 1) * BLOCK)
        o_ref[:, columns] = jnp.where(lane < limits_ref[:, b : b + 1], total[:, columns], 0.0)


def cut(maps_ref, info_ref, place, out):
    piece = out.shape[-1]
    out[...] = maps_ref[:, :, pl.ds(pl.multiple_of((info_ref[1] ^ place) * piece, piece), piece)]


def cut_other_kernel(chips, info_ref, maps_ref, o_ref):
    for k in range(chips):
        cut(maps_ref, info_ref, 2 * k + 1, o_ref.at[k])


def cut_own_kernel(chips, info_ref, maps_ref, other_ref, *outs):
    for k, out in enumerate(outs):
        cut(maps_ref, info_ref, 2 * k, out.at[0])
        out[1] = other_ref[k]


def stack_kernel(info_ref, *refs):
    *blocks, o_ref = refs
    count, owned = blocks[0].shape[:2]
    for i, block in enumerate(blocks):
        for j in range(count):
            start = (i * count + j) * owned
            o_ref[start : start + owned] = block[j]


def shards(
    entering_hidden,
    section_weight,
    section_norm_gain,
    plugin_narrowing_factors,
    plugin_widening_factors,
    reward_head,
    adapter_of_block,
    live_block_rows,
):
    sections = lax.axis_size("section")
    section = lax.axis_index("section")
    chips = lax.axis_size("chip")
    cores = lax.axis_size("core")
    owners = chips * cores
    everyone = ("chip", "core")
    batches_here, rows, piece = entering_hidden.shape
    micro = batches_here * sections
    span = BLOCK * SPAN
    per_micro = rows // span
    owned = plugin_narrowing_factors.shape[1]
    rank = plugin_narrowing_factors.shape[3]
    chunks = micro * per_micro
    pairwise = chips == 4 and cores == 2

    chip, core = lax.axis_index("chip"), lax.axis_index("core")
    if pairwise:
        near_by, far = jnp.where(core == 0, 1, 2), jnp.where(core == 0, 2, 1)
        place = chip * cores + core
        parts = [(0, 0), (0, 1), (near_by, 0), (near_by, 1), (3, 0), (far, 1), (far, 0), (3, 1)]
        order = [(chip ^ there) * cores + (core ^ other) for there, other in parts]
    else:
        place = jnp.zeros_like(core)
        order = [i * cores + (core + k) % cores for k in range(cores) for i in range(chips)]
    info = jnp.concatenate([jnp.stack([section, place] + order), adapter_of_block.reshape(-1)])
    info = info.astype(jnp.int32)

    def over_cores(part):
        return [
            lax.ppermute(part, "core", [((c + k) % cores, c) for c in range(cores)]) for k in range(1, cores)
        ]

    def over_chips(part, steps):
        pairs = [(i * cores + c, (i ^ steps[c]) * cores + c) for i in range(chips) for c in range(cores)]
        return lax.ppermute(part, everyone, pairs)

    def spread(maps, after):
        if not pairwise:
            maps = jnp.moveaxis(maps.reshape(owned, rank, owners, piece), 2, 0)
            maps = lax.all_to_all(maps, everyone, split_axis=0, concat_axis=0, tiled=True)
            table = maps.reshape(owners * owned, rank, piece)
            return lambda after: table, after
        size = 2 * maps.size
        out_shape = pltpu.VMEM((chips, owned, rank, piece), maps.dtype)
        kernel = functools.partial(cut_other_kernel, chips)
        other = call(kernel, out_shape, (info, maps), "cut_other", 0, 0, after=after)
        (swapped,) = over_cores(other)
        out_shape = [pltpu.VMEM((cores, owned, rank, piece), maps.dtype) for _ in range(chips)]
        kernel = functools.partial(cut_own_kernel, chips)
        mine, *blocks = call(kernel, out_shape, (info, maps, swapped), "cut_own", 0, 0)
        blocks = [over_chips(block, (k, k)) for k, block in zip(range(1, chips), blocks)]
        out_shape = pltpu.VMEM((owners * owned, rank, piece), maps.dtype)
        return functools.partial(call, stack_kernel, out_shape, (info, mine, *blocks), "stack", 0, 0), [mine]

    feeds = []
    for m in range(micro):
        home, slot = divmod(m, batches_here)
        block = entering_hidden[slot]
        feeds.append(block if home == 0 else lax.ppermute(block, "section", [(home, 0)]))

    def gather_start(message):
        if not pairwise:
            parts = lax.all_to_all(message, "chip", split_axis=0, concat_axis=0, tiled=True)
            return [parts] + over_cores(parts)
        first = over_chips(message, (1, 2))
        (other,) = over_cores(message)
        second = over_chips(other, (1, 2))
        return [message, other, first, second]

    def gather_end(parts, after):
        if not pairwise:
            return [(part, chips * (1 + k)) for k, part in enumerate(parts[1:])]
        _, _, first, second = parts
        if after:
            first = tie(first, after)
        else:
            second = tie(second, [sums[0][1]])
        third = over_chips(first, (2, 1))
        late = [first, second, third] + [over_cores(part)[0] for part in (first, second, third)]
        return list(zip(late, range(2, 8)))

    def prep(tick, sources, blocks, after):
        out_shape = (
            pltpu.VMEM((span, piece), jnp.bfloat16),
            pltpu.VMEM((1 if pairwise else chips, span, piece + SIDE), jnp.bfloat16),
        )
        tabled = tick > 0 or not pairwise
        kernel = functools.partial(prep_kernel, rank, owners, owned, tick, chunks, blocks, tabled)
        args = (info, *sources, section_norm_gain) + ((down,) if tabled else ())
        return call(kernel, out_shape, args, "prep", 2 * span * piece * SIDE * bool(tick), span * piece * 8 * bool(tick), after=after)

    def own_layer(parts, after):
        width = piece * owners
        kernel = functools.partial(own_kernel, [start for _, start in parts])
        out_shape = (pltpu.VMEM((span, piece), jnp.float32), pltpu.VMEM((span, SIDE), jnp.float32))
        args = (info, *[part for part, _ in parts], weight)
        return call(kernel, out_shape, args, "own", span * width * piece // 2 * bool(after), width * piece // 2 * bool(after), after=after)

    def layer(tick, parts, x, sums, terms, after):
        width = piece * owners
        kernel = functools.partial(layer_kernel, rank, owners, owned, tick, chunks, [start for _, start in parts], len(terms))
        args = (info, *[part for part, _ in parts], *terms, weight, x, up, *sums)
        out_shape = pltpu.VMEM((span, piece), jnp.bfloat16)
        return call(kernel, out_shape, args, "layer", 2 * span * width * piece, 2 * width * piece, after=after)

    arrived, state, sums, done, home_blocks, returned = {}, {}, {}, {}, {}, {}
    postponed, early = [], {}
    ticks = chunks + LAG * (sections - 1)

    def active(tick):
        return [s for s in range(sections) if 0 <= tick - LAG * s < chunks]

    def begin(tick):
        sources, blocks = [], []
        if 0 in active(tick):
            m, b = divmod(tick, per_micro)
            sources.append(feeds[m])
            blocks.append(b)
        if active(tick) != [0]:
            sources.append(arrived.pop(tick))
            if tick in early:
                sources[-1] = tie(sources[-1], [])
            blocks.append(0)
        if tick == 0:
            after = []
        else:
            after = [sums[tick - 1][1]]
        if tick in early:
            after.append(early.pop(tick))
        x, message = prep(tick, sources, blocks, after)
        parts = gather_start(message)
        state[tick] = [x, message, parts, parts[1] if pairwise else None]

    def own_chip(tick, after):
        parts = state[tick][2]
        own = [(parts[0], 0), (parts[1], 1)] if pairwise else [(parts[0], 0)]
        sums[tick] = own_layer(own, after)
        state[tick][2] = gather_end(parts, [sums[tick][1]] if after else [])

    down_maps = jnp.swapaxes(plugin_narrowing_factors[0], 1, 2)
    down = None
    if not pairwise:
        down = spread(down_maps, ())[0](after=[])
    up, begun = spread(plugin_widening_factors[0], ())
    begin(0)
    if pairwise:
        down, also = spread(down_maps, begun)
        begun = begun + also
    weight = staged(section_weight[0], [*begun, state[0][1]])
    up = up(after=[weight])
    own_chip(0, [])
    terms = []
    if pairwise:
        down = down(after=[weight])
        parts = [(state[0][1], 0), (state[0][3], 1)] + state[0][2]
        kernel = functools.partial(owner_kernel, rank, owners, owned, [start for _, start in parts])
        out_shape = pltpu.VMEM((1, span, SIDE), jnp.bfloat16)
        args = (info, *[part for part, _ in parts], down_maps)
        side = call(kernel, out_shape, args, "owner", 2 * span * piece * owners * rank, 0)
        side = call(add_kernel, out_shape, (info, side, *over_cores(side)), "add", 0, 0)
        for k in (1, 2):
            side = call(add_kernel, out_shape, (info, side, over_chips(side, (k, k))), "add", 0, 0)
        terms = [side]
    for tick in range(ticks):
        after = []
        if tick + 1 < ticks:
            begin(tick + 1)
            after.append(state[tick + 1][1])
        if tick in returned:
            after.append(returned.pop(tick))
        x, _, parts, _ = state.pop(tick)
        if pairwise:
            size = piece * piece * owners
            x = tie(x, [part for part, _ in parts[3:5]] + after, span * size, size)
        h = layer(tick, parts, x, sums[tick], terms if tick == 0 else [], after)
        if tick + 1 < ticks:
            own_chip(tick + 1, [h])
        for m, block in postponed:
            block = lax.ppermute(tie(block, [h]), "section", [(sections - 1, m // batches_here)])
            home_blocks.setdefault(m, []).append(block)
            returned[tick + 1] = block
        postponed = []
        onward = [(s, s + 1) for s in active(tick) if s + 1 < sections]
        if onward:
            arrived[tick + LAG] = lax.ppermute(h, "section", onward)
        if sections - 1 in active(tick):
            last = tick - LAG * (sections - 1)
            m = last // per_micro
            home = m // batches_here
            done[last] = h
            if home == sections - 1:
                home_blocks.setdefault(m, []).append(h)
            elif (m + 1) * per_micro + LAG * (sections - 1) + 2 < ticks:
                if last % per_micro == per_micro - 1:
                    block = [done[m * per_micro + b] for b in range(per_micro)]
                    if per_micro > 1:
                        out_shape = pltpu.VMEM((rows, piece), jnp.bfloat16)
                        block = [call(join_kernel, out_shape, (info, *block), "join", 0, rows * piece * 4)]
                    home_blocks[m] = [lax.ppermute(block[0], "section", [(sections - 1, home)])]
                    returned[tick + 1] = home_blocks[m][0]
            elif tick + 2 < ticks - 1:
                early[tick + 2] = lax.ppermute(h, "section", [(sections - 1, home)])
                home_blocks.setdefault(m, []).append(early[tick + 2])
            else:
                postponed.append((m, h))

    for m, block in postponed:
        block = lax.ppermute(block, "section", [(sections - 1, m // batches_here)])
        home_blocks.setdefault(m, []).append(block)
    hidden, scores = [], []
    for slot in range(batches_here):
        blocks = [home_blocks[home * batches_here + slot] for home in range(sections)]
        counts = [len(block) for block in blocks]
        parts = [part for block in blocks for part in block]
        out_shape = pltpu.VMEM((1, rows), jnp.float32)
        kernel = functools.partial(reward_kernel, sections, counts)
        score = call(kernel, out_shape, (info, *parts, reward_head[None]), "reward", 0, 0)
        out_shape = jax.ShapeDtypeStruct((rows, piece), jnp.bfloat16)
        kernel = functools.partial(home_kernel, sections, counts)
        hidden.append(call(kernel, out_shape, (info, *parts), "home", 2 * rows * piece, rows * piece * 4, after=[score]))
        near_by = pltpu.VMEM((1, rows), jnp.float32)
        if pairwise:
            score = call(add_kernel, near_by, (info, score, *over_cores(score)), "add", 0, rows * 4)
            terms = [score] + [over_chips(score, (k, k)) for k in (1, 2, 3)]
        else:
            terms = [lax.psum(score, everyone)]
        limits = live_block_rows[slot : slot + 1]
        out_shape = jax.ShapeDtypeStruct((1, rows), jnp.float32)
        scores.append(call(score_kernel, out_shape, (info, limits, *terms), "score", 0, rows * 4))
    if batches_here == 1:
        return (hidden[0][None], scores[0])
    return (jnp.stack(hidden), jnp.concatenate(scores, axis=0))


def solution(mesh):
    sections, owners = mesh.shape["section"], mesh.shape["mp"]
    cores = 2 if owners % 2 == 0 else 1
    fine = jax.sharding.Mesh(
        mesh.devices.reshape(sections, owners // cores, cores), ("section", "chip", "core")
    )
    mp = ("chip", "core")
    placed = (
        P("section", None, mp),
        P("section", None, mp),
        P("section", mp),
        P("section", mp, None, None),
        P("section", mp, None, None),
        P(mp),
        P(),
        P("section", None),
    )
    return jax.shard_map(
        shards,
        mesh=fine,
        in_specs=placed,
        out_specs=(P("section", None, mp), P("section", None)),
        check_vma=False,
    )
```

```python
import functools

import jax
import jax.numpy as jnp
from jax import lax
from jax.experimental import pallas as pl
from jax.experimental.pallas import tpu as pltpu
from jax.sharding import PartitionSpec as P

BLOCK = 128
SIDE = 128
LAG = 2
SPAN = 1

VMEM = pl.BlockSpec(memory_space=pltpu.VMEM)
SMEM = pl.BlockSpec(memory_space=pltpu.SMEM)


def near(x):
    return pltpu.with_memory_space_constraint(x, pltpu.VMEM)


def call(kernel, out_shape, args, name, flops, moved, limit=8, after=()):
    info, *arrays = args
    count = len(arrays)

    def body(info_ref, *refs):
        kernel(info_ref, *refs[:count], *refs[count + len(after) :])

    return pl.pallas_call(
        body,
        out_shape=out_shape,
        in_specs=[SMEM] + [VMEM] * count + [pl.BlockSpec(memory_space=pl.ANY)] * len(after),
        out_specs=jax.tree.map(lambda _: VMEM, out_shape),
        compiler_params=pltpu.CompilerParams(vmem_limit_bytes=limit << 20),
        cost_estimate=pl.CostEstimate(flops=flops, bytes_accessed=moved, transcendentals=0),
        name=name,
    )(info, *map(near, arrays), *after)


def tie(x, after, flops=0, moved=0):
    def body(*_):
        pass

    return pl.pallas_call(
        body,
        out_shape=pltpu.VMEM(x.shape, x.dtype),
        in_specs=[VMEM] + [pl.BlockSpec(memory_space=pl.ANY)] * len(after),
        out_specs=VMEM,
        input_output_aliases={0: 0},
        compiler_params=pltpu.CompilerParams(vmem_limit_bytes=1 << 20),
        cost_estimate=pl.CostEstimate(flops=flops, bytes_accessed=moved, transcendentals=0),
        name="tie",
    )(near(x), *after)


def adapter_at(info_ref, owners, owned, tick, chunks, block):
    mine = jnp.clip(tick - LAG * info_ref[0], 0, chunks - 1)
    adapter = info_ref[2 + owners + mine * SPAN + block]
    if owned == 1:
        return adapter ^ info_ref[1]
    return (lax.div(adapter, owned) ^ info_ref[1]) * owned + lax.rem(adapter, owned)


def prep_kernel(rank, owners, owned, tick, chunks, block, tabled, info_ref, *refs):
    *sources, gain_ref, x_ref, m_ref = refs
    if tabled:
        *sources, gain_ref, down_ref = sources + [gain_ref]
    copies = m_ref.shape[0]
    rows, piece = x_ref.shape
    picked = [source[b * rows : (b + 1) * rows, :].astype(jnp.float32) for source, b in zip(sources, block)]
    x = jnp.where(info_ref[0] == 0, *picked) if len(picked) == 2 else picked[0]
    x_ref[...] = x.astype(jnp.bfloat16)
    scaled = (x * gain_ref[...].astype(jnp.float32)).astype(jnp.bfloat16)
    squares = jnp.sum(x * x, axis=1, keepdims=True)
    high = squares.astype(jnp.bfloat16).astype(jnp.float32)
    low = squares - high
    lane = lax.broadcasted_iota(jnp.int32, (rows, SIDE), 1)
    inner = jnp.zeros((rows, SIDE), jnp.float32)
    if tabled:
        inner = []
        for b in range(SPAN):
            product = lax.dot_general(
                scaled[b * BLOCK : (b + 1) * BLOCK],
                down_ref[adapter_at(info_ref, owners, owned, tick, chunks, b)],
                (((1,), (1,)), ((), ())),
                preferred_element_type=jnp.float32,
            )
            inner.append(jnp.concatenate([product, jnp.zeros((BLOCK, SIDE - rank), jnp.float32)], axis=1))
        inner = jnp.concatenate(inner, axis=0) if SPAN > 1 else inner[0]
    side = jnp.where(lane == rank, high, jnp.where(lane == rank + 1, low, inner)).astype(jnp.bfloat16)
    for copy in range(copies):
        m_ref[copy, :, :piece] = scaled
        m_ref[copy, :, piece:] = side


def owner_kernel(rank, owners, owned, starts, info_ref, *refs):
    *parts, down_ref, o_ref = refs
    rows = o_ref.shape[1]
    piece = parts[0].shape[2] - SIDE
    sums = []
    for o in range(owned):
        total = None
        for part, start in zip(parts, starts):
            columns = pl.ds(pl.multiple_of(info_ref[2 + start] * piece, piece), piece)
            term = lax.dot_general(
                part[0, :, :piece], down_ref[o, :, columns], (((1,), (1,)), ((), ())), preferred_element_type=jnp.float32
            )
            total = term if total is None else total + term
        sums.append(total)
    for b in range(SPAN):
        adapter = info_ref[2 + owners + b]
        block = slice(b * BLOCK, (b + 1) * BLOCK)
        product = jnp.zeros((BLOCK, rank), jnp.float32)
        for o, total in enumerate(sums):
            product = jnp.where(adapter == info_ref[1] * owned + o, total[block], product)
        side = jnp.concatenate([product, jnp.zeros((BLOCK, SIDE - rank), jnp.float32)], axis=1)
        o_ref[0, block, :] = side.astype(jnp.bfloat16)


def stage_kernel(w_ref, *refs):
    *_, o_ref, sem = refs
    copy = pltpu.make_async_copy(w_ref, o_ref, sem)
    copy.start()
    copy.wait()


def staged(weight, after):
    return pl.pallas_call(
        stage_kernel,
        out_shape=pltpu.VMEM(weight.shape, weight.dtype),
        in_specs=[pl.BlockSpec(memory_space=pl.ANY)] * (1 + len(after)),
        out_specs=VMEM,
        scratch_shapes=[pltpu.SemaphoreType.DMA],
        compiler_params=pltpu.CompilerParams(vmem_limit_bytes=4 << 20),
        cost_estimate=pl.CostEstimate(flops=0, bytes_accessed=2 * weight.size, transcendentals=0),
        name="stage",
    )(pltpu.with_memory_space_constraint(weight, pltpu.HBM), *after)


def piece_dots(info_ref, w_ref, parts, starts, columns):
    total = None
    for part, start in zip(parts, starts):
        piece = w_ref.shape[1]
        for k in range(part.shape[0]):
            depth = pl.ds(pl.multiple_of(info_ref[2 + start + k] * piece, piece), piece)
            term = jnp.dot(part[k, :, :piece], w_ref[depth, columns], preferred_element_type=jnp.float32)
            total = term if total is None else total + term
    return total


def side_sum(parts, piece):
    return sum(part[k, :, piece:].astype(jnp.float32) for part in parts for k in range(part.shape[0]))


def own_kernel(starts, info_ref, *refs):
    *parts, w_ref, total_ref, side_ref = refs
    piece = w_ref.shape[1]
    side_ref[...] = side_sum(parts, piece)
    tile = min(piece, 256)
    for n in range(piece // tile):
        columns = slice(n * tile, (n + 1) * tile)
        total_ref[:, columns] = piece_dots(info_ref, w_ref, parts, starts, columns)


def layer_kernel(rank, owners, owned, tick, chunks, starts, extra, info_ref, *refs):
    *parts, w_ref, x_ref, up_ref, total_ref, side_ref, o_ref = refs
    piece = x_ref.shape[1]
    width = w_ref.shape[0]
    *parts, terms = [*parts[: len(parts) - extra], parts[len(parts) - extra :]]
    side = side_ref[...] + side_sum(parts, piece)
    if extra:
        side = side + side_sum(terms, 0)
    squares = side[:, rank : rank + 1] + side[:, rank + 1 : rank + 2]
    scale = lax.rsqrt(squares / width + 1e-05)
    inner = (2.0 * side[:, :rank]).astype(jnp.bfloat16)
    rows_of = [adapter_at(info_ref, owners, owned, tick, chunks, b) for b in range(SPAN)]
    tile = min(piece, 256)
    for n in range(piece // tile):
        columns = slice(n * tile, (n + 1) * tile)
        delta = [
            jnp.dot(
                inner[b * BLOCK : (b + 1) * BLOCK], up_ref[row, :, columns], preferred_element_type=jnp.float32
            )
            for b, row in enumerate(rows_of)
        ]
        total = jnp.concatenate(delta, axis=0) if SPAN > 1 else delta[0]
        total += total_ref[:, columns] + piece_dots(info_ref, w_ref, parts, starts, columns)
        h = x_ref[:, columns].astype(jnp.float32)
        o_ref[:, columns] = (h + scale * total).astype(jnp.bfloat16)


def join_kernel(info_ref, *refs):
    *blocks, o_ref = refs
    rows = blocks[0].shape[0]
    for i, block in enumerate(blocks):
        o_ref[i * rows : (i + 1) * rows, :] = block[...]


def home_kernel(sections, counts, info_ref, *refs):
    *blocks, o_ref = refs
    taken = 0
    for section, count in zip(range(sections), counts):
        own = blocks[taken : taken + count]
        taken += count

        @pl.when(info_ref[0] == section)
        def _():
            row = 0
            for block in own:
                span = block.shape[0]
                o_ref[row : row + span, :] = block[...]
                row += span


def reward_kernel(sections, counts, info_ref, *refs):
    *blocks, head_ref, score_ref = refs
    taken = 0
    for section, count in zip(range(sections), counts):
        own = blocks[taken : taken + count]
        taken += count

        @pl.when(info_ref[0] == section)
        def _():
            row = 0
            for block in own:
                span = block.shape[0]
                score_ref[:, row : row + span] = lax.dot_general(
                    head_ref[...], block[...], (((1,), (1,)), ((), ())), preferred_element_type=jnp.float32
                )
                row += span


def add_kernel(info_ref, *refs):
    *terms, o_ref = refs
    o_ref[...] = sum(term[...] for term in terms)


def score_kernel(info_ref, limits_ref, *refs):
    *terms, o_ref = refs
    total = sum(term[...] for term in terms)
    lane = lax.broadcasted_iota(jnp.int32, (1, BLOCK), 1)
    for b in range(total.shape[1] // BLOCK):
        columns = slice(b * BLOCK, (b + 1) * BLOCK)
        o_ref[:, columns] = jnp.where(lane < limits_ref[:, b : b + 1], total[:, columns], 0.0)


def cut(maps_ref, info_ref, place, out):
    piece = out.shape[-1]
    out[...] = maps_ref[:, :, pl.ds(pl.multiple_of((info_ref[1] ^ place) * piece, piece), piece)]


def cut_other_kernel(chips, info_ref, maps_ref, o_ref):
    for k in range(chips):
        cut(maps_ref, info_ref, 2 * k + 1, o_ref.at[k])


def cut_own_kernel(chips, info_ref, maps_ref, other_ref, *outs):
    for k, out in enumerate(outs):
        cut(maps_ref, info_ref, 2 * k, out.at[0])
        out[1] = other_ref[k]


def stack_kernel(info_ref, *refs):
    *blocks, o_ref = refs
    count, owned = blocks[0].shape[:2]
    for i, block in enumerate(blocks):
        for j in range(count):
            start = (i * count + j) * owned
            o_ref[start : start + owned] = block[j]


def shards(
    entering_hidden,
    section_weight,
    section_norm_gain,
    plugin_narrowing_factors,
    plugin_widening_factors,
    reward_head,
    adapter_of_block,
    live_block_rows,
):
    sections = lax.axis_size("section")
    section = lax.axis_index("section")
    chips = lax.axis_size("chip")
    cores = lax.axis_size("core")
    owners = chips * cores
    everyone = ("chip", "core")
    batches_here, rows, piece = entering_hidden.shape
    micro = batches_here * sections
    span = BLOCK * SPAN
    per_micro = rows // span
    owned = plugin_narrowing_factors.shape[1]
    rank = plugin_narrowing_factors.shape[3]
    chunks = micro * per_micro
    pairwise = chips == 4 and cores == 2

    chip, core = lax.axis_index("chip"), lax.axis_index("core")
    if pairwise:
        near_by, far = jnp.where(core == 0, 1, 2), jnp.where(core == 0, 2, 1)
        place = chip * cores + core
        parts = [(0, 0), (0, 1), (near_by, 0), (near_by, 1), (3, 0), (far, 1), (far, 0), (3, 1)]
        order = [(chip ^ there) * cores + (core ^ other) for there, other in parts]
    else:
        place = jnp.zeros_like(core)
        order = [i * cores + (core + k) % cores for k in range(cores) for i in range(chips)]
    info = jnp.concatenate([jnp.stack([section, place] + order), adapter_of_block.reshape(-1)])
    info = info.astype(jnp.int32)

    def over_cores(part):
        return [
            lax.ppermute(part, "core", [((c + k) % cores, c) for c in range(cores)]) for k in range(1, cores)
        ]

    def over_chips(part, steps):
        pairs = [(i * cores + c, (i ^ steps[c]) * cores + c) for i in range(chips) for c in range(cores)]
        return lax.ppermute(part, everyone, pairs)

    def spread(maps, after):
        if not pairwise:
            maps = jnp.moveaxis(maps.reshape(owned, rank, owners, piece), 2, 0)
            maps = lax.all_to_all(maps, everyone, split_axis=0, concat_axis=0, tiled=True)
            table = maps.reshape(owners * owned, rank, piece)
            return lambda after: table, after
        size = 2 * maps.size
        out_shape = pltpu.VMEM((chips, owned, rank, piece), maps.dtype)
        kernel = functools.partial(cut_other_kernel, chips)
        other = call(kernel, out_shape, (info, maps), "cut_other", 0, 0, after=after)
        (swapped,) = over_cores(other)
        out_shape = [pltpu.VMEM((cores, owned, rank, piece), maps.dtype) for _ in range(chips)]
        kernel = functools.partial(cut_own_kernel, chips)
        mine, *blocks = call(kernel, out_shape, (info, maps, swapped), "cut_own", 0, 0)
        blocks = [over_chips(block, (k, k)) for k, block in zip(range(1, chips), blocks)]
        out_shape = pltpu.VMEM((owners * owned, rank, piece), maps.dtype)
        return functools.partial(call, stack_kernel, out_shape, (info, mine, *blocks), "stack", 0, 0), [mine]

    feeds = []
    for m in range(micro):
        home, slot = divmod(m, batches_here)
        block = entering_hidden[slot]
        feeds.append(block if home == 0 else lax.ppermute(block, "section", [(home, 0)]))

    def gather_start(message):
        if not pairwise:
            parts = lax.all_to_all(message, "chip", split_axis=0, concat_axis=0, tiled=True)
            return [parts] + over_cores(parts)
        first = over_chips(message, (1, 2))
        (other,) = over_cores(message)
        second = over_chips(other, (1, 2))
        return [message, other, first, second]

    def gather_end(parts, after):
        if not pairwise:
            return [(part, chips * (1 + k)) for k, part in enumerate(parts[1:])]
        _, _, first, second = parts
        if after:
            first = tie(first, after)
        else:
            second = tie(second, [sums[0][1]])
        third = over_chips(first, (2, 1))
        late = [first, second, third] + [over_cores(part)[0] for part in (first, second, third)]
        return list(zip(late, range(2, 8)))

    def prep(tick, sources, blocks, after):
        out_shape = (
            pltpu.VMEM((span, piece), jnp.bfloat16),
            pltpu.VMEM((1 if pairwise else chips, span, piece + SIDE), jnp.bfloat16),
        )
        tabled = tick > 0 or not pairwise
        kernel = functools.partial(prep_kernel, rank, owners, owned, tick, chunks, blocks, tabled)
        args = (info, *sources, section_norm_gain) + ((down,) if tabled else ())
        return call(kernel, out_shape, args, "prep", 2 * span * piece * SIDE * bool(tick), span * piece * 8 * bool(tick), after=after)

    def own_layer(parts, after):
        width = piece * owners
        kernel = functools.partial(own_kernel, [start for _, start in parts])
        out_shape = (pltpu.VMEM((span, piece), jnp.float32), pltpu.VMEM((span, SIDE), jnp.float32))
        args = (info, *[part for part, _ in parts], weight)
        return call(kernel, out_shape, args, "own", span * width * piece // 2 * bool(after), width * piece // 2 * bool(after), after=after)

    def layer(tick, parts, x, sums, terms, after):
        width = piece * owners
        kernel = functools.partial(layer_kernel, rank, owners, owned, tick, chunks, [start for _, start in parts], len(terms))
        args = (info, *[part for part, _ in parts], *terms, weight, x, up, *sums)
        out_shape = pltpu.VMEM((span, piece), jnp.bfloat16)
        return call(kernel, out_shape, args, "layer", 2 * span * width * piece, 2 * width * piece, after=after)

    arrived, state, sums, done, home_blocks, returned = {}, {}, {}, {}, {}, {}
    ticks = chunks + LAG * (sections - 1)

    def active(tick):
        return [s for s in range(sections) if 0 <= tick - LAG * s < chunks]

    def begin(tick):
        sources, blocks = [], []
        if 0 in active(tick):
            m, b = divmod(tick, per_micro)
            sources.append(feeds[m])
            blocks.append(b)
        if active(tick) != [0]:
            sources.append(arrived.pop(tick))
            blocks.append(0)
        if tick == 0:
            after = []
        else:
            after = [sums[tick - 1][1]]
        x, message = prep(tick, sources, blocks, after)
        parts = gather_start(message)
        state[tick] = [x, message, parts, parts[1] if pairwise else None]

    def own_chip(tick, after):
        parts = state[tick][2]
        own = [(parts[0], 0), (parts[1], 1)] if pairwise else [(parts[0], 0)]
        sums[tick] = own_layer(own, after)
        state[tick][2] = gather_end(parts, [sums[tick][1]] if after else [])

    down_maps = jnp.swapaxes(plugin_narrowing_factors[0], 1, 2)
    down = None
    if not pairwise:
        down = spread(down_maps, ())[0](after=[])
    up, begun = spread(plugin_widening_factors[0], ())
    begin(0)
    if pairwise:
        down, also = spread(down_maps, begun)
        begun = begun + also
    weight = staged(section_weight[0], [*begun, state[0][1]])
    own_chip(0, [])
    terms = []
    if pairwise:
        down = down(after=[weight])
        parts = [(state[0][1], 0), (state[0][3], 1)] + state[0][2]
        kernel = functools.partial(owner_kernel, rank, owners, owned, [start for _, start in parts])
        out_shape = pltpu.VMEM((1, span, SIDE), jnp.bfloat16)
        args = (info, *[part for part, _ in parts], down_maps)
        side = call(kernel, out_shape, args, "owner", 2 * span * piece * owners * rank, 0)
        side = call(add_kernel, out_shape, (info, side, *over_cores(side)), "add", 0, 0)
        for k in (1, 2):
            side = call(add_kernel, out_shape, (info, side, over_chips(side, (k, k))), "add", 0, 0)
        terms = [side]
    up = up(after=[weight, *terms])
    for tick in range(ticks):
        after = []
        if tick + 1 < ticks:
            begin(tick + 1)
            after.append(state[tick + 1][1])
        if tick in returned:
            after.append(returned.pop(tick))
        x, _, parts, _ = state.pop(tick)
        if pairwise:
            size = piece * piece * owners
            x = tie(x, [part for part, _ in parts[3:5]] + after, span * size, size)
        h = layer(tick, parts, x, sums[tick], terms if tick == 0 else [], after)
        if tick + 1 < ticks:
            own_chip(tick + 1, [h])
        onward = [(s, s + 1) for s in active(tick) if s + 1 < sections]
        if onward:
            arrived[tick + LAG] = lax.ppermute(h, "section", onward)
        if sections - 1 in active(tick):
            last = tick - LAG * (sections - 1)
            m = last // per_micro
            home = m // batches_here
            done[last] = h
            if last % per_micro == per_micro - 1:
                block = [done[m * per_micro + b] for b in range(per_micro)]
                if home != sections - 1:
                    if per_micro > 1:
                        out_shape = pltpu.VMEM((rows, piece), jnp.bfloat16)
                        block = [call(join_kernel, out_shape, (info, *block), "join", 0, rows * piece * 4)]
                    block = [lax.ppermute(block[0], "section", [(sections - 1, home)])]
                    if tick + 2 < ticks:
                        returned[tick + 2] = block[0]
                home_blocks[m] = block

    hidden, scores = [], []
    for slot in range(batches_here):
        blocks = [home_blocks[home * batches_here + slot] for home in range(sections)]
        counts = [len(block) for block in blocks]
        parts = [part for block in blocks for part in block]
        out_shape = pltpu.VMEM((1, rows), jnp.float32)
        kernel = functools.partial(reward_kernel, sections, counts)
        score = call(kernel, out_shape, (info, *parts, reward_head[None]), "reward", 0, 0)
        out_shape = jax.ShapeDtypeStruct((rows, piece), jnp.bfloat16)
        kernel = functools.partial(home_kernel, sections, counts)
        hidden.append(call(kernel, out_shape, (info, *parts), "home", 2 * rows * piece, rows * piece * 4, after=[score]))
        near_by = pltpu.VMEM((1, rows), jnp.float32)
        if pairwise:
            score = call(add_kernel, near_by, (info, score, *over_cores(score)), "add", 0, rows * 4)
            terms = [score] + [over_chips(score, (k, k)) for k in (1, 2, 3)]
        else:
            terms = [lax.psum(score, everyone)]
        limits = live_block_rows[slot : slot + 1]
        out_shape = jax.ShapeDtypeStruct((1, rows), jnp.float32)
        scores.append(call(score_kernel, out_shape, (info, limits, *terms), "score", 0, rows * 4))
    if batches_here == 1:
        return (hidden[0][None], scores[0])
    return (jnp.stack(hidden), jnp.concatenate(scores, axis=0))


def solution(mesh):
    sections, owners = mesh.shape["section"], mesh.shape["mp"]
    cores = 2 if owners % 2 == 0 else 1
    fine = jax.sharding.Mesh(
        mesh.devices.reshape(sections, owners // cores, cores), ("section", "chip", "core")
    )
    mp = ("chip", "core")
    placed = (
        P("section", None, mp),
        P("section", None, mp),
        P("section", mp),
        P("section", mp, None, None),
        P("section", mp, None, None),
        P(mp),
        P(),
        P("section", None),
    )
    return jax.shard_map(
        shards,
        mesh=fine,
        in_specs=placed,
        out_specs=(P("section", None, mp), P("section", None)),
        check_vma=False,
    )
```

```python
import functools

import jax
import jax.numpy as jnp
from jax import lax
from jax.experimental import pallas as pl
from jax.experimental.pallas import tpu as pltpu
from jax.sharding import PartitionSpec as P

BLOCK = 128
SIDE = 128
LAG = 2
SPAN = 1

VMEM = pl.BlockSpec(memory_space=pltpu.VMEM)
SMEM = pl.BlockSpec(memory_space=pltpu.SMEM)


def near(x):
    return pltpu.with_memory_space_constraint(x, pltpu.VMEM)


def call(kernel, out_shape, args, name, flops, moved, limit=8, after=()):
    info, *arrays = args
    count = len(arrays)

    def body(info_ref, *refs):
        kernel(info_ref, *refs[:count], *refs[count + len(after) :])

    return pl.pallas_call(
        body,
        out_shape=out_shape,
        in_specs=[SMEM] + [VMEM] * count + [pl.BlockSpec(memory_space=pl.ANY)] * len(after),
        out_specs=jax.tree.map(lambda _: VMEM, out_shape),
        compiler_params=pltpu.CompilerParams(vmem_limit_bytes=limit << 20),
        cost_estimate=pl.CostEstimate(flops=flops, bytes_accessed=moved, transcendentals=0),
        name=name,
    )(info, *map(near, arrays), *after)


def tie(x, after, flops=0, moved=0):
    def body(*_):
        pass

    return pl.pallas_call(
        body,
        out_shape=pltpu.VMEM(x.shape, x.dtype),
        in_specs=[VMEM] + [pl.BlockSpec(memory_space=pl.ANY)] * len(after),
        out_specs=VMEM,
        input_output_aliases={0: 0},
        compiler_params=pltpu.CompilerParams(vmem_limit_bytes=1 << 20),
        cost_estimate=pl.CostEstimate(flops=flops, bytes_accessed=moved, transcendentals=0),
        name="tie",
    )(near(x), *after)


def adapter_at(info_ref, owners, owned, tick, chunks, block):
    mine = jnp.clip(tick - LAG * info_ref[0], 0, chunks - 1)
    adapter = info_ref[2 + owners + mine * SPAN + block]
    if owned == 1:
        return adapter ^ info_ref[1]
    return (lax.div(adapter, owned) ^ info_ref[1]) * owned + lax.rem(adapter, owned)


def prep_kernel(rank, owners, owned, tick, chunks, block, tabled, info_ref, *refs):
    *sources, gain_ref, x_ref, m_ref = refs
    if tabled:
        *sources, gain_ref, down_ref = sources + [gain_ref]
    copies = m_ref.shape[0]
    rows, piece = x_ref.shape
    picked = [source[b * rows : (b + 1) * rows, :].astype(jnp.float32) for source, b in zip(sources, block)]
    x = jnp.where(info_ref[0] == 0, *picked) if len(picked) == 2 else picked[0]
    x_ref[...] = x.astype(jnp.bfloat16)
    scaled = (x * gain_ref[...].astype(jnp.float32)).astype(jnp.bfloat16)
    squares = jnp.sum(x * x, axis=1, keepdims=True)
    high = squares.astype(jnp.bfloat16).astype(jnp.float32)
    low = squares - high
    lane = lax.broadcasted_iota(jnp.int32, (rows, SIDE), 1)
    inner = jnp.zeros((rows, SIDE), jnp.float32)
    if tabled:
        inner = []
        for b in range(SPAN):
            product = lax.dot_general(
                scaled[b * BLOCK : (b + 1) * BLOCK],
                down_ref[adapter_at(info_ref, owners, owned, tick, chunks, b)],
                (((1,), (1,)), ((), ())),
                preferred_element_type=jnp.float32,
            )
            inner.append(jnp.concatenate([product, jnp.zeros((BLOCK, SIDE - rank), jnp.float32)], axis=1))
        inner = jnp.concatenate(inner, axis=0) if SPAN > 1 else inner[0]
    side = jnp.where(lane == rank, high, jnp.where(lane == rank + 1, low, inner)).astype(jnp.bfloat16)
    for copy in range(copies):
        m_ref[copy, :, :piece] = scaled
        m_ref[copy, :, piece:] = side


def owner_kernel(rank, owners, owned, starts, info_ref, *refs):
    *parts, down_ref, o_ref = refs
    rows = o_ref.shape[1]
    piece = parts[0].shape[2] - SIDE
    sums = []
    for o in range(owned):
        total = None
        for part, start in zip(parts, starts):
            columns = pl.ds(pl.multiple_of(info_ref[2 + start] * piece, piece), piece)
            term = lax.dot_general(
                part[0, :, :piece], down_ref[o, :, columns], (((1,), (1,)), ((), ())), preferred_element_type=jnp.float32
            )
            total = term if total is None else total + term
        sums.append(total)
    for b in range(SPAN):
        adapter = info_ref[2 + owners + b]
        block = slice(b * BLOCK, (b + 1) * BLOCK)
        product = jnp.zeros((BLOCK, rank), jnp.float32)
        for o, total in enumerate(sums):
            product = jnp.where(adapter == info_ref[1] * owned + o, total[block], product)
        side = jnp.concatenate([product, jnp.zeros((BLOCK, SIDE - rank), jnp.float32)], axis=1)
        o_ref[0, block, :] = side.astype(jnp.bfloat16)


def stage_kernel(w_ref, *refs):
    *_, o_ref, sem = refs
    copy = pltpu.make_async_copy(w_ref, o_ref, sem)
    copy.start()
    copy.wait()


def staged(weight, after):
    return pl.pallas_call(
        stage_kernel,
        out_shape=pltpu.VMEM(weight.shape, weight.dtype),
        in_specs=[pl.BlockSpec(memory_space=pl.ANY)] * (1 + len(after)),
        out_specs=VMEM,
        scratch_shapes=[pltpu.SemaphoreType.DMA],
        compiler_params=pltpu.CompilerParams(vmem_limit_bytes=4 << 20),
        cost_estimate=pl.CostEstimate(flops=0, bytes_accessed=2 * weight.size, transcendentals=0),
        name="stage",
    )(pltpu.with_memory_space_constraint(weight, pltpu.HBM), *after)


def piece_dots(info_ref, w_ref, parts, starts, columns):
    total = None
    for part, start in zip(parts, starts):
        piece = w_ref.shape[1]
        for k in range(part.shape[0]):
            depth = pl.ds(pl.multiple_of(info_ref[2 + start + k] * piece, piece), piece)
            term = jnp.dot(part[k, :, :piece], w_ref[depth, columns], preferred_element_type=jnp.float32)
            total = term if total is None else total + term
    return total


def side_sum(parts, piece):
    return sum(part[k, :, piece:].astype(jnp.float32) for part in parts for k in range(part.shape[0]))


def own_kernel(starts, info_ref, *refs):
    *parts, w_ref, total_ref, side_ref = refs
    piece = w_ref.shape[1]
    side_ref[...] = side_sum(parts, piece)
    tile = min(piece, 256)
    for n in range(piece // tile):
        columns = slice(n * tile, (n + 1) * tile)
        total_ref[:, columns] = piece_dots(info_ref, w_ref, parts, starts, columns)


def more_kernel(starts, info_ref, *refs):
    *parts, old_total, old_side, w_ref, total_ref, side_ref = refs
    piece = w_ref.shape[1]
    side_ref[...] = old_side[...] + side_sum(parts, piece)
    tile = min(piece, 256)
    for n in range(piece // tile):
        columns = slice(n * tile, (n + 1) * tile)
        total_ref[:, columns] = old_total[:, columns] + piece_dots(info_ref, w_ref, parts, starts, columns)


def layer_kernel(rank, owners, owned, tick, chunks, starts, extra, info_ref, *refs):
    *parts, w_ref, x_ref, up_ref, total_ref, side_ref, o_ref = refs
    piece = x_ref.shape[1]
    width = w_ref.shape[0]
    *parts, terms = [*parts[: len(parts) - extra], parts[len(parts) - extra :]]
    side = side_ref[...] + side_sum(parts, piece)
    if extra:
        side = side + side_sum(terms, 0)
    squares = side[:, rank : rank + 1] + side[:, rank + 1 : rank + 2]
    scale = lax.rsqrt(squares / width + 1e-05)
    inner = (2.0 * side[:, :rank]).astype(jnp.bfloat16)
    rows_of = [adapter_at(info_ref, owners, owned, tick, chunks, b) for b in range(SPAN)]
    tile = min(piece, 256)
    for n in range(piece // tile):
        columns = slice(n * tile, (n + 1) * tile)
        delta = [
            jnp.dot(
                inner[b * BLOCK : (b + 1) * BLOCK], up_ref[row, :, columns], preferred_element_type=jnp.float32
            )
            for b, row in enumerate(rows_of)
        ]
        total = jnp.concatenate(delta, axis=0) if SPAN > 1 else delta[0]
        total += total_ref[:, columns] + piece_dots(info_ref, w_ref, parts, starts, columns)
        h = x_ref[:, columns].astype(jnp.float32)
        o_ref[:, columns] = (h + scale * total).astype(jnp.bfloat16)


def join_kernel(info_ref, *refs):
    *blocks, o_ref = refs
    rows = blocks[0].shape[0]
    for i, block in enumerate(blocks):
        o_ref[i * rows : (i + 1) * rows, :] = block[...]


def home_kernel(sections, counts, info_ref, *refs):
    *blocks, o_ref = refs
    taken = 0
    for section, count in zip(range(sections), counts):
        own = blocks[taken : taken + count]
        taken += count

        @pl.when(info_ref[0] == section)
        def _():
            row = 0
            for block in own:
                span = block.shape[0]
                o_ref[row : row + span, :] = block[...]
                row += span


def reward_kernel(sections, counts, info_ref, *refs):
    *blocks, head_ref, score_ref = refs
    taken = 0
    for section, count in zip(range(sections), counts):
        own = blocks[taken : taken + count]
        taken += count

        @pl.when(info_ref[0] == section)
        def _():
            row = 0
            for block in own:
                span = block.shape[0]
                score_ref[:, row : row + span] = lax.dot_general(
                    head_ref[...], block[...], (((1,), (1,)), ((), ())), preferred_element_type=jnp.float32
                )
                row += span


def add_kernel(info_ref, *refs):
    *terms, o_ref = refs
    o_ref[...] = sum(term[...] for term in terms)


def score_kernel(info_ref, limits_ref, *refs):
    *terms, o_ref = refs
    total = sum(term[...] for term in terms)
    lane = lax.broadcasted_iota(jnp.int32, (1, BLOCK), 1)
    for b in range(total.shape[1] // BLOCK):
        columns = slice(b * BLOCK, (b + 1) * BLOCK)
        o_ref[:, columns] = jnp.where(lane < limits_ref[:, b : b + 1], total[:, columns], 0.0)


def cut(maps_ref, info_ref, place, out):
    piece = out.shape[-1]
    out[...] = maps_ref[:, :, pl.ds(pl.multiple_of((info_ref[1] ^ place) * piece, piece), piece)]


def cut_other_kernel(chips, info_ref, maps_ref, o_ref):
    for k in range(chips):
        cut(maps_ref, info_ref, 2 * k + 1, o_ref.at[k])


def cut_own_kernel(chips, info_ref, maps_ref, other_ref, *outs):
    for k, out in enumerate(outs):
        cut(maps_ref, info_ref, 2 * k, out.at[0])
        out[1] = other_ref[k]


def stack_kernel(info_ref, *refs):
    *blocks, o_ref = refs
    count, owned = blocks[0].shape[:2]
    for i, block in enumerate(blocks):
        for j in range(count):
            start = (i * count + j) * owned
            o_ref[start : start + owned] = block[j]


def shards(
    entering_hidden,
    section_weight,
    section_norm_gain,
    plugin_narrowing_factors,
    plugin_widening_factors,
    reward_head,
    adapter_of_block,
    live_block_rows,
):
    sections = lax.axis_size("section")
    section = lax.axis_index("section")
    chips = lax.axis_size("chip")
    cores = lax.axis_size("core")
    owners = chips * cores
    everyone = ("chip", "core")
    batches_here, rows, piece = entering_hidden.shape
    micro = batches_here * sections
    span = BLOCK * SPAN
    per_micro = rows // span
    owned = plugin_narrowing_factors.shape[1]
    rank = plugin_narrowing_factors.shape[3]
    chunks = micro * per_micro
    pairwise = chips == 4 and cores == 2

    chip, core = lax.axis_index("chip"), lax.axis_index("core")
    if pairwise:
        near_by, far = jnp.where(core == 0, 1, 2), jnp.where(core == 0, 2, 1)
        place = chip * cores + core
        parts = [(0, 0), (0, 1), (near_by, 0), (near_by, 1), (3, 0), (far, 1), (far, 0), (3, 1)]
        order = [(chip ^ there) * cores + (core ^ other) for there, other in parts]
    else:
        place = jnp.zeros_like(core)
        order = [i * cores + (core + k) % cores for k in range(cores) for i in range(chips)]
    info = jnp.concatenate([jnp.stack([section, place] + order), adapter_of_block.reshape(-1)])
    info = info.astype(jnp.int32)

    def over_cores(part):
        return [
            lax.ppermute(part, "core", [((c + k) % cores, c) for c in range(cores)]) for k in range(1, cores)
        ]

    def over_chips(part, steps):
        pairs = [(i * cores + c, (i ^ steps[c]) * cores + c) for i in range(chips) for c in range(cores)]
        return lax.ppermute(part, everyone, pairs)

    def spread(maps, after):
        if not pairwise:
            maps = jnp.moveaxis(maps.reshape(owned, rank, owners, piece), 2, 0)
            maps = lax.all_to_all(maps, everyone, split_axis=0, concat_axis=0, tiled=True)
            table = maps.reshape(owners * owned, rank, piece)
            return lambda after: table, after
        size = 2 * maps.size
        out_shape = pltpu.VMEM((chips, owned, rank, piece), maps.dtype)
        kernel = functools.partial(cut_other_kernel, chips)
        other = call(kernel, out_shape, (info, maps), "cut_other", 0, 0, after=after)
        (swapped,) = over_cores(other)
        out_shape = [pltpu.VMEM((cores, owned, rank, piece), maps.dtype) for _ in range(chips)]
        kernel = functools.partial(cut_own_kernel, chips)
        mine, *blocks = call(kernel, out_shape, (info, maps, swapped), "cut_own", 0, 0)
        blocks = [over_chips(block, (k, k)) for k, block in zip(range(1, chips), blocks)]
        out_shape = pltpu.VMEM((owners * owned, rank, piece), maps.dtype)
        return functools.partial(call, stack_kernel, out_shape, (info, mine, *blocks), "stack", 0, 0), [mine]

    feeds = []
    for m in range(micro):
        home, slot = divmod(m, batches_here)
        block = entering_hidden[slot]
        feeds.append(block if home == 0 else lax.ppermute(block, "section", [(home, 0)]))

    def gather_start(message):
        if not pairwise:
            parts = lax.all_to_all(message, "chip", split_axis=0, concat_axis=0, tiled=True)
            return [parts] + over_cores(parts)
        first = over_chips(message, (1, 2))
        (other,) = over_cores(message)
        second = over_chips(other, (1, 2))
        return [message, other, first, second]

    def gather_end(parts, after):
        if not pairwise:
            return [(part, chips * (1 + k)) for k, part in enumerate(parts[1:])]
        _, _, first, second = parts
        if after:
            first = tie(first, after)
        else:
            second = tie(second, [sums[0][1]])
        third = over_chips(first, (2, 1))
        late = [first, second, third] + [over_cores(part)[0] for part in (first, second, third)]
        return list(zip(late, range(2, 8)))

    def prep(tick, sources, blocks, after):
        out_shape = (
            pltpu.VMEM((span, piece), jnp.bfloat16),
            pltpu.VMEM((1 if pairwise else chips, span, piece + SIDE), jnp.bfloat16),
        )
        tabled = tick > 0 or not pairwise
        kernel = functools.partial(prep_kernel, rank, owners, owned, tick, chunks, blocks, tabled)
        args = (info, *sources, section_norm_gain) + ((down,) if tabled else ())
        return call(kernel, out_shape, args, "prep", 2 * span * piece * SIDE * bool(tick), span * piece * 8 * bool(tick), after=after)

    def own_layer(parts, after):
        width = piece * owners
        kernel = functools.partial(own_kernel, [start for _, start in parts])
        out_shape = (pltpu.VMEM((span, piece), jnp.float32), pltpu.VMEM((span, SIDE), jnp.float32))
        args = (info, *[part for part, _ in parts], weight)
        return call(kernel, out_shape, args, "own", span * width * piece // 2 * bool(after), width * piece // 2 * bool(after), after=after)

    def more_layer(parts, sums):
        kernel = functools.partial(more_kernel, [start for _, start in parts])
        out_shape = (pltpu.VMEM((span, piece), jnp.float32), pltpu.VMEM((span, SIDE), jnp.float32))
        args = (info, *[part for part, _ in parts], *sums, weight)
        return call(kernel, out_shape, args, "more", 0, 0)

    def layer(tick, parts, x, sums, terms, after):
        width = piece * owners
        kernel = functools.partial(layer_kernel, rank, owners, owned, tick, chunks, [start for _, start in parts], len(terms))
        args = (info, *[part for part, _ in parts], *terms, weight, x, up, *sums)
        out_shape = pltpu.VMEM((span, piece), jnp.bfloat16)
        return call(kernel, out_shape, args, "layer", 2 * span * width * piece, 2 * width * piece, after=after)

    arrived, state, sums, done, home_blocks, returned = {}, {}, {}, {}, {}, {}
    ticks = chunks + LAG * (sections - 1)

    def active(tick):
        return [s for s in range(sections) if 0 <= tick - LAG * s < chunks]

    def begin(tick):
        sources, blocks = [], []
        if 0 in active(tick):
            m, b = divmod(tick, per_micro)
            sources.append(feeds[m])
            blocks.append(b)
        if active(tick) != [0]:
            sources.append(arrived.pop(tick))
            blocks.append(0)
        if tick == 0:
            after = []
        else:
            after = [sums[tick - 1][1]]
        x, message = prep(tick, sources, blocks, after)
        parts = gather_start(message)
        state[tick] = [x, message, parts, parts[1] if pairwise else None]

    def own_chip(tick, after):
        parts = state[tick][2]
        own = [(parts[0], 0), (parts[1], 1)] if pairwise else [(parts[0], 0)]
        sums[tick] = own_layer(own, after)
        state[tick][2] = gather_end(parts, [sums[tick][1]] if after else [])
        if pairwise and after:
            sums[tick] = more_layer(state[tick][2][:2], sums[tick])
            state[tick][2] = state[tick][2][2:]

    down_maps = jnp.swapaxes(plugin_narrowing_factors[0], 1, 2)
    down = None
    if not pairwise:
        down = spread(down_maps, ())[0](after=[])
    up, begun = spread(plugin_widening_factors[0], ())
    begin(0)
    if pairwise:
        down, also = spread(down_maps, begun)
        begun = begun + also
    weight = staged(section_weight[0], [*begun, state[0][1]])
    up = up(after=[weight])
    own_chip(0, [])
    terms = []
    if pairwise:
        down = down(after=[weight])
        parts = [(state[0][1], 0), (state[0][3], 1)] + state[0][2]
        kernel = functools.partial(owner_kernel, rank, owners, owned, [start for _, start in parts])
        out_shape = pltpu.VMEM((1, span, SIDE), jnp.bfloat16)
        args = (info, *[part for part, _ in parts], down_maps)
        side = call(kernel, out_shape, args, "owner", 2 * span * piece * owners * rank, 0)
        side = call(add_kernel, out_shape, (info, side, *over_cores(side)), "add", 0, 0)
        terms = [side] + [over_chips(side, (k, k)) for k in (1, 2, 3)]
    for tick in range(ticks):
        after = []
        if tick + 1 < ticks:
            begin(tick + 1)
            after.append(state[tick + 1][1])
        if tick in returned:
            after.append(returned.pop(tick))
        x, _, parts, _ = state.pop(tick)
        if pairwise:
            size = piece * piece * owners
            x = tie(x, [part for part, start in parts if start in (5, 6)] + after, span * size, size)
        h = layer(tick, parts, x, sums[tick], terms if tick == 0 else [], after)
        if tick + 1 < ticks:
            own_chip(tick + 1, [h])
        onward = [(s, s + 1) for s in active(tick) if s + 1 < sections]
        if onward:
            arrived[tick + LAG] = lax.ppermute(h, "section", onward)
        if sections - 1 in active(tick):
            last = tick - LAG * (sections - 1)
            m = last // per_micro
            home = m // batches_here
            done[last] = h
            if last % per_micro == per_micro - 1:
                block = [done[m * per_micro + b] for b in range(per_micro)]
                if home != sections - 1:
                    if per_micro > 1:
                        out_shape = pltpu.VMEM((rows, piece), jnp.bfloat16)
                        block = [call(join_kernel, out_shape, (info, *block), "join", 0, rows * piece * 4)]
                    block = [lax.ppermute(block[0], "section", [(sections - 1, home)])]
                    if tick + 2 < ticks:
                        returned[tick + 2] = block[0]
                home_blocks[m] = block

    hidden, scores = [], []
    for slot in range(batches_here):
        blocks = [home_blocks[home * batches_here + slot] for home in range(sections)]
        counts = [len(block) for block in blocks]
        parts = [part for block in blocks for part in block]
        out_shape = pltpu.VMEM((1, rows), jnp.float32)
        kernel = functools.partial(reward_kernel, sections, counts)
        score = call(kernel, out_shape, (info, *parts, reward_head[None]), "reward", 0, 0)
        out_shape = jax.ShapeDtypeStruct((rows, piece), jnp.bfloat16)
        kernel = functools.partial(home_kernel, sections, counts)
        hidden.append(call(kernel, out_shape, (info, *parts), "home", 2 * rows * piece, rows * piece * 4, after=[score]))
        near_by = pltpu.VMEM((1, rows), jnp.float32)
        if pairwise:
            score = call(add_kernel, near_by, (info, score, *over_cores(score)), "add", 0, rows * 4)
            terms = [score] + [over_chips(score, (k, k)) for k in (1, 2, 3)]
        else:
            terms = [lax.psum(score, everyone)]
        limits = live_block_rows[slot : slot + 1]
        out_shape = jax.ShapeDtypeStruct((1, rows), jnp.float32)
        scores.append(call(score_kernel, out_shape, (info, limits, *terms), "score", 0, rows * 4))
    if batches_here == 1:
        return (hidden[0][None], scores[0])
    return (jnp.stack(hidden), jnp.concatenate(scores, axis=0))


def solution(mesh):
    sections, owners = mesh.shape["section"], mesh.shape["mp"]
    cores = 2 if owners % 2 == 0 else 1
    fine = jax.sharding.Mesh(
        mesh.devices.reshape(sections, owners // cores, cores), ("section", "chip", "core")
    )
    mp = ("chip", "core")
    placed = (
        P("section", None, mp),
        P("section", None, mp),
        P("section", mp),
        P("section", mp, None, None),
        P("section", mp, None, None),
        P(mp),
        P(),
        P("section", None),
    )
    return jax.shard_map(
        shards,
        mesh=fine,
        in_specs=placed,
        out_specs=(P("section", None, mp), P("section", None)),
        check_vma=False,
    )
```

```python
import functools

import jax
import jax.numpy as jnp
from jax import lax
from jax.experimental import pallas as pl
from jax.experimental.pallas import tpu as pltpu
from jax.sharding import PartitionSpec as P

BLOCK = 128
SIDE = 128
LAG = 2
SPAN = 1

VMEM = pl.BlockSpec(memory_space=pltpu.VMEM)
SMEM = pl.BlockSpec(memory_space=pltpu.SMEM)


def near(x):
    return pltpu.with_memory_space_constraint(x, pltpu.VMEM)


def call(kernel, out_shape, args, name, flops, moved, limit=8, after=()):
    info, *arrays = args
    count = len(arrays)

    def body(info_ref, *refs):
        kernel(info_ref, *refs[:count], *refs[count + len(after) :])

    return pl.pallas_call(
        body,
        out_shape=out_shape,
        in_specs=[SMEM] + [VMEM] * count + [pl.BlockSpec(memory_space=pl.ANY)] * len(after),
        out_specs=jax.tree.map(lambda _: VMEM, out_shape),
        compiler_params=pltpu.CompilerParams(vmem_limit_bytes=limit << 20),
        cost_estimate=pl.CostEstimate(flops=flops, bytes_accessed=moved, transcendentals=0),
        name=name,
    )(info, *map(near, arrays), *after)


def tie(x, after, flops=0, moved=0):
    def body(*_):
        pass

    return pl.pallas_call(
        body,
        out_shape=pltpu.VMEM(x.shape, x.dtype),
        in_specs=[VMEM] + [pl.BlockSpec(memory_space=pl.ANY)] * len(after),
        out_specs=VMEM,
        input_output_aliases={0: 0},
        compiler_params=pltpu.CompilerParams(vmem_limit_bytes=1 << 20),
        cost_estimate=pl.CostEstimate(flops=flops, bytes_accessed=moved, transcendentals=0),
        name="tie",
    )(near(x), *after)


def adapter_at(info_ref, owners, owned, tick, chunks, block):
    mine = jnp.clip(tick - LAG * info_ref[0], 0, chunks - 1)
    adapter = info_ref[2 + owners + mine * SPAN + block]
    if owned == 1:
        return adapter ^ info_ref[1]
    return (lax.div(adapter, owned) ^ info_ref[1]) * owned + lax.rem(adapter, owned)


def prep_kernel(rank, owners, owned, tick, chunks, block, tabled, info_ref, *refs):
    *sources, gain_ref, x_ref, m_ref = refs
    if tabled:
        *sources, gain_ref, down_ref = sources + [gain_ref]
    copies = m_ref.shape[0]
    rows, piece = x_ref.shape
    picked = [source[b * rows : (b + 1) * rows, :].astype(jnp.float32) for source, b in zip(sources, block)]
    x = jnp.where(info_ref[0] == 0, *picked) if len(picked) == 2 else picked[0]
    x_ref[...] = x.astype(jnp.bfloat16)
    scaled = (x * gain_ref[...].astype(jnp.float32)).astype(jnp.bfloat16)
    squares = jnp.sum(x * x, axis=1, keepdims=True)
    high = squares.astype(jnp.bfloat16).astype(jnp.float32)
    low = squares - high
    lane = lax.broadcasted_iota(jnp.int32, (rows, SIDE), 1)
    inner = jnp.zeros((rows, SIDE), jnp.float32)
    if tabled:
        inner = []
        for b in range(SPAN):
            product = lax.dot_general(
                scaled[b * BLOCK : (b + 1) * BLOCK],
                down_ref[adapter_at(info_ref, owners, owned, tick, chunks, b)],
                (((1,), (1,)), ((), ())),
                preferred_element_type=jnp.float32,
            )
            inner.append(jnp.concatenate([product, jnp.zeros((BLOCK, SIDE - rank), jnp.float32)], axis=1))
        inner = jnp.concatenate(inner, axis=0) if SPAN > 1 else inner[0]
    side = jnp.where(lane == rank, high, jnp.where(lane == rank + 1, low, inner)).astype(jnp.bfloat16)
    for copy in range(copies):
        m_ref[copy, :, :piece] = scaled
        m_ref[copy, :, piece:] = side


def owner_kernel(rank, owners, owned, starts, info_ref, *refs):
    *parts, down_ref, o_ref = refs
    rows = o_ref.shape[1]
    piece = parts[0].shape[2] - SIDE
    sums = []
    for o in range(owned):
        total = None
        for part, start in zip(parts, starts):
            columns = pl.ds(pl.multiple_of(info_ref[2 + start] * piece, piece), piece)
            term = lax.dot_general(
                part[0, :, :piece], down_ref[o, :, columns], (((1,), (1,)), ((), ())), preferred_element_type=jnp.float32
            )
            total = term if total is None else total + term
        sums.append(total)
    for b in range(SPAN):
        adapter = info_ref[2 + owners + b]
        block = slice(b * BLOCK, (b + 1) * BLOCK)
        product = jnp.zeros((BLOCK, rank), jnp.float32)
        for o, total in enumerate(sums):
            product = jnp.where(adapter == info_ref[1] * owned + o, total[block], product)
        side = jnp.concatenate([product, jnp.zeros((BLOCK, SIDE - rank), jnp.float32)], axis=1)
        o_ref[0, block, :] = side.astype(jnp.bfloat16)


def stage_kernel(w_ref, *refs):
    *_, o_ref, sem = refs
    copy = pltpu.make_async_copy(w_ref, o_ref, sem)
    copy.start()
    copy.wait()


def staged(weight, after):
    return pl.pallas_call(
        stage_kernel,
        out_shape=pltpu.VMEM(weight.shape, weight.dtype),
        in_specs=[pl.BlockSpec(memory_space=pl.ANY)] * (1 + len(after)),
        out_specs=VMEM,
        scratch_shapes=[pltpu.SemaphoreType.DMA],
        compiler_params=pltpu.CompilerParams(vmem_limit_bytes=4 << 20),
        cost_estimate=pl.CostEstimate(flops=0, bytes_accessed=2 * weight.size, transcendentals=0),
        name="stage",
    )(pltpu.with_memory_space_constraint(weight, pltpu.HBM), *after)


def piece_dots(info_ref, w_ref, parts, starts, columns):
    total = None
    for part, start in zip(parts, starts):
        piece = w_ref.shape[1]
        for k in range(part.shape[0]):
            depth = pl.ds(pl.multiple_of(info_ref[2 + start + k] * piece, piece), piece)
            term = jnp.dot(part[k, :, :piece], w_ref[depth, columns], preferred_element_type=jnp.float32)
            total = term if total is None else total + term
    return total


def side_sum(parts, piece):
    return sum(part[k, :, piece:].astype(jnp.float32) for part in parts for k in range(part.shape[0]))


def own_kernel(starts, info_ref, *refs):
    *parts, w_ref, total_ref, side_ref = refs
    piece = w_ref.shape[1]
    side_ref[...] = side_sum(parts, piece)
    tile = min(piece, 256)
    for n in range(piece // tile):
        columns = slice(n * tile, (n + 1) * tile)
        total_ref[:, columns] = piece_dots(info_ref, w_ref, parts, starts, columns)


def more_kernel(starts, info_ref, *refs):
    *parts, old_total, old_side, w_ref, total_ref, side_ref = refs
    piece = w_ref.shape[1]
    side_ref[...] = old_side[...] + side_sum(parts, piece)
    tile = min(piece, 256)
    for n in range(piece // tile):
        columns = slice(n * tile, (n + 1) * tile)
        total_ref[:, columns] = old_total[:, columns] + piece_dots(info_ref, w_ref, parts, starts, columns)


def layer_kernel(rank, owners, owned, tick, chunks, starts, extra, info_ref, *refs):
    *parts, w_ref, x_ref, up_ref, total_ref, side_ref, o_ref = refs
    piece = x_ref.shape[1]
    width = w_ref.shape[0]
    *parts, terms = [*parts[: len(parts) - extra], parts[len(parts) - extra :]]
    side = side_ref[...] + side_sum(parts, piece)
    if extra:
        side = side + side_sum(terms, 0)
    squares = side[:, rank : rank + 1] + side[:, rank + 1 : rank + 2]
    scale = lax.rsqrt(squares / width + 1e-05)
    inner = (2.0 * side[:, :rank]).astype(jnp.bfloat16)
    rows_of = [adapter_at(info_ref, owners, owned, tick, chunks, b) for b in range(SPAN)]
    tile = min(piece, 256)
    for n in range(piece // tile):
        columns = slice(n * tile, (n + 1) * tile)
        delta = [
            jnp.dot(
                inner[b * BLOCK : (b + 1) * BLOCK], up_ref[row, :, columns], preferred_element_type=jnp.float32
            )
            for b, row in enumerate(rows_of)
        ]
        total = jnp.concatenate(delta, axis=0) if SPAN > 1 else delta[0]
        total += total_ref[:, columns] + piece_dots(info_ref, w_ref, parts, starts, columns)
        h = x_ref[:, columns].astype(jnp.float32)
        o_ref[:, columns] = (h + scale * total).astype(jnp.bfloat16)


def join_kernel(info_ref, *refs):
    *blocks, o_ref = refs
    rows = blocks[0].shape[0]
    for i, block in enumerate(blocks):
        o_ref[i * rows : (i + 1) * rows, :] = block[...]


def home_kernel(sections, counts, info_ref, *refs):
    *blocks, o_ref = refs
    taken = 0
    for section, count in zip(range(sections), counts):
        own = blocks[taken : taken + count]
        taken += count

        @pl.when(info_ref[0] == section)
        def _():
            row = 0
            for block in own:
                span = block.shape[0]
                o_ref[row : row + span, :] = block[...]
                row += span


def reward_kernel(sections, counts, info_ref, *refs):
    *blocks, head_ref, score_ref = refs
    taken = 0
    for section, count in zip(range(sections), counts):
        own = blocks[taken : taken + count]
        taken += count

        @pl.when(info_ref[0] == section)
        def _():
            row = 0
            for block in own:
                span = block.shape[0]
                score_ref[:, row : row + span] = lax.dot_general(
                    head_ref[...], block[...], (((1,), (1,)), ((), ())), preferred_element_type=jnp.float32
                )
                row += span


def add_kernel(info_ref, *refs):
    *terms, o_ref = refs
    o_ref[...] = sum(term[...] for term in terms)


def score_kernel(info_ref, limits_ref, *refs):
    *terms, o_ref = refs
    total = sum(term[...] for term in terms)
    lane = lax.broadcasted_iota(jnp.int32, (1, BLOCK), 1)
    for b in range(total.shape[1] // BLOCK):
        columns = slice(b * BLOCK, (b + 1) * BLOCK)
        o_ref[:, columns] = jnp.where(lane < limits_ref[:, b : b + 1], total[:, columns], 0.0)


def cut(maps_ref, info_ref, place, out):
    piece = out.shape[-1]
    out[...] = maps_ref[:, :, pl.ds(pl.multiple_of((info_ref[1] ^ place) * piece, piece), piece)]


def cut_other_kernel(chips, info_ref, maps_ref, o_ref):
    for k in range(chips):
        cut(maps_ref, info_ref, 2 * k + 1, o_ref.at[k])


def cut_own_kernel(chips, info_ref, maps_ref, other_ref, *outs):
    for k, out in enumerate(outs):
        cut(maps_ref, info_ref, 2 * k, out.at[0])
        out[1] = other_ref[k]


def stack_kernel(info_ref, *refs):
    *blocks, o_ref = refs
    count, owned = blocks[0].shape[:2]
    for i, block in enumerate(blocks):
        for j in range(count):
            start = (i * count + j) * owned
            o_ref[start : start + owned] = block[j]


def shards(
    entering_hidden,
    section_weight,
    section_norm_gain,
    plugin_narrowing_factors,
    plugin_widening_factors,
    reward_head,
    adapter_of_block,
    live_block_rows,
):
    sections = lax.axis_size("section")
    section = lax.axis_index("section")
    chips = lax.axis_size("chip")
    cores = lax.axis_size("core")
    owners = chips * cores
    everyone = ("chip", "core")
    batches_here, rows, piece = entering_hidden.shape
    micro = batches_here * sections
    span = BLOCK * SPAN
    per_micro = rows // span
    owned = plugin_narrowing_factors.shape[1]
    rank = plugin_narrowing_factors.shape[3]
    chunks = micro * per_micro
    pairwise = chips == 4 and cores == 2

    chip, core = lax.axis_index("chip"), lax.axis_index("core")
    if pairwise:
        near_by, far = jnp.where(core == 0, 1, 2), jnp.where(core == 0, 2, 1)
        place = chip * cores + core
        parts = [(0, 0), (0, 1), (near_by, 0), (near_by, 1), (3, 0), (far, 1), (far, 0), (3, 1)]
        order = [(chip ^ there) * cores + (core ^ other) for there, other in parts]
    else:
        place = jnp.zeros_like(core)
        order = [i * cores + (core + k) % cores for k in range(cores) for i in range(chips)]
    info = jnp.concatenate([jnp.stack([section, place] + order), adapter_of_block.reshape(-1)])
    info = info.astype(jnp.int32)

    def over_cores(part):
        return [
            lax.ppermute(part, "core", [((c + k) % cores, c) for c in range(cores)]) for k in range(1, cores)
        ]

    def over_chips(part, steps):
        pairs = [(i * cores + c, (i ^ steps[c]) * cores + c) for i in range(chips) for c in range(cores)]
        return lax.ppermute(part, everyone, pairs)

    def spread(maps, after):
        if not pairwise:
            maps = jnp.moveaxis(maps.reshape(owned, rank, owners, piece), 2, 0)
            maps = lax.all_to_all(maps, everyone, split_axis=0, concat_axis=0, tiled=True)
            table = maps.reshape(owners * owned, rank, piece)
            return lambda after: table, after
        size = 2 * maps.size
        out_shape = pltpu.VMEM((chips, owned, rank, piece), maps.dtype)
        kernel = functools.partial(cut_other_kernel, chips)
        other = call(kernel, out_shape, (info, maps), "cut_other", 0, 0, after=after)
        (swapped,) = over_cores(other)
        out_shape = [pltpu.VMEM((cores, owned, rank, piece), maps.dtype) for _ in range(chips)]
        kernel = functools.partial(cut_own_kernel, chips)
        mine, *blocks = call(kernel, out_shape, (info, maps, swapped), "cut_own", 0, 0)
        blocks = [over_chips(block, (k, k)) for k, block in zip(range(1, chips), blocks)]
        out_shape = pltpu.VMEM((owners * owned, rank, piece), maps.dtype)
        return functools.partial(call, stack_kernel, out_shape, (info, mine, *blocks), "stack", 0, 0), [mine]

    feeds = []
    for m in range(micro):
        home, slot = divmod(m, batches_here)
        block = entering_hidden[slot]
        feeds.append(block if home == 0 else lax.ppermute(block, "section", [(home, 0)]))

    def gather_start(message):
        if not pairwise:
            parts = lax.all_to_all(message, "chip", split_axis=0, concat_axis=0, tiled=True)
            return [parts] + over_cores(parts)
        first = over_chips(message, (1, 2))
        (other,) = over_cores(message)
        second = over_chips(other, (1, 2))
        return [message, other, first, second]

    def gather_end(parts, after):
        if not pairwise:
            return [(part, chips * (1 + k)) for k, part in enumerate(parts[1:])]
        _, _, first, second = parts
        if after:
            first = tie(first, after)
        else:
            second = tie(second, [sums[0][1]])
        third = over_chips(first, (2, 1))
        late = [first, second, third] + [over_cores(part)[0] for part in (first, second, third)]
        return list(zip(late, range(2, 8)))

    def prep(tick, sources, blocks, after):
        out_shape = (
            pltpu.VMEM((span, piece), jnp.bfloat16),
            pltpu.VMEM((1 if pairwise else chips, span, piece + SIDE), jnp.bfloat16),
        )
        tabled = tick > 0 or not pairwise
        kernel = functools.partial(prep_kernel, rank, owners, owned, tick, chunks, blocks, tabled)
        args = (info, *sources, section_norm_gain) + ((down,) if tabled else ())
        return call(kernel, out_shape, args, "prep", 2 * span * piece * SIDE * bool(tick), span * piece * 8 * bool(tick), after=after)

    def own_layer(parts, after):
        width = piece * owners
        kernel = functools.partial(own_kernel, [start for _, start in parts])
        out_shape = (pltpu.VMEM((span, piece), jnp.float32), pltpu.VMEM((span, SIDE), jnp.float32))
        args = (info, *[part for part, _ in parts], weight)
        return call(kernel, out_shape, args, "own", span * width * piece // 2 * bool(after), width * piece // 2 * bool(after), after=after)

    def more_layer(parts, sums):
        kernel = functools.partial(more_kernel, [start for _, start in parts])
        out_shape = (pltpu.VMEM((span, piece), jnp.float32), pltpu.VMEM((span, SIDE), jnp.float32))
        args = (info, *[part for part, _ in parts], *sums, weight)
        return call(kernel, out_shape, args, "more", 0, 0)

    def layer(tick, parts, x, sums, terms, after):
        width = piece * owners
        kernel = functools.partial(layer_kernel, rank, owners, owned, tick, chunks, [start for _, start in parts], len(terms))
        args = (info, *[part for part, _ in parts], *terms, weight, x, up, *sums)
        out_shape = pltpu.VMEM((span, piece), jnp.bfloat16)
        return call(kernel, out_shape, args, "layer", 2 * span * width * piece, 2 * width * piece, after=after)

    arrived, state, sums, done, home_blocks, returned = {}, {}, {}, {}, {}, {}
    ticks = chunks + LAG * (sections - 1)

    def active(tick):
        return [s for s in range(sections) if 0 <= tick - LAG * s < chunks]

    def begin(tick):
        sources, blocks = [], []
        if 0 in active(tick):
            m, b = divmod(tick, per_micro)
            sources.append(feeds[m])
            blocks.append(b)
        if active(tick) != [0]:
            sources.append(arrived.pop(tick))
            blocks.append(0)
        if tick == 0:
            after = []
        else:
            after = [sums[tick - 1][1]]
        x, message = prep(tick, sources, blocks, after)
        parts = gather_start(message)
        state[tick] = [x, message, parts, parts[1] if pairwise else None]

    def own_chip(tick, after):
        parts = state[tick][2]
        own = [(parts[0], 0), (parts[1], 1)] if pairwise else [(parts[0], 0)]
        sums[tick] = own_layer(own, after)
        state[tick][2] = gather_end(parts, [sums[tick][1]] if after else [])
        if pairwise and after:
            sums[tick] = more_layer(state[tick][2][:2], sums[tick])
            state[tick][2] = state[tick][2][2:]

    down_maps = jnp.swapaxes(plugin_narrowing_factors[0], 1, 2)
    down = None
    if not pairwise:
        down = spread(down_maps, ())[0](after=[])
    up, begun = spread(plugin_widening_factors[0], ())
    begin(0)
    if pairwise:
        down, also = spread(down_maps, begun)
        begun = begun + also
    weight = staged(section_weight[0], [*begun, state[0][1]])
    up = up(after=[weight])
    own_chip(0, [])
    terms = []
    if pairwise:
        down = down(after=[weight])
        parts = [(state[0][1], 0), (state[0][3], 1)] + state[0][2]
        kernel = functools.partial(owner_kernel, rank, owners, owned, [start for _, start in parts])
        out_shape = pltpu.VMEM((1, span, SIDE), jnp.bfloat16)
        args = (info, *[part for part, _ in parts], down_maps)
        side = call(kernel, out_shape, args, "owner", 2 * span * piece * owners * rank, 0)
        side = call(add_kernel, out_shape, (info, side, *over_cores(side)), "add", 0, 0)
        terms = [side] + [over_chips(side, (k, k)) for k in (1, 2, 3)]
    for tick in range(ticks):
        after = []
        if tick + 1 < ticks:
            begin(tick + 1)
            after.append(state[tick + 1][1])
        if tick in returned:
            after.append(returned.pop(tick))
        x, _, parts, _ = state.pop(tick)
        if pairwise:
            size = piece * piece * owners
            x = tie(x, [part for part, start in parts if start in (5, 6)] + after, span * size, size)
        h = layer(tick, parts, x, sums[tick], terms if tick == 0 else [], after)
        if tick + 1 < ticks:
            own_chip(tick + 1, [h])
        onward = [(s, s + 1) for s in active(tick) if s + 1 < sections]
        if onward:
            arrived[tick + LAG] = lax.ppermute(h, "section", onward)
        if sections - 1 in active(tick):
            last = tick - LAG * (sections - 1)
            m = last // per_micro
            home = m // batches_here
            done[last] = h
            if last % per_micro == per_micro - 1:
                block = [done[m * per_micro + b] for b in range(per_micro)]
                if home != sections - 1:
                    if per_micro > 1:
                        out_shape = pltpu.VMEM((rows, piece), jnp.bfloat16)
                        block = [call(join_kernel, out_shape, (info, *block), "join", 0, rows * piece * 4)]
                    block = [lax.ppermute(block[0], "section", [(sections - 1, home)])]
                    wait = 2 if home == 0 else 1
                    if tick + wait < ticks:
                        returned[tick + wait] = block[0]
                home_blocks[m] = block

    hidden, scores = [], []
    for slot in range(batches_here):
        blocks = [home_blocks[home * batches_here + slot] for home in range(sections)]
        counts = [len(block) for block in blocks]
        parts = [part for block in blocks for part in block]
        out_shape = pltpu.VMEM((1, rows), jnp.float32)
        kernel = functools.partial(reward_kernel, sections, counts)
        score = call(kernel, out_shape, (info, *parts, reward_head[None]), "reward", 0, 0)
        out_shape = jax.ShapeDtypeStruct((rows, piece), jnp.bfloat16)
        kernel = functools.partial(home_kernel, sections, counts)
        hidden.append(call(kernel, out_shape, (info, *parts), "home", 2 * rows * piece, rows * piece * 4, after=[score]))
        near_by = pltpu.VMEM((1, rows), jnp.float32)
        if pairwise:
            score = call(add_kernel, near_by, (info, score, *over_cores(score)), "add", 0, rows * 4)
            terms = [score] + [over_chips(score, (k, k)) for k in (1, 2, 3)]
        else:
            terms = [lax.psum(score, everyone)]
        limits = live_block_rows[slot : slot + 1]
        out_shape = jax.ShapeDtypeStruct((1, rows), jnp.float32)
        scores.append(call(score_kernel, out_shape, (info, limits, *terms), "score", 0, rows * 4))
    if batches_here == 1:
        return (hidden[0][None], scores[0])
    return (jnp.stack(hidden), jnp.concatenate(scores, axis=0))


def solution(mesh):
    sections, owners = mesh.shape["section"], mesh.shape["mp"]
    cores = 2 if owners % 2 == 0 else 1
    fine = jax.sharding.Mesh(
        mesh.devices.reshape(sections, owners // cores, cores), ("section", "chip", "core")
    )
    mp = ("chip", "core")
    placed = (
        P("section", None, mp),
        P("section", None, mp),
        P("section", mp),
        P("section", mp, None, None),
        P("section", mp, None, None),
        P(mp),
        P(),
        P("section", None),
    )
    return jax.shard_map(
        shards,
        mesh=fine,
        in_specs=placed,
        out_specs=(P("section", None, mp), P("section", None)),
        check_vma=False,
    )
```
